32 devices in a mesh: dp: 16 (over z, y, core), tensor: 2 (over x).
Axes of the slice: x: 2, y: 2, z: 4, core: 2. Of those that a mesh axis runs over, the one named last changes fastest.
Arguments:
- tokens: bfloat16 [9216, 768], P('dp'), may hold values from -6 to 6
- cont_lengths: int32 [16, 2], P('dp'), may hold values from 1 to 320, 512 in all within a row
- routes: int32 [9216, 2], P('dp'), may hold values from 0 to 15, all different within a row; in each aligned block of 576 rows (0 to 575, 576 to 1151, ...) at most 92 rows name the same one
- route_gates: float32 [9216, 2], P('dp'), may hold values from 0.25 to 0.75
- w_qkv: bfloat16 [3, 768, 768], P(None, None, 'tensor'), may hold values from -0.21875 to 0.21875
- w_attn_out: bfloat16 [768, 768], P('tensor'), may hold values from -0.875 to 0.875
- norm_attn: float32 [768], replicated, may hold values from 0.5 to 1.5
- norm_ffn: float32 [768], replicated, may hold values from 0.5 to 1.5
- shared_in: bfloat16 [2, 768, 2048], P(None, None, 'tensor'), may hold values from -0.21875 to 0.21875
- shared_out: bfloat16 [2048, 768], P('tensor'), may hold values from -0.125 to 0.125
- expert_in: bfloat16 [2, 768, 32768], P(None, None, ('dp', 'tensor')), may hold values from -0.21875 to 0.21875
- expert_out: bfloat16 [32768, 768], P(('dp', 'tensor')), may hold values from -0.125 to 0.125
- cotangent: bfloat16 [9216, 768], P('dp'), may hold values from -6 to 6
Outputs:
- output: bfloat16 [9216, 768], P('dp')
- grad_tokens: bfloat16 [9216, 768], P('dp')
- grad_qkv: float32 [3, 768, 768], P(None, 'dp', 'tensor')
- grad_attn_out: float32 [768, 768], P('tensor', 'dp')
- grad_norm_attn: float32 [768], P('dp')
- grad_norm_ffn: float32 [768], P('dp')
- grad_shared_in: float32 [2, 768, 2048], P(None, 'dp', 'tensor')
- grad_shared_out: float32 [2048, 768], P('tensor', 'dp')
- grad_expert_in: float32 [2, 768, 32768], P(None, None, ('dp', 'tensor'))
- grad_expert_out: float32 [32768, 768], P(('dp', 'tensor'))
The draws below stay inside these ranges and needn't reach their ends.
Inputs may be any that keep to these rules, and one draw needn't show every extreme that they name: `routes`: each row names 2 different experts. Among the 576 rows of one group no expert is named more than 92 times; in some groups one is named exactly 92 times. `cont_lengths`: the lengths of a group's continuations sum to 512; none has more than 320 tokens.
All inputs are finite; a program needn't handle non-finite values.
Results may differ from the reference program's by a relative error of at most 0.02.
Values may be sent and summed in bfloat16 or wider, within the bound.
A program may use at most 320 MiB of HBM per device.

```python
import math
import jax
import jax.numpy as jnp
import numpy as np
from jax import lax

D = 768
H = 12
HD = 64
FS = 2048
FE = 2048
EXPERTS = 16
TOP = 2
PROMPT = 64
CONT_LEN = 256
CONTS = 2
CONT_MAX = 320
TOK_DEV = 576
CAP = 92
GROUPS = 16
TOKENS = 9216
N_DP = 16
N_TENSOR = 2


def steps_of(key, extent, shards, low, high):
    loudness = 1.0
    for dim, shards_of in shards:
        steps = jax.random.uniform(jax.random.fold_in(jax.random.fold_in(key, 6), dim), (shards_of,), jnp.float32, low / len(shards), high / len(shards))
        loudness = loudness * jnp.repeat(jnp.exp(steps), extent[dim] // shards_of).reshape((-1,) + (1,) * (len(extent) - 1 - dim))
    return loudness


def split_up(count, total, reach, lean):
    loads = [(1 << 20) // math.isqrt(standing ** lean) + 1 for standing in range(2, count + 1)]
    spare, counts = total - reach - (count - 1), [1] * (count - 1)
    while spare > 0:
        free = [i for i in range(count - 1) if counts[i] < reach]
        mass, budget = sum([loads[i] for i in free]), spare
        for i in free:
            extra = min(reach - counts[i], max(1, budget * loads[i] // mass), spare)
            counts[i] = counts[i] + extra
            spare = spare - extra
    return np.array([reach] + counts)


def ragged(key, count, total, reach, skew):
    if count == 2:
        one = jax.random.randint(key, (), max(1, total - reach), min(reach, total - 1) + 1)
        return jnp.stack([one, total - one])
    sizes = jnp.asarray(split_up(count, total, reach, skew), jnp.int32)
    twos = (count - 1) // 2
    source_of, taker = sizes[1:1 + 2 * twos:2], sizes[2:2 + 2 * twos:2]
    slack = jnp.minimum(source_of - 1, reach - taker)
    shifted = jax.random.randint(jax.random.fold_in(key, 1), (twos,), 0, 1 << 20) % (slack + 1)
    sizes = sizes.at[1:1 + 2 * twos:2].set(source_of - shifted).at[2:2 + 2 * twos:2].set(taker + shifted)
    return sizes[jax.random.permutation(jax.random.fold_in(key, 2), count)]


def deal_out(stream_key, own, number, rows, amount, top, limit, skew):
    order = jax.random.permutation(stream_key, amount)
    packed, ordinary = load_shares(amount, rows * top, limit, skew, True), load_shares(amount, rows * top, limit, skew, False)
    places = jnp.arange(amount)

    def named(tallies, rotation):
        used = int((tallies > 0).sum())
        fixed = max(1, used // 4)
        passed = fixed + (places - fixed + rotation * (used - fixed)) % max(1, amount - fixed)
        return jnp.zeros((amount,), jnp.int32).at[order[jnp.where(places < fixed, places, passed)]].set(jnp.asarray(tallies, jnp.int32))

    tallies = jnp.where(number % 4 == 0, named(packed, number // 4), named(ordinary, number - number // 4 - 1))
    mixed = jax.random.permutation(jax.random.fold_in(own, 3), amount)
    source_of, taker = mixed[0:amount // 2 * 2:2], mixed[1:amount // 2 * 2:2]
    margin = jnp.minimum(tallies[source_of] - 1, limit - tallies[taker]) // 2
    margin = jnp.where((source_of == order[0]) | (taker == order[0]) | (tallies[taker] == 0), 0, jnp.maximum(margin, 0))
    passed = jax.random.randint(jax.random.fold_in(own, 4), (amount // 2,), 0, 1 << 20) % (margin + 1)
    tallies = tallies.at[source_of].add(-passed).at[taker].add(passed)
    labels = jnp.searchsorted(jnp.cumsum(tallies), jnp.arange(rows * top), side="right").astype(jnp.int32)
    table = labels.reshape(top, rows).T
    table = table[jax.random.permutation(jax.random.fold_in(own, 1), rows)]
    rotation = jax.random.randint(jax.random.fold_in(own, 2), (rows, 1), 0, top)
    return jnp.take_along_axis(table, (jnp.arange(top)[None, :] + rotation) % top, axis=1)


def load_shares(amount, total, most, skew, full):
    portions = [(1 << 20) // math.isqrt(rank ** skew) + 1 for rank in range(1, amount + 1)]
    largest = most if full else min(most, max(-(-total // amount), total * portions[0] // sum(portions)))
    least = 1 if total - largest >= amount - 1 else 0
    holding, rest = [largest] + [least] * (amount - 1), total - largest - least * (amount - 1)
    while rest > 0:
        candidates = [i for i in range(1, amount) if holding[i] < largest] or [i for i in range(1, amount) if holding[i] < most]
        whole, left = sum([portions[i] for i in candidates]), rest
        for i in candidates:
            addition = min(most - holding[i], max(1, left * portions[i] // whole), rest)
            holding[i] = holding[i] + addition
            rest = rest - addition
    return np.array(holding)


def scatter_about(rng, dims, scale, reach, pieces=(), kind=jnp.bfloat16):
    factor_of = steps_of(rng, dims, pieces, -0.22, 0.18) if pieces else 1.0
    array = jax.random.normal(rng, dims, jnp.float32) * scale * factor_of
    return jnp.minimum(jnp.maximum(array, -reach), reach).astype(kind)


def setup_inputs(seed: int = 0) -> dict:
    seeds = jax.random.split(jax.random.key(seed), 14)
    tokens = scatter_about(seeds[0], (TOKENS, D), 1.0, 6.0, ((0, 16),))
    cont_lengths = jax.vmap(lambda own: ragged(own, CONTS, CONTS * CONT_LEN, CONT_MAX, 0))(jax.random.split(seeds[1], GROUPS)).reshape((GROUPS, CONTS)).astype(jnp.int32)
    routes_keys = jax.random.split(jax.random.fold_in(seeds[2], 1), TOKENS // TOK_DEV)
    routes_turns = jax.random.permutation(jax.random.fold_in(seeds[2], 3), TOKENS // TOK_DEV)
    routes = jax.vmap(lambda own, number: deal_out(jax.random.fold_in(seeds[2], 2), own, number, TOK_DEV, EXPERTS, TOP, CAP, 0))(routes_keys, routes_turns).reshape((TOKENS, TOP))
    route_gates = jnp.clip(0.25 + 0.5 * jax.random.uniform(seeds[3], (TOKENS, TOP), jnp.float32) ** steps_of(seeds[3], (TOKENS, TOP), ((0, 16),), -0.2, 0.2), 0.25, 0.75)
    w_qkv = scatter_about(seeds[4], (3, D, H * HD), D ** -0.5, 0.21875, ((2, 2),))
    w_attn_out = scatter_about(seeds[5], (H * HD, D), (H * HD // 16) ** -0.5, 0.875, ((0, 2),))
    norm_attn = jnp.clip(1.0 + 0.1 * jax.random.normal(seeds[6], (D,), jnp.float32), 0.5, 1.5)
    norm_ffn = jnp.clip(1.0 + 0.1 * jax.random.normal(seeds[7], (D,), jnp.float32), 0.5, 1.5)
    shared_in = scatter_about(seeds[8], (2, D, FS), D ** -0.5, 0.21875, ((2, 2),))
    shared_out = scatter_about(seeds[9], (FS, D), FS ** -0.5, 0.125, ((0, 2),))
    expert_in = scatter_about(seeds[10], (2, D, EXPERTS * FE), D ** -0.5, 0.21875, ((2, 32),))
    expert_out = scatter_about(seeds[11], (EXPERTS * FE, D), FE ** -0.5, 0.125, ((0, 32),))
    cotangent = scatter_about(seeds[12], (TOKENS, D), 1.0, 6.0, ((0, 16),))
    return {"tokens": tokens, "cont_lengths": cont_lengths, "routes": routes, "route_gates": route_gates, "w_qkv": w_qkv, "w_attn_out": w_attn_out, "norm_attn": norm_attn, "norm_ffn": norm_ffn, "shared_in": shared_in, "shared_out": shared_out, "expert_in": expert_in, "expert_out": expert_out, "cotangent": cotangent}


@jax.custom_vjp
def low(v):
    return lax.optimization_barrier(v.astype(jnp.bfloat16)).astype(jnp.float32)

@jax.custom_vjp
def low_back(v):
    return v

def low_keep(v):
    return (low(v), None)

def low_pass(kept, grad):
    return (grad,)

def back_keep(v):
    return (v, None)

def back_low(kept, grad):
    return (low(grad),)
low.defvjp(low_keep, low_pass)
low_back.defvjp(back_keep, back_low)
highest = lax.Precision.HIGHEST
epsilon = 1e-06

def rms_norm(values, gain):
    return values * lax.rsqrt(lax.optimization_barrier(jnp.mean(values * values, axis=-1, keepdims=True)) + epsilon) * gain

def silu_act(values):
    return values * jax.nn.sigmoid(values)

def group_layout(lengths):
    row_index = jnp.arange(TOK_DEV, dtype=jnp.int32)
    cont_ends = PROMPT + jnp.cumsum(lengths, dtype=jnp.int32)
    begins = cont_ends - lengths
    later = lax.optimization_barrier(jnp.sum((row_index[:, None] >= cont_ends[None, :]).astype(jnp.int32), axis=1, dtype=jnp.int32))
    segment = jnp.where(row_index < PROMPT, 0, 1 + later).astype(jnp.int32)
    member = (segment[:, None] == jnp.arange(1, CONTS + 1, dtype=jnp.int32)[None, :]).astype(jnp.int32)
    offset = lax.optimization_barrier(jnp.sum(member * begins[None, :], axis=1, dtype=jnp.int32))
    position = jnp.where(segment == 0, row_index, PROMPT + row_index - offset)
    allowed = (row_index[None, :] <= row_index[:, None]) & ((segment[None, :] == 0) | (segment[None, :] == segment[:, None]))
    return (position, allowed)

def rope_tables(position):
    half_size = HD // 2
    inv_freq = 10000.0 ** (-jnp.arange(half_size, dtype=jnp.float32) / half_size)
    angles = position.astype(jnp.float32)[:, None] * inv_freq[None, :]
    return (jnp.cos(angles)[:, None, :], jnp.sin(angles)[:, None, :])

def rotate_pairs(values, cosine, sine):
    half_size = values.shape[-1] // 2
    front_half = values[..., :half_size]
    back_half = values[..., half_size:]
    return jnp.concatenate([front_half * cosine - back_half * sine, front_half * sine + back_half * cosine], axis=-1)

def dispatch_plan(routes):
    flat_routes = routes.reshape(-1)
    one_hot = (flat_routes[:, None] == jnp.arange(EXPERTS, dtype=jnp.int32)[None, :]).astype(jnp.int32)
    earlier = jnp.cumsum(one_hot, axis=0, dtype=jnp.int32) - one_hot
    place_in = lax.optimization_barrier(jnp.sum(earlier * one_hot, axis=1, dtype=jnp.int32))
    target = flat_routes * CAP + place_in
    pair_count = flat_routes.shape[0]
    slot_table = jnp.full((EXPERTS * CAP,), pair_count, jnp.int32).at[target].set(jnp.arange(pair_count, dtype=jnp.int32))
    return (target, slot_table)

def group_layer(weights, items):
    w_qkv, w_attn_out, norm_attn, norm_ffn, shared_in, shared_out, expert_in, expert_out = weights
    tokens, lengths, routes, gates = items
    position, allowed = group_layout(lengths)
    cosine, sine = rope_tables(position)
    normed_attn = low(rms_norm(tokens, norm_attn))
    projected = low_back(jnp.einsum('td,sdf->stf', normed_attn, w_qkv, precision=highest))
    query = low(rotate_pairs(projected[0].reshape(TOK_DEV, H, HD), cosine, sine))
    key_rows = low(rotate_pairs(projected[1].reshape(TOK_DEV, H, HD), cosine, sine))
    value_rows = low(projected[2].reshape(TOK_DEV, H, HD))
    score = low_back(jnp.einsum('qhd,khd->hqk', query, key_rows, precision=highest) * HD ** (-0.5))
    score = jnp.where(allowed[None], score, -1000000000.0)
    row_max = lax.optimization_barrier(jnp.max(score, axis=-1, keepdims=True))
    exponent = jnp.exp(score - row_max)
    probs = low(exponent / lax.optimization_barrier(jnp.sum(exponent, axis=-1, keepdims=True)))
    attended = jnp.einsum('hqk,khd->qhd', probs, value_rows, precision=highest).reshape(TOK_DEV, H * HD)
    attended = low(low_back(attended))
    resid = tokens + low_back(jnp.dot(attended, w_attn_out, precision=highest))
    normed_ffn = low(rms_norm(resid, norm_ffn))
    gate_up = low_back(jnp.einsum('td,sdf->stf', normed_ffn, shared_in, precision=highest))
    shared_act = low(silu_act(gate_up[0]) * gate_up[1])
    shared = low_back(jnp.dot(shared_act, shared_out, precision=highest))
    target, slot_table = dispatch_plan(routes)
    padded = jnp.concatenate([normed_ffn, jnp.zeros((1, D), jnp.float32)], axis=0)
    rows = jnp.take(padded, slot_table // TOP, axis=0).reshape(EXPERTS, CAP, D)
    blocks = N_TENSOR * (N_DP // EXPERTS)
    block_size = FE // blocks
    rows_each = low_back(jnp.broadcast_to(rows[None], (blocks, EXPERTS, CAP, D)))
    expert_w = expert_in.reshape(2, D, EXPERTS, blocks, block_size)
    gate_e = low_back(jnp.einsum('kecd,dekx->kecx', rows_each, expert_w[0], precision=highest))
    up_e = low_back(jnp.einsum('kecd,dekx->kecx', rows_each, expert_w[1], precision=highest))
    act_e = low(silu_act(gate_e) * up_e)
    down_w = expert_out.reshape(EXPERTS, blocks, block_size, D)
    parts = low(jnp.einsum('kecx,ekxd->kecd', act_e, down_w, precision=highest))
    expert_rows = low_back(lax.optimization_barrier(jnp.sum(parts, axis=0))).reshape(EXPERTS * CAP, D)
    picked = jnp.take(expert_rows, target, axis=0).reshape(TOK_DEV, TOP, D)
    mixed = lax.optimization_barrier(jnp.sum(gates[:, :, None] * picked, axis=1))
    return resid + shared + mixed

def reference(tokens, cont_lengths, routes, route_gates, w_qkv, w_attn_out, norm_attn, norm_ffn, shared_in, shared_out, expert_in, expert_out, cotangent):
    floats = tuple((item.astype(jnp.float32) for item in (tokens, w_qkv, w_attn_out, norm_attn, norm_ffn, shared_in, shared_out, expert_in, expert_out)))
    routes_all = routes.reshape(N_DP, TOK_DEV, TOP)
    gates_all = route_gates.astype(jnp.float32).reshape(N_DP, TOK_DEV, TOP)
    stepper = jax.checkpoint(group_layer)

    def forward(tokens_f, *weights):

        def one_group(items):
            return stepper(weights, items)
        grouped = lax.map(one_group, (tokens_f.reshape(N_DP, TOK_DEV, D), cont_lengths, routes_all, gates_all))
        return grouped.reshape(TOKENS, D)
    output, pullback = jax.vjp(forward, *floats)
    grads = pullback(cotangent.astype(jnp.float32))
    return (output.astype(jnp.bfloat16), grads[0].astype(jnp.bfloat16), grads[1], grads[2], grads[3], grads[4], grads[5], grads[6], grads[7], grads[8])
```

```python
import functools

import jax
import jax.numpy as jnp
from jax import lax
from jax.experimental import pallas as pl
from jax.experimental.pallas import tpu as pltpu
from jax.sharding import PartitionSpec as P

HD = 64
EXPERTS = 16
TOP = 2
PROMPT = 64
CAP = 92


epsilon = 1e-06


def rms_parts(values, gain):
    factor = lax.rsqrt(jnp.mean(values * values, axis=-1, keepdims=True) + epsilon)
    return (values * factor * gain, factor)


def rms_back(values, factor, gain, incoming):
    weighted = incoming * gain
    inner = jnp.mean(weighted * values, axis=-1, keepdims=True)
    return (
        factor * weighted - values * factor * factor * factor * inner,
        jnp.sum(incoming * values * factor, axis=0),
    )


def silu_act(values):
    return values * jax.nn.sigmoid(values)


def swiglu_back(gate_up, d_act):
    sigma = jax.nn.sigmoid(gate_up[0])
    d_gate = d_act * gate_up[1] * sigma * (1.0 + gate_up[0] * (1.0 - sigma))
    d_upper = d_act * gate_up[0] * sigma
    return jnp.stack([d_gate, d_upper]).astype(jnp.bfloat16)


def group_layout(lengths, rows_here):
    row_index = jnp.arange(rows_here, dtype=jnp.int32)
    cont_ends = PROMPT + jnp.cumsum(lengths, dtype=jnp.int32)
    begins = cont_ends - lengths
    later = jnp.sum(
        (row_index[:, None] >= cont_ends[None, :]).astype(jnp.int32), axis=1, dtype=jnp.int32
    )
    segment = jnp.where(row_index < PROMPT, 0, 1 + later)
    member = (
        segment[:, None] == jnp.arange(1, lengths.shape[0] + 1, dtype=jnp.int32)[None, :]
    ).astype(jnp.int32)
    offset = jnp.sum(member * begins[None, :], axis=1, dtype=jnp.int32)
    position = jnp.where(segment == 0, row_index, PROMPT + row_index - offset)
    allowed = (row_index[None, :] <= row_index[:, None]) & (
        (segment[None, :] == 0) | (segment[None, :] == segment[:, None])
    )
    return (position, allowed)


def rope_tables(position):
    half_size = HD // 2
    inv_freq = 10000.0 ** (-jnp.arange(half_size, dtype=jnp.float32) / half_size)
    angles = position.astype(jnp.float32)[:, None] * inv_freq[None, :]
    return (jnp.cos(angles)[:, None, :], jnp.sin(angles)[:, None, :])


def rotate_pairs(values, cosine, sine):
    half_size = values.shape[-1] // 2
    front_half = values[..., :half_size]
    back_half = values[..., half_size:]
    return jnp.concatenate(
        [front_half * cosine - back_half * sine, front_half * sine + back_half * cosine], axis=-1
    )


def dispatch_plan(routes):
    flat_routes = routes.reshape(-1)
    one_hot = (flat_routes[:, None] == jnp.arange(EXPERTS, dtype=jnp.int32)[None, :]).astype(
        jnp.int32
    )
    earlier = jnp.cumsum(one_hot, axis=0, dtype=jnp.int32) - one_hot
    place_in = jnp.sum(earlier * one_hot, axis=1, dtype=jnp.int32)
    target = flat_routes * CAP + place_in
    pair_count = flat_routes.shape[0]
    slot_table = (
        jnp.full((EXPERTS * CAP,), pair_count, jnp.int32)
        .at[target]
        .set(jnp.arange(pair_count, dtype=jnp.int32))
    )
    return (target, slot_table)


def spread_rows(padded, indices, copies):
    model_width = padded.shape[1]
    picked = jnp.take(padded, indices, axis=0).reshape(EXPERTS, 1, CAP, model_width)
    return jnp.broadcast_to(picked, (EXPERTS, copies, CAP, model_width)).reshape(
        EXPERTS * copies, CAP, model_width
    )


def collect_rows(returned, target, copies, rows_here):
    model_width = returned.shape[2]
    summed = jnp.sum(returned.reshape(EXPERTS, copies, CAP, model_width), axis=1, dtype=jnp.float32)
    summed = summed.reshape(EXPERTS * CAP, model_width)
    return jnp.take(summed, target, axis=0).reshape(rows_here, TOP, model_width)


def local(
    tokens,
    cont_lengths,
    routes,
    route_gates,
    w_qkv,
    w_attn_out,
    norm_attn,
    norm_ffn,
    shared_in,
    shared_out,
    expert_in,
    expert_out,
    cotangent,
):
    rows_here = tokens.shape[0]
    model_width = tokens.shape[1]
    groups = lax.axis_size("dp")
    copies = groups // EXPERTS
    head_count = w_qkv.shape[2] // HD
    score_scale = HD ** (-0.5)
    inputs = tokens.astype(jnp.float32)
    position, allowed = group_layout(cont_lengths[0], rows_here)
    cosine, sine = rope_tables(position)
    normed_a, factor_a = rms_parts(inputs, norm_attn)
    normed_attn = normed_a.astype(jnp.bfloat16)
    projected = jnp.einsum("td,sdf->stf", normed_attn, w_qkv, preferred_element_type=jnp.float32)
    query = rotate_pairs(projected[0].reshape(rows_here, head_count, HD), cosine, sine).astype(
        jnp.bfloat16
    )
    key_rows = rotate_pairs(projected[1].reshape(rows_here, head_count, HD), cosine, sine).astype(
        jnp.bfloat16
    )
    value_rows = projected[2].reshape(rows_here, head_count, HD).astype(jnp.bfloat16)
    score = (
        jnp.einsum("qhd,khd->hqk", query, key_rows, preferred_element_type=jnp.float32)
        * score_scale
    )
    score = jnp.where(allowed[None], score, -1000000000.0)
    row_max = jnp.max(score, axis=-1, keepdims=True)
    exponent = jnp.exp(score - row_max)
    row_total = jnp.sum(exponent, axis=-1, keepdims=True)
    log_total = row_max + jnp.log(row_total)
    weights_b = (exponent / row_total).astype(jnp.bfloat16)
    attended = jnp.einsum("hqk,khd->qhd", weights_b, value_rows, preferred_element_type=jnp.float32)
    attended = attended.reshape(rows_here, head_count * HD).astype(jnp.bfloat16)
    attn_part = jnp.dot(attended, w_attn_out, preferred_element_type=jnp.float32)
    resid = inputs + lax.psum(attn_part.astype(jnp.bfloat16), "tensor").astype(jnp.float32)
    normed_f, factor_f = rms_parts(resid, norm_ffn)
    normed_ffn = normed_f.astype(jnp.bfloat16)
    gate_up = jnp.einsum("td,sdf->stf", normed_ffn, shared_in, preferred_element_type=jnp.float32)
    shared_act = (silu_act(gate_up[0]) * gate_up[1]).astype(jnp.bfloat16)
    shared_part = jnp.dot(shared_act, shared_out, preferred_element_type=jnp.float32)
    target, slot_table = dispatch_plan(routes)
    padded_rows = jnp.concatenate([normed_ffn, jnp.zeros((1, model_width), jnp.bfloat16)], axis=0)
    send_rows = spread_rows(padded_rows, slot_table // TOP, copies)
    arrived = lax.all_to_all(send_rows, "dp", split_axis=0, concat_axis=0, tiled=True)
    expert_input = arrived.reshape(groups * CAP, model_width)
    expert_gu = jnp.einsum(
        "rd,sdf->srf", expert_input, expert_in, preferred_element_type=jnp.float32
    )
    expert_act = (silu_act(expert_gu[0]) * expert_gu[1]).astype(jnp.bfloat16)
    expert_part = jnp.dot(expert_act, expert_out, preferred_element_type=jnp.float32).astype(
        jnp.bfloat16
    )
    returned = lax.all_to_all(
        expert_part.reshape(groups, CAP, model_width), "dp", split_axis=0, concat_axis=0, tiled=True
    )
    picked = collect_rows(returned, target, copies, rows_here)
    mixed = jnp.sum(route_gates[:, :, None] * picked, axis=1)
    ffn_total = lax.psum((shared_part + mixed).astype(jnp.bfloat16), "tensor").astype(jnp.float32)
    output = (resid + ffn_total).astype(jnp.bfloat16)
    upstream = cotangent.astype(jnp.float32)
    d_shared_act = jnp.einsum(
        "td,fd->tf", cotangent, shared_out, preferred_element_type=jnp.float32
    )
    d_shared_gu = swiglu_back(gate_up, d_shared_act)
    d_normed = jnp.einsum("stf,sdf->td", d_shared_gu, shared_in, preferred_element_type=jnp.float32)
    g_shared_in = jnp.einsum(
        "td,stf->sdf", normed_ffn, d_shared_gu, preferred_element_type=jnp.float32
    )
    g_shared_out = jnp.einsum(
        "tf,td->fd", shared_act, cotangent, preferred_element_type=jnp.float32
    )
    pair_grad = (
        (route_gates[:, :, None] * upstream[:, None, :])
        .reshape(rows_here * TOP, model_width)
        .astype(jnp.bfloat16)
    )
    padded_grad = jnp.concatenate([pair_grad, jnp.zeros((1, model_width), jnp.bfloat16)], axis=0)
    send_grad = spread_rows(padded_grad, slot_table, copies)
    again_rows = spread_rows(padded_rows, slot_table // TOP, copies)
    grad_arrived, rows_arrived = (
        lax.all_to_all(send_grad, "dp", split_axis=0, concat_axis=0, tiled=True),
        lax.all_to_all(again_rows, "dp", split_axis=0, concat_axis=0, tiled=True),
    )
    rows_back = rows_arrived.reshape(groups * CAP, model_width)
    d_expert_rows = grad_arrived.reshape(groups * CAP, model_width)
    back_gu = jnp.einsum("rd,sdf->srf", rows_back, expert_in, preferred_element_type=jnp.float32)
    back_act = (silu_act(back_gu[0]) * back_gu[1]).astype(jnp.bfloat16)
    d_expert_act = jnp.einsum(
        "rd,fd->rf", d_expert_rows, expert_out, preferred_element_type=jnp.float32
    )
    d_expert_gu = swiglu_back(back_gu, d_expert_act)
    d_expert_in = jnp.einsum(
        "srf,sdf->rd", d_expert_gu, expert_in, preferred_element_type=jnp.float32
    ).astype(jnp.bfloat16)
    g_expert_in = jnp.einsum(
        "rd,srf->sdf", rows_back, d_expert_gu, preferred_element_type=jnp.float32
    )
    g_expert_out = jnp.einsum(
        "rf,rd->fd", back_act, d_expert_rows, preferred_element_type=jnp.float32
    )
    d_returned = lax.all_to_all(
        d_expert_in.reshape(groups, CAP, model_width), "dp", split_axis=0, concat_axis=0, tiled=True
    )
    d_normed = d_normed + jnp.sum(collect_rows(d_returned, target, copies, rows_here), axis=1)
    d_normed = lax.psum(d_normed.astype(jnp.bfloat16), "tensor").astype(jnp.float32)
    d_resid_norm, g_norm_ffn = rms_back(resid, factor_f, norm_ffn, d_normed)
    d_resid = upstream + d_resid_norm
    d_resid_b = d_resid.astype(jnp.bfloat16)
    g_attn_out = jnp.einsum("tf,td->fd", attended, d_resid_b, preferred_element_type=jnp.float32)
    d_attended = jnp.einsum("td,fd->tf", d_resid_b, w_attn_out, preferred_element_type=jnp.float32)
    d_attended = d_attended.astype(jnp.bfloat16).reshape(rows_here, head_count, HD)
    recomputed = (
        jnp.einsum("qhd,khd->hqk", query, key_rows, preferred_element_type=jnp.float32)
        * score_scale
    )
    recomputed = jnp.where(allowed[None], recomputed, -1000000000.0)
    probs = jnp.exp(recomputed - log_total)
    probs_b = probs.astype(jnp.bfloat16)
    d_probs = jnp.einsum("qhd,khd->hqk", d_attended, value_rows, preferred_element_type=jnp.float32)
    d_value = jnp.einsum("hqk,qhd->khd", probs_b, d_attended, preferred_element_type=jnp.float32)
    inner = jnp.sum(d_probs * probs, axis=-1, keepdims=True)
    d_score = (probs * (d_probs - inner)).astype(jnp.bfloat16)
    d_query = (
        jnp.einsum("hqk,khd->qhd", d_score, key_rows, preferred_element_type=jnp.float32)
        * score_scale
    )
    d_key = (
        jnp.einsum("hqk,qhd->khd", d_score, query, preferred_element_type=jnp.float32) * score_scale
    )
    d_query = rotate_pairs(d_query, cosine, -sine).reshape(rows_here, head_count * HD)
    d_key = rotate_pairs(d_key, cosine, -sine).reshape(rows_here, head_count * HD)
    d_qkv = jnp.stack([d_query, d_key, d_value.reshape(rows_here, head_count * HD)]).astype(
        jnp.bfloat16
    )
    g_qkv = jnp.einsum("td,stf->sdf", normed_attn, d_qkv, preferred_element_type=jnp.float32)
    d_normed_attn = jnp.einsum("stf,sdf->td", d_qkv, w_qkv, preferred_element_type=jnp.float32)
    d_normed_attn = lax.psum(d_normed_attn.astype(jnp.bfloat16), "tensor").astype(jnp.float32)
    d_input_norm, g_norm_attn = rms_back(inputs, factor_a, norm_attn, d_normed_attn)
    grad_tokens = (d_resid + d_input_norm).astype(jnp.bfloat16)
    summed_all = (
        lax.psum_scatter(g_qkv, "dp", scatter_dimension=1, tiled=True),
        lax.psum_scatter(g_attn_out, "dp", scatter_dimension=1, tiled=True),
        lax.psum_scatter(g_norm_attn, "dp", scatter_dimension=0, tiled=True),
        lax.psum_scatter(g_shared_in, "dp", scatter_dimension=1, tiled=True),
        lax.psum_scatter(g_shared_out, "dp", scatter_dimension=1, tiled=True),
        lax.psum_scatter(g_norm_ffn, "dp", scatter_dimension=0, tiled=True),
    )
    return (
        output,
        grad_tokens,
        summed_all[0],
        summed_all[1],
        summed_all[2],
        summed_all[5],
        summed_all[3],
        summed_all[4],
        g_expert_in,
        g_expert_out,
    )


VMEM_BYTES = 64000 * 1024
FOLD = 96
MESH = pl.DeviceIdType.MESH
VM = pl.BlockSpec(memory_space=pltpu.VMEM)
ANY = pl.BlockSpec(memory_space=pl.ANY)
f32 = jnp.float32
bf16 = jnp.bfloat16


def round_up(value, unit):
    return (value + unit - 1) // unit * unit


def dot(a, b):
    return jnp.dot(a, b, preferred_element_type=f32)


def dot_nt(a, b):
    return lax.dot_general(a, b, (((1,), (1,)), ((), ())), preferred_element_type=f32)


def dot_tn(a, b):
    return lax.dot_general(a, b, (((0,), (0,)), ((), ())), preferred_element_type=f32)


def sigmoid(values):
    return 0.5 * jnp.tanh(0.5 * values) + 0.5


def swap_halves(values):
    lane = lax.broadcasted_iota(jnp.int32, values.shape, 1)
    ahead = pltpu.roll(values, values.shape[1] - HD // 2, 1)
    behind = pltpu.roll(values, HD // 2, 1)
    return jnp.where(lax.rem(lane, HD) < HD // 2, ahead, behind)


def hello(groups):
    me, t = lax.axis_index("dp"), lax.axis_index("tensor")
    barrier = pltpu.get_barrier_semaphore()

    def greet(k, carry):
        pl.semaphore_signal(
            barrier, inc=1, device_id=(lax.rem(me + k, groups), t), device_id_type=MESH
        )
        return carry

    lax.fori_loop(1, groups, greet, 0)
    pl.semaphore_signal(barrier, inc=1, device_id=(me, 1 - t), device_id_type=MESH)
    pl.semaphore_wait(barrier, groups)


def fill_bias(bias, segr, segc, rows):
    step = FOLD

    def body(i, carry):
        at = pl.ds(pl.multiple_of(i * step, step), step)
        row = lax.broadcasted_iota(jnp.int32, (step, rows), 0) + i * step
        col = lax.broadcasted_iota(jnp.int32, (step, rows), 1)
        own = segc[at, :]
        other = segr[...]
        ok = (col <= row) & ((other == 0) | (other == own))
        bias[at, :] = jnp.where(ok, 0.0, -1000000000.0)
        return carry

    lax.fori_loop(0, rows // step, body, 0)


def send(src, dst, ssem, rsem, to):
    return pltpu.make_async_remote_copy(
        src_ref=src, dst_ref=dst, send_sem=ssem, recv_sem=rsem, device_id=to, device_id_type=MESH
    )


def front_kernel(
    G, tok, na, nf, cos, sin, segr, segc, rT, gT, wqkv, wo, cot, si, so, ei, eo,
    qkv, lse, att_own, normed_a, resid, plan, gate, part, shp, dres, gnf, gsh, gein, geout,
    bias, att, wo2, slot, drows, normed, rows, vsi, vso, vei, veo,
    act_s, dgu_s, act_e, dgu_e, dnsh, dnsh_r, dxs, dxr, rets, ret, dnb, turned, tall, wide, pale,
    s_x, r_x, s_c, r_c, s_r, r_r, s_f, r_f, s_dx, r_dx, s_ret, r_ret, lsem, osem,
):
    T, D = tok.shape
    HL = wqkv.shape[2]
    F = si.shape[2]
    C = plan.shape[0] // G
    half = D // 2
    scale = HD ** (-0.5)
    me, t = lax.axis_index("dp"), lax.axis_index("tensor")
    mine = pl.ds(pl.multiple_of(t * half, 128), half)
    theirs = pl.ds(pl.multiple_of((1 - t) * half, 128), half)
    partner = (me, 1 - t)

    loads = [
        pltpu.make_async_copy(a, b, lsem.at[i])
        for i, (a, b) in enumerate(((si, vsi), (so, vso), (ei, vei), (eo, veo)))
    ]
    for c in loads:
        c.start()
    hello(G)
    wo_copy = send(wo, wo2, s_x.at[0], r_x.at[0], partner)
    wo_copy.start()

    names = lax.broadcasted_iota(jnp.int32, (EXPERTS, T), 0)
    picks0, picks1 = rT[0:1, :] == names, rT[1:2, :] == names
    member = jnp.where(picks0 | picks1, 1.0, 0.0)
    upper = jnp.where(
        lax.broadcasted_iota(jnp.int32, (T, T), 0) < lax.broadcasted_iota(jnp.int32, (T, T), 1),
        1.0,
        0.0,
    ).astype(bf16)
    slot[...] = jnp.where(member > 0.0, dot(member.astype(bf16), upper), -1.0)
    gate[...] = jnp.where(picks0, gT[0:1, :], 0.0) + jnp.where(picks1, gT[1:2, :], 0.0)

    def row_at(k):
        return pl.ds(pl.multiple_of(k * C, C), C)

    def cot_copy(k):
        return send(
            part.at[row_at(k)], drows.at[row_at(k)], s_c.at[k], r_c.at[k],
            (lax.rem(me + k, G), t),
        )

    def cot_step(k, carry):
        e = lax.rem(me + k, G)
        at = pl.ds(pl.multiple_of(k * C, C), C)
        place = lax.broadcasted_iota(jnp.int32, (C, T), 0).astype(f32)
        hit = slot[pl.ds(e, 1), :] == place
        picked = jnp.where(hit, 1.0, 0.0).astype(bf16)
        plan[at, :] = picked
        weight = jnp.sum(jnp.where(hit, gate[pl.ds(e, 1), :], 0.0), axis=1, keepdims=True)
        grad = (dot(picked, cot[...]) * weight).astype(bf16)
        part[at, :] = grad

        @pl.when(k > 0)
        def _():
            cot_copy(k).start()

        @pl.when(k == 0)
        def _():
            drows[at, :] = grad

        return carry

    lax.fori_loop(0, G, cot_step, 0)

    fill_bias(bias, segr, segc, T)

    def norm_step(i, carry):
        at = pl.ds(pl.multiple_of(i * FOLD, FOLD), FOLD)
        x = tok[at, :].astype(f32)
        r = lax.rsqrt(jnp.mean(x * x, axis=1, keepdims=True) + epsilon)
        normed_a[at, :] = (x * r * na[...]).astype(bf16)
        return carry

    lax.fori_loop(0, T // FOLD, norm_step, 0)

    def project(s, turned):
        full = dot(normed_a[...], wqkv[s])
        for j in range(HL // 128):
            x = full[:, j * 128 : (j + 1) * 128]
            if turned:
                x = x * cos[...] + swap_halves(x) * sin[...]
            qkv[s, :, j * 128 : (j + 1) * 128] = x.astype(bf16)

    project(0, True)
    project(1, True)
    project(2, False)
    lane = lax.broadcasted_iota(jnp.int32, (T, 128), 1)

    def att_copy(j):
        at = pl.ds(pl.multiple_of(j * 128, 128), 128)
        return send(att_own.at[:, at], att.at[:, at], s_x.at[1 + j], r_x.at[1 + j], partner)

    lse[...] = jnp.zeros_like(lse)

    def attend(j, carry):
        at = pl.ds(pl.multiple_of(j * 128, 128), 128)
        q, k, v = qkv[0, :, at], qkv[1, :, at], qkv[2, :, at]
        outs = []
        for i in range(2):
            inside = (lane < HD) if i == 0 else (lane >= HD)
            s = dot_nt(jnp.where(inside, q, jnp.zeros_like(q)), k) * scale + bias[...]
            top = jnp.max(s, axis=1, keepdims=True)
            e = jnp.exp(s - top)
            total = jnp.sum(e, axis=1, keepdims=True)
            p = (e * (1.0 / total)).astype(bf16)
            lse[...] = jnp.where(lane == 2 * j + i, top + jnp.log(total), lse[...])
            outs.append(dot(p, v))
        att_own[:, at] = jnp.where(lane < HD, outs[0], outs[1]).astype(bf16)
        att_copy(j).start()
        return carry

    lax.fori_loop(0, HL // 128, attend, 0)
    wo_copy.wait()
    own_out = dot(att_own[...], wo[...])
    for j in range(HL // 128):
        att_copy(j).wait()
    resid[...] = tok[...].astype(f32) + own_out + dot(att[...], wo2[...])

    def norm2_step(i, carry):
        at = pl.ds(pl.multiple_of(i * FOLD, FOLD), FOLD)
        x = resid[at, :]
        r = lax.rsqrt(jnp.mean(x * x, axis=1, keepdims=True) + epsilon)
        normed[at, :] = (x * r * nf[...]).astype(bf16)
        return carry

    lax.fori_loop(0, T // FOLD, norm2_step, 0)

    def row_copy(k):
        return send(
            rets.at[row_at(k)], rows.at[row_at(k), mine], s_r.at[k], r_r.at[k], (lax.rem(me + k, G), t)
        )

    def row_pass(k):
        return send(
            rows.at[row_at(k), mine], rows.at[row_at(k), mine], s_f.at[k], r_f.at[k], partner
        )

    def row_step(k, carry):
        values = dot(plan[row_at(k), :], normed[:, mine]).astype(bf16)
        rets[row_at(k), :] = values

        @pl.when(k > 0)
        def _():
            row_copy(k).start()

        @pl.when(k == 0)
        def _():
            rows[row_at(k), mine] = values
            row_pass(k).start()

        return carry

    lax.fori_loop(0, G, row_step, 0)

    loads[0].wait()
    loads[1].wait()
    tile = 256

    def hand_on(k):
        row_copy(k).wait_recv()
        row_pass(k).start()

    def shared_step(u, carry):
        at = pl.ds(pl.multiple_of(u * tile, tile), tile)
        pre = dot(normed[...], vsi[0, :, at])
        up = dot(normed[...], vsi[1, :, at])
        d_act = dot_nt(cot[...], vso[at, :])
        s = sigmoid(pre)
        gs = pre * s
        act_s[:, at] = (gs * up).astype(bf16)
        dgu_s[0, :, at] = (d_act * up * (s + gs * (1.0 - s))).astype(bf16)
        dgu_s[1, :, at] = (d_act * gs).astype(bf16)
        return carry

    lax.fori_loop(0, F // tile, shared_step, 0)
    for k in range(1, 6):
        hand_on(k)
    dnsh[...] = (dot_nt(dgu_s[0], vsi[0]) + dot_nt(dgu_s[1], vsi[1])).astype(bf16)
    dnsh_copy = send(dnsh.at[:, theirs], dnsh_r, s_x.at[4], r_x.at[4], partner)
    for k in range(6, 9):
        hand_on(k)
    shp[...] = dot(act_s[...], vso[...]).astype(bf16)
    for k in range(9, 11):
        hand_on(k)

    side = round_up(T, 128)
    turned[:, 0:T] = normed[...].T
    turned[:, side : side + T] = cot[...].T
    tiles = F // tile

    def gsh_copy(i):
        at = pl.ds(pl.multiple_of(i * tile, tile), tile)
        return pltpu.make_async_copy(pale.at[lax.rem(i, 2)], gsh.at[:, at], osem.at[lax.rem(i, 2)])

    def gsh_step(i, carry):
        @pl.when(i > 1)
        def _():
            gsh_copy(i - 2).wait()

        u = lax.rem(i, tiles)
        at = pl.ds(pl.multiple_of(u * tile, tile), tile)

        @pl.when(i < 2 * tiles)
        def _():
            pale[lax.rem(i, 2)] = dot(turned[:, 0:T], dgu_s[i // tiles, :, at]).astype(bf16)

        @pl.when(i >= 2 * tiles)
        def _():
            pale[lax.rem(i, 2)] = dot(turned[:, side : side + T], act_s[:, at]).astype(bf16)

        gsh_copy(i).start()
        return carry

    lax.fori_loop(0, 3 * tiles, gsh_step, 0)
    for k in range(11, G):
        hand_on(k)
    dnsh_copy.start()
    gsh_copy(3 * tiles - 2).wait()
    gsh_copy(3 * tiles - 1).wait()

    loads[2].wait()
    loads[3].wait()
    per = 4
    M = per * C

    def dx_copy(c):
        at = pl.ds(pl.multiple_of(c * M, M), M)
        return send(dxs.at[at, theirs], dxr.at[at], s_dx.at[c], r_dx.at[c], partner)

    def ret_copy(k):
        return send(
            rets.at[row_at(k)], ret.at[row_at(k)], s_ret.at[k], r_ret.at[k],
            (lax.rem(me - k + G, G), t),
        )

    def expert_chunk(c):
        for k in range(c * per, (c + 1) * per):
            row_pass(k).wait_recv()
            if k > 0:
                cot_copy(k).wait_recv()
        block = pl.ds(c * M, M)

        def unit_step(u, carry):
            at = pl.ds(pl.multiple_of(u * tile, tile), tile)
            pre = dot(rows[block, :], vei[0, :, at])
            up = dot(rows[block, :], vei[1, :, at])
            d_act = dot_nt(drows[block, :], veo[at, :])
            s = sigmoid(pre)
            gs = pre * s
            act_e[block, at] = (gs * up).astype(bf16)
            dgu_e[0, block, at] = (d_act * up * (s + gs * (1.0 - s))).astype(bf16)
            dgu_e[1, block, at] = (d_act * gs).astype(bf16)
            return carry

        lax.fori_loop(0, F // tile, unit_step, 0)
        dx = dot_nt(dgu_e[0, block, :], vei[0]) + dot_nt(dgu_e[1, block, :], vei[1])
        dxs[block, :] = dx.astype(bf16)
        dx_copy(c).start()

    for k in range(1, G):
        row_copy(k).wait_send()

    def return_chunk(c):
        block = pl.ds(c * M, M)
        dx_copy(c).wait_recv()
        total = (dxs[block, mine].astype(f32) + dxr[block, :].astype(f32)).astype(bf16)
        rets[block, :] = total
        for k in range(c * per, (c + 1) * per):
            if k > 0:
                ret_copy(k).start()
        if c == 0:
            ret[0:C, :] = total[0:C, :]

    chunks = G // per
    for c in range(chunks):
        expert_chunk(c)
        if c > 0:
            return_chunk(c - 1)
    return_chunk(chunks - 1)

    for k in range(1, G):
        cot_copy(k).wait_send()

    def part_step(c, carry):
        block = pl.ds(pl.multiple_of(c * M, M), M)
        part[block, :] = dot(act_e[block, :], veo[...]).astype(bf16)
        return carry

    lax.fori_loop(0, chunks, part_step, 0)
    turned[...] = rows[...].T

    def gein_copy(i):
        at = pl.ds(pl.multiple_of(lax.rem(i, tiles) * tile, tile), tile)
        return pltpu.make_async_copy(
            tall.at[lax.rem(i, 2)], gein.at[i // tiles, :, at], osem.at[lax.rem(i, 2)]
        )

    def gein_step(i, carry):
        @pl.when(i > 1)
        def _():
            gein_copy(i - 2).wait()

        at = pl.ds(pl.multiple_of(lax.rem(i, tiles) * tile, tile), tile)
        tall[lax.rem(i, 2)] = dot(turned[...], dgu_e[i // tiles, :, at])
        gein_copy(i).start()
        return carry

    lax.fori_loop(0, 2 * tiles, gein_step, 0)

    def geout_copy(i):
        at = pl.ds(pl.multiple_of(i * tile, tile), tile)
        return pltpu.make_async_copy(
            wide.at[lax.rem(i, 2)], geout.at[at, :], osem.at[2 + lax.rem(i, 2)]
        )

    def geout_step(i, carry):
        @pl.when(i > 1)
        def _():
            geout_copy(i - 2).wait()

        at = pl.ds(pl.multiple_of(i * tile, tile), tile)
        wide[lax.rem(i, 2)] = dot_tn(act_e[:, at], drows[...])
        geout_copy(i).start()
        return carry

    lax.fori_loop(0, tiles, geout_step, 0)
    gein_copy(2 * tiles - 2).wait()
    gein_copy(2 * tiles - 1).wait()
    geout_copy(tiles - 2).wait()
    geout_copy(tiles - 1).wait()

    dnsh_copy.wait()
    total = dnsh[:, mine].astype(f32) + dnsh_r[...].astype(f32)
    for c in range(chunks):
        for k in range(c * per, (c + 1) * per):
            if k > 0:
                ret_copy(k).wait_recv()
        block = pl.ds(c * M, M)
        total = total + dot_tn(plan[block, :], ret[block, :])
    dnb[:, mine] = total.astype(bf16)
    dnb_copy = send(dnb.at[:, mine], dnb.at[:, mine], s_x.at[5], r_x.at[5], partner)
    dnb_copy.start()
    dnb_copy.wait()

    def dres_step(i, carry):
        at = pl.ds(pl.multiple_of(i * FOLD, FOLD), FOLD)
        y = dnb[at, :].astype(f32)
        x = resid[at, :]
        r = lax.rsqrt(jnp.mean(x * x, axis=1, keepdims=True) + epsilon)
        a = y * nf[...]
        inner = jnp.mean(a * x, axis=1, keepdims=True)
        xr = x * r
        dres[at, :] = cot[at, :].astype(f32) + r * a - xr * (r * r * inner)
        return carry + jnp.sum(y * xr, axis=0, keepdims=True)

    gnf[...] = jnp.broadcast_to(
        lax.fori_loop(0, T // FOLD, dres_step, jnp.zeros((1, D), f32)), gnf.shape
    )
    for k in range(G):
        row_pass(k).wait_send()
    for k in range(1, G):
        ret_copy(k).wait_send()
    for c in range(chunks):
        dx_copy(c).wait_send()


def back_kernel(
    G, tok, na, cos, sin, segr, segc, wqkv, wo, qkv, lse, att_own, normed_a, resid, plan, gate,
    part, shp, dres, gnf, gsh,
    out, gtok, gw1, gw2,
    bias, dresb, da, dqkv, turned, pay, partr, po, ro, shpr, gated, dna, dnar, gna, gnar, ob,
    o1, a1, b1, c1, d1, o2, a2, b2, c2, d2,
    s_x, r_x, s_p, r_p, s_ret, r_ret, s_w, r_w, lsem,
):
    T, D = tok.shape
    HL = wqkv.shape[2]
    C = plan.shape[0] // G
    half = D // 2
    share = D // G
    scale = HD ** (-0.5)
    zs = G // 4
    me, t = lax.axis_index("dp"), lax.axis_index("tensor")
    core, y, z = lax.rem(me, 2), lax.rem(me // 2, 2), me // 4
    mine = pl.ds(pl.multiple_of(t * half, 128), half)
    theirs = pl.ds(pl.multiple_of((1 - t) * half, 128), half)
    partner = (me, 1 - t)
    per = 4
    M = per * C
    chunks = G // per

    def row_at(k):
        return pl.ds(pl.multiple_of(k * C, C), C)

    def fold_core(n, src, a):
        return send(src.at[:, :, 1 - core], a, s_w.at[n, 0], r_w.at[n, 0], (me + 1 - 2 * core, t))

    def fold_y(n, o, b):
        return send(o.at[:, 1 - y], b, s_w.at[n, 1], r_w.at[n, 1], (me + 2 - 4 * y, t))

    def fold_z(n, c, d, k):
        to = lax.rem(z + k, zs)
        return send(
            c.at[to], d.at[k - 1], s_w.at[n, 1 + k], r_w.at[n, 1 + k],
            (to * 4 + lax.rem(me, 4), t),
        )

    def add_core(own, o, a):
        def body(i, carry):
            u, v = i // 2, lax.rem(i, 2)
            first = o[u, v] if own is None else own[u, v, core]
            o[u, v] = (first.astype(f32) + a[u, v].astype(f32)).astype(bf16)
            return carry

        lax.fori_loop(0, 2 * zs, body, 0)

    def add_y(o, b, c):
        def body(i, carry):
            c[i] = (o[i, y].astype(f32) + b[i].astype(f32)).astype(bf16)
            return carry

        lax.fori_loop(0, zs, body, 0)

    def add_z(c, d, w):
        total = c[z].astype(f32)
        for k in range(1, zs):
            total = total + d[k - 1].astype(f32)
        w[...] = total

    def part_copy(c):
        block = pl.ds(c * M, M)
        return send(part.at[block, theirs], partr.at[block], s_p.at[c], r_p.at[c], partner)

    def ret_copy(k):
        return send(
            po.at[row_at(k)], ro.at[row_at(k)], s_ret.at[k], r_ret.at[k],
            (lax.rem(me - k + G, G), t),
        )

    def return_chunk(c):
        block = pl.ds(c * M, M)
        part_copy(c).wait_recv()
        total = (part[block, mine].astype(f32) + partr[block, :].astype(f32)).astype(bf16)
        po[block, :] = total
        for k in range(c * per, (c + 1) * per):
            if k > 0:
                ret_copy(k).start()
        if c == 0:
            ro[0:C, :] = total[0:C, :]

    own1 = pltpu.make_async_copy(gsh.at[:, :, core], o1, lsem.at[0])
    own1.start()
    hello(G)
    core1 = fold_core(0, gsh, a1)
    core1.start()
    for c in range(chunks):
        part_copy(c).start()
    shp_copy = send(shp.at[:, theirs], shpr, s_x.at[0], r_x.at[0], partner)
    shp_copy.start()

    fill_bias(bias, segr, segc, T)
    dresb[...] = dres[...].astype(bf16)
    da[...] = dot_nt(dresb[...], wo[...]).astype(bf16)
    own1.wait()
    core1.wait()
    add_core(None, o1, a1)
    y1 = fold_y(0, o1, b1)
    y1.start()
    lane = lax.broadcasted_iota(jnp.int32, (T, 128), 1)

    def attend(j, carry):
        at = pl.ds(pl.multiple_of(j * 128, 128), 128)
        q, k, v, g = qkv[0, :, at], qkv[1, :, at], qkv[2, :, at], da[:, at]
        none = jnp.zeros_like(q)
        dq = dk = dv = jnp.zeros((T, 128), f32)
        for i in range(2):
            inside = (lane < HD) if i == 0 else (lane >= HD)
            qi, ki, gi = jnp.where(inside, q, none), jnp.where(inside, k, none), jnp.where(inside, g, none)
            total = jnp.sum(jnp.where(lane == 2 * j + i, lse[...], 0.0), axis=1, keepdims=True)
            p = jnp.exp(dot_nt(qi, k) * scale + bias[...] - total)
            dp = dot_nt(gi, v)
            inner = jnp.sum(dp * p, axis=1, keepdims=True)
            ds = (p * (dp - inner)).astype(bf16)
            dv = dv + dot_tn(p.astype(bf16), gi)
            dq = dq + dot(ds, ki)
            dk = dk + dot_tn(ds, qi)
        dq, dk = dq * scale, dk * scale
        dqkv[0, :, at] = (dq * cos[...] - swap_halves(dq) * sin[...]).astype(bf16)
        dqkv[1, :, at] = (dk * cos[...] - swap_halves(dk) * sin[...]).astype(bf16)
        dqkv[2, :, at] = dv.astype(bf16)

        @pl.when(j == 0)
        def _():
            y1.wait()
            add_y(o1, b1, c1)
            for s in range(1, zs):
                fold_z(0, c1, d1, s).start()
            return_chunk(0)
            return_chunk(1)

        @pl.when(j == 1)
        def _():
            return_chunk(2)

        return carry

    lax.fori_loop(0, HL // 128, attend, 0)
    return_chunk(3)

    dna[...] = (dot_nt(dqkv[0], wqkv[0]) + dot_nt(dqkv[1], wqkv[1]) + dot_nt(dqkv[2], wqkv[2])).astype(bf16)
    dna_copy = send(dna, dnar, s_x.at[1], r_x.at[1], partner)
    dna_copy.start()

    def gain_step(i, carry):
        at = pl.ds(pl.multiple_of(i * FOLD, FOLD), FOLD)
        x = tok[at, :].astype(f32)
        r = lax.rsqrt(jnp.mean(x * x, axis=1, keepdims=True) + epsilon)
        return carry + jnp.sum(dna[at, :].astype(f32) * x * r, axis=0, keepdims=True)

    gna[...] = jnp.broadcast_to(
        lax.fori_loop(0, T // FOLD, gain_step, jnp.zeros((1, D), f32)), gna.shape
    )
    gna_copy = send(gna, gnar, s_x.at[3], r_x.at[3], partner)
    gna_copy.start()

    turned[...] = normed_a[...].T
    for s in range(3):
        pay[:, :, :, :, s * HL : (s + 1) * HL] = dot(turned[...], dqkv[s]).astype(bf16).reshape(zs, 2, 2, share, HL)
    turned[...] = dresb[...].T
    pay[:, :, :, :, 3 * HL : 4 * HL] = dot(turned[...], att_own[...]).astype(bf16).reshape(zs, 2, 2, share, HL)
    gna_copy.wait()
    row = lax.broadcasted_iota(jnp.int32, (128, D), 0)
    gains = jnp.where(row == 0, gnf[0:1, :], jnp.where(row == 1, gna[0:1, :] + gnar[0:1, :], 0.0))
    pay[:, :, :, :, 4 * HL :] = gains.T.astype(bf16).reshape(zs, 2, 2, share, 128)
    core2 = fold_core(1, pay, a2)
    core2.start()
    for s in range(1, zs):
        fold_z(0, c1, d1, s).wait()
    add_z(c1, d1, gw1)
    core2.wait()
    add_core(pay, o2, a2)
    y2 = fold_y(1, o2, b2)
    y2.start()

    shp_copy.wait()
    mixed = shp[:, mine].astype(f32) + shpr[...].astype(f32)
    for c in range(chunks):
        for k in range(c * per, (c + 1) * per):
            if k > 0:
                ret_copy(k).wait_recv()
            weights = gate[pl.ds(lax.rem(me + k, G), 1), :]
            gated[(k - c * per) * C : (k - c * per + 1) * C, :] = (
                plan[row_at(k), :].astype(f32) * weights
            ).astype(bf16)
        mixed = mixed + dot_tn(gated[...], ro[c * M : (c + 1) * M, :])
    ob[:, mine] = (resid[:, mine] + mixed).astype(bf16)
    out_copy = send(ob.at[:, mine], ob.at[:, mine], s_x.at[2], r_x.at[2], partner)
    out_copy.start()
    y2.wait()
    add_y(o2, b2, c2)
    for s in range(1, zs):
        fold_z(1, c2, d2, s).start()

    dna_copy.wait()

    def last_step(i, carry):
        at = pl.ds(pl.multiple_of(i * FOLD, FOLD), FOLD)
        x = tok[at, :].astype(f32)
        r = lax.rsqrt(jnp.mean(x * x, axis=1, keepdims=True) + epsilon)
        a = (dna[at, :].astype(f32) + dnar[at, :].astype(f32)) * na[...]
        inner = jnp.mean(a * x, axis=1, keepdims=True)
        gtok[at, :] = (dres[at, :] + r * a - x * (r * r * r * inner)).astype(bf16)
        return carry

    lax.fori_loop(0, T // FOLD, last_step, 0)
    out_copy.wait()
    out[...] = ob[...]
    for s in range(1, zs):
        fold_z(1, c2, d2, s).wait()
    add_z(c2, d2, gw2)
    for c in range(chunks):
        part_copy(c).wait_send()
    for k in range(1, G):
        ret_copy(k).wait_send()


def fused(
    tokens, cont_lengths, routes, route_gates, w_qkv, w_attn_out, norm_attn, norm_ffn,
    shared_in, shared_out, expert_in, expert_out, cotangent,
):
    T, D = tokens.shape
    G = lax.axis_size("dp")
    HL, F, FX = w_qkv.shape[2], shared_in.shape[2], expert_in.shape[2]
    C = round_up(CAP, 16)
    S = G * C
    half, share, zs = D // 2, D // G, G // 4
    row_index = jnp.arange(T, dtype=jnp.int32)
    ends = PROMPT + jnp.cumsum(cont_lengths[0], dtype=jnp.int32)
    later = jnp.sum((row_index[:, None] >= ends[None, :]).astype(jnp.int32), axis=1)
    segment = jnp.where(row_index < PROMPT, 0, 1 + later)
    member = (segment[:, None] == jnp.arange(1, ends.shape[0] + 1, dtype=jnp.int32)[None, :])
    offset = jnp.sum(member.astype(jnp.int32) * (ends - cont_lengths[0])[None, :], axis=1)
    position = jnp.where(segment == 0, row_index, PROMPT + row_index - offset)
    lane = jnp.arange(128, dtype=jnp.int32)
    inv_freq = 10000.0 ** (-(lane % (HD // 2)).astype(f32) / (HD // 2))
    angles = position.astype(f32)[:, None] * inv_freq[None, :]
    cos = jnp.cos(angles)
    sin = jnp.sin(angles) * jnp.where(lane % HD < HD // 2, -1.0, 1.0)[None, :]
    segr, segc = segment[None, :], segment[:, None]
    na, nf = norm_attn[None, :], norm_ffn[None, :]
    rT, gT = routes.T, route_gates.T
    shape = jax.ShapeDtypeStruct
    dma = pltpu.SemaphoreType.DMA
    tile = 256
    front = pl.pallas_call(
        functools.partial(front_kernel, G),
        out_shape=(
            shape((3, T, HL), bf16), shape((T, 128), f32), shape((T, HL), bf16),
            shape((T, D), bf16), shape((T, D), f32), shape((S, T), bf16), shape((EXPERTS, T), f32),
            shape((S, D), bf16), shape((T, D), bf16), shape((T, D), f32), shape((8, D), f32),
            shape((D, 3 * F), bf16), shape((2, D, FX), f32), shape((FX, D), f32),
        ),
        in_specs=[VM] * 12 + [ANY] * 4,
        out_specs=(VM,) * 11 + (ANY,) * 3,
        scratch_shapes=[
            pltpu.VMEM((T, T), f32),
            pltpu.VMEM((T, HL), bf16),
            pltpu.VMEM((HL, D), bf16),
            pltpu.VMEM((EXPERTS, T), f32),
            pltpu.VMEM((S, D), bf16),
            pltpu.VMEM((T, D), bf16),
            pltpu.VMEM((S, D), bf16),
            pltpu.VMEM((2, D, F), bf16),
            pltpu.VMEM((F, D), bf16),
            pltpu.VMEM((2, D, FX), bf16),
            pltpu.VMEM((FX, D), bf16),
            pltpu.VMEM((T, F), bf16),
            pltpu.VMEM((2, T, F), bf16),
            pltpu.VMEM((S, FX), bf16),
            pltpu.VMEM((2, S, FX), bf16),
            pltpu.VMEM((T, D), bf16),
            pltpu.VMEM((T, half), bf16),
            pltpu.VMEM((S, D), bf16),
            pltpu.VMEM((S, half), bf16),
            pltpu.VMEM((S, half), bf16),
            pltpu.VMEM((S, half), bf16),
            pltpu.VMEM((T, D), bf16),
            pltpu.VMEM((D, S), bf16),
            pltpu.VMEM((2, D, tile), f32),
            pltpu.VMEM((2, tile, D), f32),
            pltpu.VMEM((2, D, tile), bf16),
            dma((6,)), dma((6,)), dma((G,)), dma((G,)), dma((G,)), dma((G,)), dma((G,)), dma((G,)),
            dma((4,)), dma((4,)), dma((G,)), dma((G,)), dma((4,)), dma((4,)),
        ],
        compiler_params=pltpu.CompilerParams(
            collective_id=0, has_side_effects=True, vmem_limit_bytes=VMEM_BYTES
        ),
        name="front",
    )(
        tokens, na, nf, cos, sin, segr, segc, rT, gT, w_qkv, w_attn_out, cotangent,
        shared_in, shared_out, expert_in, expert_out,
    )
    qkv, lse, att_own, normed_a, resid, plan, gate, part, shp, dres, gnf, gsh, gein, geout = front
    W1, W2 = 3 * F, 4 * HL + 128
    fold = [(zs, 2, share), (zs, 2, share), (zs, share), (zs, share), (zs - 1, share)]
    out, gtok, gw1, gw2 = pl.pallas_call(
        functools.partial(back_kernel, G),
        out_shape=(
            shape((T, D), bf16), shape((T, D), bf16), shape((share, W1), f32), shape((share, W2), f32),
        ),
        in_specs=[VM] * 19 + [ANY],
        out_specs=(VM,) * 4,
        scratch_shapes=[
            pltpu.VMEM((T, T), f32),
            pltpu.VMEM((T, D), bf16),
            pltpu.VMEM((T, HL), bf16),
            pltpu.VMEM((3, T, HL), bf16),
            pltpu.VMEM((D, T), bf16),
            pltpu.VMEM((zs, 2, 2, share, W2), bf16),
            pltpu.VMEM((S, half), bf16),
            pltpu.VMEM((S, half), bf16),
            pltpu.VMEM((S, half), bf16),
            pltpu.VMEM((T, half), bf16),
            pltpu.VMEM((4 * C, T), bf16),
            pltpu.VMEM((T, D), bf16),
            pltpu.VMEM((T, D), bf16),
            pltpu.VMEM((8, D), f32),
            pltpu.VMEM((8, D), f32),
            pltpu.VMEM((T, D), bf16),
            *[pltpu.VMEM((*s, W1), bf16) for s in fold],
            *[pltpu.VMEM((*s, W2), bf16) for s in fold],
            dma((4,)), dma((4,)), dma((4,)), dma((4,)), dma((G,)), dma((G,)),
            dma((2, 1 + zs)), dma((2, 1 + zs)), dma((1,)),
        ],
        compiler_params=pltpu.CompilerParams(
            collective_id=1, has_side_effects=True, vmem_limit_bytes=VMEM_BYTES
        ),
        name="back",
    )(
        tokens, na, cos, sin, segr, segc, w_qkv, w_attn_out, qkv, lse, att_own, normed_a, resid,
        plan, gate, part, shp, dres, gnf, gsh.reshape(zs, 2, 2, share, W1),
    )
    return (
        out,
        gtok,
        gw2[:, : 3 * HL].reshape(share, 3, HL).transpose(1, 0, 2),
        gw2[:, 3 * HL : 4 * HL].T,
        gw2[:, 4 * HL + 1],
        gw2[:, 4 * HL],
        gw1[:, : 2 * F].reshape(share, 2, F).transpose(1, 0, 2),
        gw1[:, 2 * F :].T,
        gein,
        geout,
    )


def solution(mesh):
    placed = (
        P("dp", None),
        P("dp", None),
        P("dp", None),
        P("dp", None),
        P(None, None, "tensor"),
        P("tensor", None),
        P(),
        P(),
        P(None, None, "tensor"),
        P("tensor", None),
        P(None, None, ("dp", "tensor")),
        P(("dp", "tensor"), None),
        P("dp", None),
    )
    return jax.shard_map(
        fused if mesh.shape["dp"] == EXPERTS else local,
        mesh=mesh,
        in_specs=placed,
        out_specs=(
            P("dp", None),
            P("dp", None),
            P(None, "dp", "tensor"),
            P("tensor", "dp"),
            P("dp"),
            P("dp"),
            P(None, "dp", "tensor"),
            P("tensor", "dp"),
            P(None, None, ("dp", "tensor")),
            P(("dp", "tensor"), None),
        ),
        check_vma=False,
    )
```

```python
import functools
import math

import jax
import jax.numpy as jnp
from jax import lax
from jax.experimental import pallas as pl
from jax.experimental.pallas import tpu as pltpu
from jax.sharding import PartitionSpec as P

HD = 64
EXPERTS = 16
TOP = 2
PROMPT = 64
CAP = 92


epsilon = 1e-06


def rms_parts(values, gain):
    factor = lax.rsqrt(jnp.mean(values * values, axis=-1, keepdims=True) + epsilon)
    return (values * factor * gain, factor)


def rms_back(values, factor, gain, incoming):
    weighted = incoming * gain
    inner = jnp.mean(weighted * values, axis=-1, keepdims=True)
    return (
        factor * weighted - values * factor * factor * factor * inner,
        jnp.sum(incoming * values * factor, axis=0),
    )


def silu_act(values):
    return values * jax.nn.sigmoid(values)


def swiglu_back(gate_up, d_act):
    sigma = jax.nn.sigmoid(gate_up[0])
    d_gate = d_act * gate_up[1] * sigma * (1.0 + gate_up[0] * (1.0 - sigma))
    d_upper = d_act * gate_up[0] * sigma
    return jnp.stack([d_gate, d_upper]).astype(jnp.bfloat16)


def group_layout(lengths, rows_here):
    row_index = jnp.arange(rows_here, dtype=jnp.int32)
    cont_ends = PROMPT + jnp.cumsum(lengths, dtype=jnp.int32)
    begins = cont_ends - lengths
    later = jnp.sum(
        (row_index[:, None] >= cont_ends[None, :]).astype(jnp.int32), axis=1, dtype=jnp.int32
    )
    segment = jnp.where(row_index < PROMPT, 0, 1 + later)
    member = (
        segment[:, None] == jnp.arange(1, lengths.shape[0] + 1, dtype=jnp.int32)[None, :]
    ).astype(jnp.int32)
    offset = jnp.sum(member * begins[None, :], axis=1, dtype=jnp.int32)
    position = jnp.where(segment == 0, row_index, PROMPT + row_index - offset)
    allowed = (row_index[None, :] <= row_index[:, None]) & (
        (segment[None, :] == 0) | (segment[None, :] == segment[:, None])
    )
    return (position, allowed)


def rope_tables(position):
    half_size = HD // 2
    inv_freq = 10000.0 ** (-jnp.arange(half_size, dtype=jnp.float32) / half_size)
    angles = position.astype(jnp.float32)[:, None] * inv_freq[None, :]
    return (jnp.cos(angles)[:, None, :], jnp.sin(angles)[:, None, :])


def rotate_pairs(values, cosine, sine):
    half_size = values.shape[-1] // 2
    front_half = values[..., :half_size]
    back_half = values[..., half_size:]
    return jnp.concatenate(
        [front_half * cosine - back_half * sine, front_half * sine + back_half * cosine], axis=-1
    )


def dispatch_plan(routes):
    flat_routes = routes.reshape(-1)
    one_hot = (flat_routes[:, None] == jnp.arange(EXPERTS, dtype=jnp.int32)[None, :]).astype(
        jnp.int32
    )
    earlier = jnp.cumsum(one_hot, axis=0, dtype=jnp.int32) - one_hot
    place_in = jnp.sum(earlier * one_hot, axis=1, dtype=jnp.int32)
    target = flat_routes * CAP + place_in
    pair_count = flat_routes.shape[0]
    slot_table = (
        jnp.full((EXPERTS * CAP,), pair_count, jnp.int32)
        .at[target]
        .set(jnp.arange(pair_count, dtype=jnp.int32))
    )
    return (target, slot_table)


def spread_rows(padded, indices, copies):
    model_width = padded.shape[1]
    picked = jnp.take(padded, indices, axis=0).reshape(EXPERTS, 1, CAP, model_width)
    return jnp.broadcast_to(picked, (EXPERTS, copies, CAP, model_width)).reshape(
        EXPERTS * copies, CAP, model_width
    )


def collect_rows(returned, target, copies, rows_here):
    model_width = returned.shape[2]
    summed = jnp.sum(returned.reshape(EXPERTS, copies, CAP, model_width), axis=1, dtype=jnp.float32)
    summed = summed.reshape(EXPERTS * CAP, model_width)
    return jnp.take(summed, target, axis=0).reshape(rows_here, TOP, model_width)


def local(
    tokens,
    cont_lengths,
    routes,
    route_gates,
    w_qkv,
    w_attn_out,
    norm_attn,
    norm_ffn,
    shared_in,
    shared_out,
    expert_in,
    expert_out,
    cotangent,
):
    rows_here = tokens.shape[0]
    model_width = tokens.shape[1]
    groups = lax.axis_size("dp")
    copies = groups // EXPERTS
    head_count = w_qkv.shape[2] // HD
    score_scale = HD ** (-0.5)
    inputs = tokens.astype(jnp.float32)
    position, allowed = group_layout(cont_lengths[0], rows_here)
    cosine, sine = rope_tables(position)
    normed_a, factor_a = rms_parts(inputs, norm_attn)
    normed_attn = normed_a.astype(jnp.bfloat16)
    projected = jnp.einsum("td,sdf->stf", normed_attn, w_qkv, preferred_element_type=jnp.float32)
    query = rotate_pairs(projected[0].reshape(rows_here, head_count, HD), cosine, sine).astype(
        jnp.bfloat16
    )
    key_rows = rotate_pairs(projected[1].reshape(rows_here, head_count, HD), cosine, sine).astype(
        jnp.bfloat16
    )
    value_rows = projected[2].reshape(rows_here, head_count, HD).astype(jnp.bfloat16)
    score = (
        jnp.einsum("qhd,khd->hqk", query, key_rows, preferred_element_type=jnp.float32)
        * score_scale
    )
    score = jnp.where(allowed[None], score, -1000000000.0)
    row_max = jnp.max(score, axis=-1, keepdims=True)
    exponent = jnp.exp(score - row_max)
    row_total = jnp.sum(exponent, axis=-1, keepdims=True)
    log_total = row_max + jnp.log(row_total)
    weights_b = (exponent / row_total).astype(jnp.bfloat16)
    attended = jnp.einsum("hqk,khd->qhd", weights_b, value_rows, preferred_element_type=jnp.float32)
    attended = attended.reshape(rows_here, head_count * HD).astype(jnp.bfloat16)
    attn_part = jnp.dot(attended, w_attn_out, preferred_element_type=jnp.float32)
    resid = inputs + lax.psum(attn_part.astype(jnp.bfloat16), "tensor").astype(jnp.float32)
    normed_f, factor_f = rms_parts(resid, norm_ffn)
    normed_ffn = normed_f.astype(jnp.bfloat16)
    gate_up = jnp.einsum("td,sdf->stf", normed_ffn, shared_in, preferred_element_type=jnp.float32)
    shared_act = (silu_act(gate_up[0]) * gate_up[1]).astype(jnp.bfloat16)
    shared_part = jnp.dot(shared_act, shared_out, preferred_element_type=jnp.float32)
    target, slot_table = dispatch_plan(routes)
    padded_rows = jnp.concatenate([normed_ffn, jnp.zeros((1, model_width), jnp.bfloat16)], axis=0)
    send_rows = spread_rows(padded_rows, slot_table // TOP, copies)
    arrived = lax.all_to_all(send_rows, "dp", split_axis=0, concat_axis=0, tiled=True)
    expert_input = arrived.reshape(groups * CAP, model_width)
    expert_gu = jnp.einsum(
        "rd,sdf->srf", expert_input, expert_in, preferred_element_type=jnp.float32
    )
    expert_act = (silu_act(expert_gu[0]) * expert_gu[1]).astype(jnp.bfloat16)
    expert_part = jnp.dot(expert_act, expert_out, preferred_element_type=jnp.float32).astype(
        jnp.bfloat16
    )
    returned = lax.all_to_all(
        expert_part.reshape(groups, CAP, model_width), "dp", split_axis=0, concat_axis=0, tiled=True
    )
    picked = collect_rows(returned, target, copies, rows_here)
    mixed = jnp.sum(route_gates[:, :, None] * picked, axis=1)
    ffn_total = lax.psum((shared_part + mixed).astype(jnp.bfloat16), "tensor").astype(jnp.float32)
    output = (resid + ffn_total).astype(jnp.bfloat16)
    upstream = cotangent.astype(jnp.float32)
    d_shared_act = jnp.einsum(
        "td,fd->tf", cotangent, shared_out, preferred_element_type=jnp.float32
    )
    d_shared_gu = swiglu_back(gate_up, d_shared_act)
    d_normed = jnp.einsum("stf,sdf->td", d_shared_gu, shared_in, preferred_element_type=jnp.float32)
    g_shared_in = jnp.einsum(
        "td,stf->sdf", normed_ffn, d_shared_gu, preferred_element_type=jnp.float32
    )
    g_shared_out = jnp.einsum(
        "tf,td->fd", shared_act, cotangent, preferred_element_type=jnp.float32
    )
    pair_grad = (
        (route_gates[:, :, None] * upstream[:, None, :])
        .reshape(rows_here * TOP, model_width)
        .astype(jnp.bfloat16)
    )
    padded_grad = jnp.concatenate([pair_grad, jnp.zeros((1, model_width), jnp.bfloat16)], axis=0)
    send_grad = spread_rows(padded_grad, slot_table, copies)
    again_rows = spread_rows(padded_rows, slot_table // TOP, copies)
    grad_arrived, rows_arrived = (
        lax.all_to_all(send_grad, "dp", split_axis=0, concat_axis=0, tiled=True),
        lax.all_to_all(again_rows, "dp", split_axis=0, concat_axis=0, tiled=True),
    )
    rows_back = rows_arrived.reshape(groups * CAP, model_width)
    d_expert_rows = grad_arrived.reshape(groups * CAP, model_width)
    back_gu = jnp.einsum("rd,sdf->srf", rows_back, expert_in, preferred_element_type=jnp.float32)
    back_act = (silu_act(back_gu[0]) * back_gu[1]).astype(jnp.bfloat16)
    d_expert_act = jnp.einsum(
        "rd,fd->rf", d_expert_rows, expert_out, preferred_element_type=jnp.float32
    )
    d_expert_gu = swiglu_back(back_gu, d_expert_act)
    d_expert_in = jnp.einsum(
        "srf,sdf->rd", d_expert_gu, expert_in, preferred_element_type=jnp.float32
    ).astype(jnp.bfloat16)
    g_expert_in = jnp.einsum(
        "rd,srf->sdf", rows_back, d_expert_gu, preferred_element_type=jnp.float32
    )
    g_expert_out = jnp.einsum(
        "rf,rd->fd", back_act, d_expert_rows, preferred_element_type=jnp.float32
    )
    d_returned = lax.all_to_all(
        d_expert_in.reshape(groups, CAP, model_width), "dp", split_axis=0, concat_axis=0, tiled=True
    )
    d_normed = d_normed + jnp.sum(collect_rows(d_returned, target, copies, rows_here), axis=1)
    d_normed = lax.psum(d_normed.astype(jnp.bfloat16), "tensor").astype(jnp.float32)
    d_resid_norm, g_norm_ffn = rms_back(resid, factor_f, norm_ffn, d_normed)
    d_resid = upstream + d_resid_norm
    d_resid_b = d_resid.astype(jnp.bfloat16)
    g_attn_out = jnp.einsum("tf,td->fd", attended, d_resid_b, preferred_element_type=jnp.float32)
    d_attended = jnp.einsum("td,fd->tf", d_resid_b, w_attn_out, preferred_element_type=jnp.float32)
    d_attended = d_attended.astype(jnp.bfloat16).reshape(rows_here, head_count, HD)
    recomputed = (
        jnp.einsum("qhd,khd->hqk", query, key_rows, preferred_element_type=jnp.float32)
        * score_scale
    )
    recomputed = jnp.where(allowed[None], recomputed, -1000000000.0)
    probs = jnp.exp(recomputed - log_total)
    probs_b = probs.astype(jnp.bfloat16)
    d_probs = jnp.einsum("qhd,khd->hqk", d_attended, value_rows, preferred_element_type=jnp.float32)
    d_value = jnp.einsum("hqk,qhd->khd", probs_b, d_attended, preferred_element_type=jnp.float32)
    inner = jnp.sum(d_probs * probs, axis=-1, keepdims=True)
    d_score = (probs * (d_probs - inner)).astype(jnp.bfloat16)
    d_query = (
        jnp.einsum("hqk,khd->qhd", d_score, key_rows, preferred_element_type=jnp.float32)
        * score_scale
    )
    d_key = (
        jnp.einsum("hqk,qhd->khd", d_score, query, preferred_element_type=jnp.float32) * score_scale
    )
    d_query = rotate_pairs(d_query, cosine, -sine).reshape(rows_here, head_count * HD)
    d_key = rotate_pairs(d_key, cosine, -sine).reshape(rows_here, head_count * HD)
    d_qkv = jnp.stack([d_query, d_key, d_value.reshape(rows_here, head_count * HD)]).astype(
        jnp.bfloat16
    )
    g_qkv = jnp.einsum("td,stf->sdf", normed_attn, d_qkv, preferred_element_type=jnp.float32)
    d_normed_attn = jnp.einsum("stf,sdf->td", d_qkv, w_qkv, preferred_element_type=jnp.float32)
    d_normed_attn = lax.psum(d_normed_attn.astype(jnp.bfloat16), "tensor").astype(jnp.float32)
    d_input_norm, g_norm_attn = rms_back(inputs, factor_a, norm_attn, d_normed_attn)
    grad_tokens = (d_resid + d_input_norm).astype(jnp.bfloat16)
    summed_all = (
        lax.psum_scatter(g_qkv, "dp", scatter_dimension=1, tiled=True),
        lax.psum_scatter(g_attn_out, "dp", scatter_dimension=1, tiled=True),
        lax.psum_scatter(g_norm_attn, "dp", scatter_dimension=0, tiled=True),
        lax.psum_scatter(g_shared_in, "dp", scatter_dimension=1, tiled=True),
        lax.psum_scatter(g_shared_out, "dp", scatter_dimension=1, tiled=True),
        lax.psum_scatter(g_norm_ffn, "dp", scatter_dimension=0, tiled=True),
    )
    return (
        output,
        grad_tokens,
        summed_all[0],
        summed_all[1],
        summed_all[2],
        summed_all[5],
        summed_all[3],
        summed_all[4],
        g_expert_in,
        g_expert_out,
    )


VMEM_BYTES = 64000 * 1024
FOLD = 96
SPLIT = 7
MESH = pl.DeviceIdType.MESH
VM = pl.BlockSpec(memory_space=pltpu.VMEM)
ANY = pl.BlockSpec(memory_space=pl.ANY)
f32 = jnp.float32
bf16 = jnp.bfloat16


def round_up(value, unit):
    return (value + unit - 1) // unit * unit


def dot(a, b):
    return jnp.dot(a, b, preferred_element_type=f32)


def dot_nt(a, b):
    return lax.dot_general(a, b, (((1,), (1,)), ((), ())), preferred_element_type=f32)


def dot_tn(a, b):
    return lax.dot_general(a, b, (((0,), (0,)), ((), ())), preferred_element_type=f32)


def sigmoid(values):
    return 0.5 * jnp.tanh(0.5 * values) + 0.5


def swap_halves(values):
    lane = lax.broadcasted_iota(jnp.int32, values.shape, 1)
    ahead = pltpu.roll(values, values.shape[1] - HD // 2, 1)
    behind = pltpu.roll(values, HD // 2, 1)
    return jnp.where(lax.rem(lane, HD) < HD // 2, ahead, behind)


def hello(groups):
    me, t = lax.axis_index("dp"), lax.axis_index("tensor")
    barrier = pltpu.get_barrier_semaphore()

    def greet(k, carry):
        pl.semaphore_signal(
            barrier, inc=1, device_id=(lax.rem(me + k, groups), t), device_id_type=MESH
        )
        return carry

    lax.fori_loop(1, groups, greet, 0)
    pl.semaphore_signal(barrier, inc=1, device_id=(me, 1 - t), device_id_type=MESH)
    pl.semaphore_wait(barrier, groups)


def segment_of(index, lens):
    segment = jnp.where(index < PROMPT, 0, 1)
    end = PROMPT
    for c in range(lens.shape[1]):
        end = end + lens[0, c]
        segment = segment + jnp.where(index >= end, 1, 0)
    return segment


def position_of(index, lens):
    segment = segment_of(index, lens)
    position, end = index, PROMPT
    for c in range(lens.shape[1]):
        position = jnp.where(segment == c + 1, PROMPT + index - end, position)
        end = end + lens[0, c]
    return position


def fill_bias(bias, lens, rows):
    step = FOLD

    def body(i, carry):
        at = pl.ds(pl.multiple_of(i * step, step), step)
        row = lax.broadcasted_iota(jnp.int32, (step, rows), 0) + i * step
        col = lax.broadcasted_iota(jnp.int32, (step, rows), 1)
        own = segment_of(lax.broadcasted_iota(jnp.int32, (step, 1), 0) + i * step, lens)
        other = segment_of(lax.broadcasted_iota(jnp.int32, (1, rows), 1), lens)
        ok = (col <= row) & ((other == 0) | (other == own))
        bias[at, :] = jnp.where(ok, 0.0, -1000000000.0)
        return carry

    lax.fori_loop(0, rows // step, body, 0)


def fill_angles(cos, sin, lens, rows):
    step = FOLD

    def body(i, carry):
        at = pl.ds(pl.multiple_of(i * step, step), step)
        lane = lax.broadcasted_iota(jnp.int32, (step, 128), 1)
        row = lax.broadcasted_iota(jnp.int32, (step, 128), 0) + i * step
        power = lax.rem(lane, HD // 2).astype(f32) * (-math.log(10000.0) / (HD // 2))
        angle = position_of(row, lens).astype(f32) * jnp.exp(power)
        cos[at, :] = jnp.cos(angle)
        sine = jnp.sin(angle)
        sin[at, :] = jnp.where(lax.rem(lane, HD) < HD // 2, -sine, sine)
        return carry

    lax.fori_loop(0, rows // step, body, 0)


def send(src, dst, ssem, rsem, to):
    return pltpu.make_async_remote_copy(
        src_ref=src, dst_ref=dst, send_sem=ssem, recv_sem=rsem, device_id=to, device_id_type=MESH
    )


def front_kernel(
    G, na, nf, lens, rT, gT, h_tok, h_wqkv, h_wo, h_cot, si, so, ei, eo,
    h_qkv, h_lse, h_att, h_normed_a, h_resid, h_plan, h_gate, h_cos, h_sin, h_part, h_shp, h_dres, h_gnf,
    gsh, gein, geout,
    tok, wqkv, wo, cot, cos, sin,
    qkv, lse, att_own, normed_a, resid, plan, gate, part, shp, dres, gnf,
    bias, att, wo2, slot, drows, normed, rows, vsi, vso, vei, veo,
    act_s, dgu_s, act_e, dgu_e, dnsh, dnsh_r, dxs, dxr, rets, ret, dnb, turned, tall, wide, pale,
    s_x, r_x, s_c, r_c, s_cf, r_cf, s_r, r_r, s_f, r_f, s_dx, r_dx, s_ret, r_ret, lsem, osem, ksem,
):
    T, D = tok.shape
    HL = wqkv.shape[2]
    F = si.shape[2]
    C = plan.shape[0] // G
    half = D // 2
    scale = HD ** (-0.5)
    me, t = lax.axis_index("dp"), lax.axis_index("tensor")
    mine = pl.ds(pl.multiple_of(t * half, 128), half)
    theirs = pl.ds(pl.multiple_of((1 - t) * half, 128), half)
    partner = (me, 1 - t)

    core = lax.rem(me, 2)
    loads = [
        pltpu.make_async_copy(a, b, lsem.at[i])
        for i, (a, b) in enumerate(
            ((h_cot, cot), (h_tok, tok), (h_wqkv, wqkv), (h_wo, wo), (si, vsi), (so, vso), (ei, vei), (eo, veo))
        )
    ]
    for c in loads:
        c.start()
    keeps = [
        pltpu.make_async_copy(a, b, ksem.at[i])
        for i, (a, b) in enumerate(
            (
                (qkv, h_qkv), (lse, h_lse), (att_own, h_att), (normed_a, h_normed_a), (resid, h_resid),
                (plan, h_plan), (gate, h_gate), (cos, h_cos), (sin, h_sin), (part, h_part), (shp, h_shp),
                (dres, h_dres), (gnf, h_gnf),
            )
        )
    ]
    hello(G)
    part_wo = pl.ds(pl.multiple_of(core * (HL // 2), 16), HL // 2)
    wo_copy = send(h_wo.at[part_wo], wo2.at[part_wo], s_x.at[0], r_x.at[0], partner)
    wo_copy.start()
    wo_pass = send(
        wo2.at[part_wo], wo2.at[part_wo], s_x.at[6], r_x.at[6], (me + 1 - 2 * core, t)
    )

    names = lax.broadcasted_iota(jnp.int32, (EXPERTS, T), 0)
    picks0, picks1 = rT[0:1, :] == names, rT[1:2, :] == names
    member = jnp.where(picks0 | picks1, 1.0, 0.0)
    upper = jnp.where(
        lax.broadcasted_iota(jnp.int32, (T, T), 0) < lax.broadcasted_iota(jnp.int32, (T, T), 1),
        1.0,
        0.0,
    ).astype(bf16)
    slot[...] = jnp.where(member > 0.0, dot(member.astype(bf16), upper), -1.0)
    gate[...] = jnp.where(picks0, gT[0:1, :], 0.0) + jnp.where(picks1, gT[1:2, :], 0.0)

    def row_at(k):
        return pl.ds(pl.multiple_of(k * C, C), C)

    def cot_copy(k):
        return send(
            part.at[row_at(k)], drows.at[row_at(k)], s_c.at[k], r_c.at[k], (lax.rem(me + k, G), t)
        )

    def cot_half(k):
        return send(
            part.at[row_at(k), mine], drows.at[row_at(k), mine], s_c.at[k], r_c.at[k],
            (lax.rem(me + k, G), t),
        )

    def cot_pass(k):
        return send(
            drows.at[row_at(k), mine], drows.at[row_at(k), mine], s_cf.at[k], r_cf.at[k], partner
        )

    def cot_step(k, carry):
        e = lax.rem(me + k, G)
        at = pl.ds(pl.multiple_of(k * C, C), C)
        place = lax.broadcasted_iota(jnp.int32, (C, T), 0).astype(f32)
        hit = slot[pl.ds(e, 1), :] == place
        picked = jnp.where(hit, 1.0, 0.0).astype(bf16)
        plan[at, :] = picked
        weight = jnp.sum(jnp.where(hit, gate[pl.ds(e, 1), :], 0.0), axis=1, keepdims=True)
        grad = (dot(picked, cot[...]) * weight).astype(bf16)
        part[at, :] = grad

        @pl.when(k > SPLIT)
        def _():
            cot_copy(k).start()

        @pl.when((k > 0) & (k <= SPLIT))
        def _():
            cot_half(k).start()

        @pl.when(k == 0)
        def _():
            drows[at, :] = grad

        return carry

    loads[0].wait()
    lax.fori_loop(0, G, cot_step, 0)
    keeps[5].start()
    keeps[6].start()

    fill_angles(cos, sin, lens, T)
    keeps[7].start()
    keeps[8].start()
    fill_bias(bias, lens, T)
    loads[1].wait()

    def norm_step(i, carry):
        at = pl.ds(pl.multiple_of(i * FOLD, FOLD), FOLD)
        x = tok[at, :].astype(f32)
        r = lax.rsqrt(jnp.mean(x * x, axis=1, keepdims=True) + epsilon)
        normed_a[at, :] = (x * r * na[...].reshape(1, D)).astype(bf16)
        return carry

    lax.fori_loop(0, T // FOLD, norm_step, 0)
    keeps[3].start()
    loads[2].wait()
    loads[3].wait()

    def project(s, turned):
        full = dot(normed_a[...], wqkv[s])
        for j in range(HL // 128):
            x = full[:, j * 128 : (j + 1) * 128]
            if turned:
                x = x * cos[...] + swap_halves(x) * sin[...]
            qkv[s, :, j * 128 : (j + 1) * 128] = x.astype(bf16)

    project(0, True)
    project(1, True)
    project(2, False)
    keeps[0].start()
    lane = lax.broadcasted_iota(jnp.int32, (T, 128), 1)

    def att_copy(j):
        at = pl.ds(pl.multiple_of(j * 128, 128), 128)
        return send(att_own.at[:, at], att.at[:, at], s_x.at[1 + j], r_x.at[1 + j], partner)

    lse[...] = jnp.zeros_like(lse)

    def attend(j, carry):
        at = pl.ds(pl.multiple_of(j * 128, 128), 128)
        q, k, v = qkv[0, :, at], qkv[1, :, at], qkv[2, :, at]
        outs = []
        for i in range(2):
            inside = (lane < HD) if i == 0 else (lane >= HD)
            s = dot_nt(jnp.where(inside, q, jnp.zeros_like(q)), k) * scale + bias[...]
            top = jnp.max(s, axis=1, keepdims=True)
            e = jnp.exp(s - top)
            total = jnp.sum(e, axis=1, keepdims=True)
            p = (e * (1.0 / total)).astype(bf16)
            lse[...] = jnp.where(lane == 2 * j + i, top + jnp.log(total), lse[...])
            outs.append(dot(p, v))
        att_own[:, at] = jnp.where(lane < HD, outs[0], outs[1]).astype(bf16)
        att_copy(j).start()
        return carry

    wo_copy.wait()
    wo_pass.start()
    lax.fori_loop(0, HL // 128, attend, 0)
    keeps[1].start()
    keeps[2].start()
    own_out = dot(att_own[...], wo[...])
    wo_pass.wait()
    for j in range(HL // 128):
        att_copy(j).wait()
    for k in range(1, SPLIT + 1):
        cot_half(k).wait_recv()
        cot_pass(k).start()
    resid[...] = tok[...].astype(f32) + own_out + dot(att[...], wo2[...])

    def norm2_step(i, carry):
        at = pl.ds(pl.multiple_of(i * FOLD, FOLD), FOLD)
        x = resid[at, :]
        r = lax.rsqrt(jnp.mean(x * x, axis=1, keepdims=True) + epsilon)
        normed[at, :] = (x * r * nf[...].reshape(1, D)).astype(bf16)
        return carry

    lax.fori_loop(0, T // FOLD, norm2_step, 0)
    keeps[4].start()

    def row_copy(k):
        return send(
            rets.at[row_at(k)], rows.at[row_at(k), mine], s_r.at[k], r_r.at[k], (lax.rem(me + k, G), t)
        )

    def row_pass(k):
        return send(
            rows.at[row_at(k), mine], rows.at[row_at(k), mine], s_f.at[k], r_f.at[k], partner
        )

    def row_step(k, carry):
        values = dot(plan[row_at(k), :], normed[:, mine]).astype(bf16)
        rets[row_at(k), :] = values

        @pl.when(k > 0)
        def _():
            row_copy(k).start()

        @pl.when(k == 0)
        def _():
            rows[row_at(k), mine] = values
            row_pass(k).start()

        return carry

    lax.fori_loop(0, G, row_step, 0)

    loads[4].wait()
    loads[5].wait()
    tile = 256
    tiles = F // tile

    def hand_on(k):
        row_copy(k).wait_recv()
        row_pass(k).start()

    def shared_step(u, carry):
        at = pl.ds(pl.multiple_of(u * tile, tile), tile)
        pre = dot(normed[...], vsi[0, :, at])
        up = dot(normed[...], vsi[1, :, at])
        d_act = dot_nt(cot[...], vso[at, :])
        s = sigmoid(pre)
        gs = pre * s
        act_s[:, at] = (gs * up).astype(bf16)
        dgu_s[0, :, at] = (d_act * up * (s + gs * (1.0 - s))).astype(bf16)
        dgu_s[1, :, at] = (d_act * gs).astype(bf16)
        return carry

    side = round_up(T, 128)

    def gsh_copy(i):
        at = pl.ds(pl.multiple_of(i * tile, tile), tile)
        return pltpu.make_async_copy(pale.at[lax.rem(i, 2)], gsh.at[:, at], osem.at[lax.rem(i, 2)])

    def gsh_step(i, carry):
        @pl.when(i > 1)
        def _():
            gsh_copy(i - 2).wait()

        u = lax.rem(i, tiles)
        at = pl.ds(pl.multiple_of(u * tile, tile), tile)

        @pl.when(i < 2 * tiles)
        def _():
            pale[lax.rem(i, 2)] = dot(turned[:, 0:T], dgu_s[i // tiles, :, at]).astype(bf16)

        @pl.when(i >= 2 * tiles)
        def _():
            pale[lax.rem(i, 2)] = dot(turned[:, side : side + T], act_s[:, at]).astype(bf16)

        gsh_copy(i).start()
        return carry

    per = 4
    M = per * C
    chunks = G // per

    def dx_copy(c):
        at = pl.ds(pl.multiple_of(c * M, M), M)
        return send(dxs.at[at, theirs], dxr.at[at], s_dx.at[c], r_dx.at[c], partner)

    def ret_copy(k):
        return send(
            rets.at[row_at(k)], ret.at[row_at(k)], s_ret.at[k], r_ret.at[k],
            (lax.rem(me - k + G, G), t),
        )

    def expert_chunk(c):
        for k in range(c * per, (c + 1) * per):
            row_pass(k).wait_recv()
            if k > SPLIT:
                cot_copy(k).wait_recv()
            elif k > 0:
                cot_pass(k).wait_recv()
        block = pl.ds(c * M, M)

        def unit_step(u, carry):
            at = pl.ds(pl.multiple_of(u * tile, tile), tile)
            pre = dot(rows[block, :], vei[0, :, at])
            up = dot(rows[block, :], vei[1, :, at])
            d_act = dot_nt(drows[block, :], veo[at, :])
            s = sigmoid(pre)
            gs = pre * s
            act_e[block, at] = (gs * up).astype(bf16)
            dgu_e[0, block, at] = (d_act * up * (s + gs * (1.0 - s))).astype(bf16)
            dgu_e[1, block, at] = (d_act * gs).astype(bf16)
            return carry

        lax.fori_loop(0, F // tile, unit_step, 0)
        dx = dot_nt(dgu_e[0, block, :], vei[0]) + dot_nt(dgu_e[1, block, :], vei[1])
        dxs[block, :] = dx.astype(bf16)
        dx_copy(c).start()

    def return_chunk(c):
        block = pl.ds(c * M, M)
        dx_copy(c).wait_recv()
        total = (dxs[block, mine].astype(f32) + dxr[block, :].astype(f32)).astype(bf16)
        for k in range(c * per, (c + 1) * per):
            if k > 0:
                row_copy(k).wait_send()
        rets[block, :] = total
        for k in range(c * per, (c + 1) * per):
            if k > 0:
                ret_copy(k).start()
        if c == 0:
            ret[0:C, :] = total[0:C, :]

    lax.fori_loop(0, F // tile, shared_step, 0)
    for k in range(1, 4):
        hand_on(k)
    dnsh[...] = (dot_nt(dgu_s[0], vsi[0]) + dot_nt(dgu_s[1], vsi[1])).astype(bf16)
    dnsh_copy = send(dnsh.at[:, theirs], dnsh_r, s_x.at[4], r_x.at[4], partner)
    loads[6].wait()
    loads[7].wait()
    for k in range(4, 6):
        hand_on(k)
    expert_chunk(0)
    for k in range(6, 8):
        hand_on(k)
    shp[...] = dot(act_s[...], vso[...]).astype(bf16)
    keeps[10].start()
    turned[:, 0:T] = normed[...].T
    turned[:, side : side + T] = cot[...].T
    return_chunk(0)
    expert_chunk(1)
    for k in range(8, 12):
        hand_on(k)
    lax.fori_loop(0, 2 * tiles, gsh_step, 0)
    return_chunk(1)
    expert_chunk(2)
    for k in range(12, G):
        hand_on(k)
    dnsh_copy.start()
    lax.fori_loop(2 * tiles, 3 * tiles, gsh_step, 0)
    return_chunk(2)
    expert_chunk(3)
    gsh_copy(3 * tiles - 2).wait()
    gsh_copy(3 * tiles - 1).wait()

    for k in range(1, G):
        (cot_copy(k) if k > SPLIT else cot_half(k)).wait_send()

    def part_step(c, carry):
        block = pl.ds(pl.multiple_of(c * M, M), M)
        part[block, :] = dot(act_e[block, :], veo[...]).astype(bf16)
        return carry

    lax.fori_loop(0, chunks, part_step, 0)
    keeps[9].start()
    return_chunk(3)
    turned[...] = rows[...].T

    def gein_copy(i):
        at = pl.ds(pl.multiple_of(lax.rem(i, tiles) * tile, tile), tile)
        return pltpu.make_async_copy(
            tall.at[lax.rem(i, 2)], gein.at[i // tiles, :, at], osem.at[lax.rem(i, 2)]
        )

    def gein_step(i, carry):
        @pl.when(i > 1)
        def _():
            gein_copy(i - 2).wait()

        at = pl.ds(pl.multiple_of(lax.rem(i, tiles) * tile, tile), tile)
        tall[lax.rem(i, 2)] = dot(turned[...], dgu_e[i // tiles, :, at]).astype(bf16)
        gein_copy(i).start()
        return carry

    lax.fori_loop(0, 2 * tiles, gein_step, 0)

    def geout_copy(i):
        at = pl.ds(pl.multiple_of(i * tile, tile), tile)
        return pltpu.make_async_copy(
            wide.at[lax.rem(i, 2)], geout.at[at, :], osem.at[2 + lax.rem(i, 2)]
        )

    def geout_step(i, carry):
        @pl.when(i > 1)
        def _():
            geout_copy(i - 2).wait()

        at = pl.ds(pl.multiple_of(i * tile, tile), tile)
        wide[lax.rem(i, 2)] = dot_tn(act_e[:, at], drows[...]).astype(bf16)
        geout_copy(i).start()
        return carry

    lax.fori_loop(0, tiles, geout_step, 0)
    gein_copy(2 * tiles - 2).wait()
    gein_copy(2 * tiles - 1).wait()
    geout_copy(tiles - 2).wait()
    geout_copy(tiles - 1).wait()

    dnsh_copy.wait()
    total = dnsh[:, mine].astype(f32) + dnsh_r[...].astype(f32)
    for c in range(chunks):
        for k in range(c * per, (c + 1) * per):
            if k > 0:
                ret_copy(k).wait_recv()
        block = pl.ds(c * M, M)
        total = total + dot_tn(plan[block, :], ret[block, :])
    dnb[:, mine] = total.astype(bf16)
    dnb_copy = send(dnb.at[:, mine], dnb.at[:, mine], s_x.at[5], r_x.at[5], partner)
    dnb_copy.start()
    dnb_copy.wait()

    def dres_step(i, carry):
        at = pl.ds(pl.multiple_of(i * FOLD, FOLD), FOLD)
        y = dnb[at, :].astype(f32)
        x = resid[at, :]
        r = lax.rsqrt(jnp.mean(x * x, axis=1, keepdims=True) + epsilon)
        a = y * nf[...].reshape(1, D)
        inner = jnp.mean(a * x, axis=1, keepdims=True)
        xr = x * r
        dres[at, :] = cot[at, :].astype(f32) + r * a - xr * (r * r * inner)
        return carry + jnp.sum(y * xr, axis=0, keepdims=True)

    gnf[...] = jnp.broadcast_to(
        lax.fori_loop(0, T // FOLD, dres_step, jnp.zeros((1, D), f32)), gnf.shape
    )
    keeps[11].start()
    keeps[12].start()
    for k in range(G):
        row_pass(k).wait_send()
    for k in range(1, SPLIT + 1):
        cot_pass(k).wait_send()
    for k in range(1, G):
        ret_copy(k).wait_send()
    for c in range(chunks):
        dx_copy(c).wait_send()
    for c in keeps:
        c.wait()


def back_kernel(
    G, na, lens, h_tok, h_wqkv, h_wo, h_qkv, h_lse, h_att, h_normed_a, h_resid, h_plan, h_gate,
    h_cos, h_sin, h_part, h_shp, h_dres, h_gnf, gsh,
    out, gtok, gw1, gw2,
    tok, wqkv, wo, qkv, lse, att_own, normed_a, resid, plan, gate, cos, sin, part, shp, dres, gnf,
    bias, dresb, da, dqkv, turned, pay, partr, po, ro, shpr, gated, dna, dnar, gna, gnar, ob,
    o1, a1, b1, c1, d1, o2, a2, b2, c2, d2,
    s_x, r_x, s_p, r_p, s_ret, r_ret, s_w, r_w, lsem,
):
    T, D = tok.shape
    HL = wqkv.shape[2]
    C = plan.shape[0] // G
    half = D // 2
    share = D // G
    scale = HD ** (-0.5)
    zs = G // 4
    me, t = lax.axis_index("dp"), lax.axis_index("tensor")
    core, y, z = lax.rem(me, 2), lax.rem(me // 2, 2), me // 4
    mine = pl.ds(pl.multiple_of(t * half, 128), half)
    theirs = pl.ds(pl.multiple_of((1 - t) * half, 128), half)
    partner = (me, 1 - t)
    per = 4
    M = per * C
    chunks = G // per

    def row_at(k):
        return pl.ds(pl.multiple_of(k * C, C), C)

    def fold_core(n, src, a):
        return send(src.at[:, :, 1 - core], a, s_w.at[n, 0], r_w.at[n, 0], (me + 1 - 2 * core, t))

    def fold_y(n, o, b, cols):
        return send(
            o.at[:, 1 - y, :, cols], b.at[:, :, cols], s_w.at[n, 1], r_w.at[n, 1], (me + 2 - 4 * y, t)
        )

    def fold_z(n, c, d, cols, k):
        to = lax.rem(z + k, zs)
        return send(
            c.at[to, :, cols], d.at[k - 1, :, cols], s_w.at[n, 1 + k], r_w.at[n, 1 + k],
            (to * 4 + lax.rem(me, 4), t),
        )

    def add_core(own, o, a):
        def body(i, carry):
            u, v = i // 2, lax.rem(i, 2)
            first = o[u, v] if own is None else own[u, v, core]
            o[u, v] = (first.astype(f32) + a[u, v].astype(f32)).astype(bf16)
            return carry

        lax.fori_loop(0, 2 * zs, body, 0)

    def add_y(o, b, c, cols):
        def body(i, carry):
            c[i, :, cols] = (o[i, y, :, cols].astype(f32) + b[i, :, cols].astype(f32)).astype(bf16)
            return carry

        lax.fori_loop(0, zs, body, 0)

    def add_z(c, d, w, cols):
        total = c[z, :, cols].astype(f32)
        for k in range(1, zs):
            total = total + d[k - 1, :, cols].astype(f32)
        w[:, cols] = total

    def part_copy(c):
        block = pl.ds(c * M, M)
        return send(h_part.at[block, theirs], partr.at[block], s_p.at[c], r_p.at[c], partner)

    def ret_copy(k):
        return send(
            po.at[row_at(k)], ro.at[row_at(k)], s_ret.at[k], r_ret.at[k],
            (lax.rem(me - k + G, G), t),
        )

    def return_chunk(c):
        block = pl.ds(c * M, M)
        part_copy(c).wait_recv()
        total = (part[block, :].astype(f32) + partr[block, :].astype(f32)).astype(bf16)
        po[block, :] = total
        for k in range(c * per, (c + 1) * per):
            if k > 0:
                ret_copy(k).start()
        if c == 0:
            ro[0:C, :] = total[0:C, :]

    pairs = (
        (h_dres, dres), (h_wo, wo), (h_qkv, qkv), (h_lse, lse), (h_cos, cos), (h_sin, sin),
        (gsh.at[:, :, core], o1), (h_part.at[:, mine], part), (h_wqkv, wqkv), (h_tok, tok),
        (h_normed_a, normed_a), (h_att, att_own), (h_gnf, gnf), (h_shp.at[:, mine], shp),
        (h_plan, plan), (h_gate, gate), (h_resid.at[:, mine], resid),
    )
    loads = [pltpu.make_async_copy(a, b, lsem.at[i]) for i, (a, b) in enumerate(pairs)]
    for c in loads:
        c.start()
    hello(G)
    core1 = fold_core(0, gsh, a1)
    core1.start()
    for c in range(chunks):
        part_copy(c).start()

    fill_bias(bias, lens, T)
    loads[0].wait()
    loads[1].wait()
    dresb[...] = dres[...].astype(bf16)
    da[...] = dot_nt(dresb[...], wo[...]).astype(bf16)
    loads[6].wait()
    core1.wait()
    add_core(None, o1, a1)
    W1 = gw1.shape[1]
    halves = [slice(i * (W1 // 2), (i + 1) * (W1 // 2)) for i in range(2)]
    ys = [fold_y(i, o1, b1, halves[i]) for i in range(2)]
    for c in ys:
        c.start()
    for i in range(2, 6):
        loads[i].wait()
    lane = lax.broadcasted_iota(jnp.int32, (T, 128), 1)

    def attend(j, carry):
        at = pl.ds(pl.multiple_of(j * 128, 128), 128)
        q, k, v, g = qkv[0, :, at], qkv[1, :, at], qkv[2, :, at], da[:, at]
        none = jnp.zeros_like(q)
        dq = dk = dv = jnp.zeros((T, 128), f32)
        for i in range(2):
            inside = (lane < HD) if i == 0 else (lane >= HD)
            qi, ki, gi = jnp.where(inside, q, none), jnp.where(inside, k, none), jnp.where(inside, g, none)
            total = jnp.sum(jnp.where(lane == 2 * j + i, lse[...], 0.0), axis=1, keepdims=True)
            p = jnp.exp(dot_nt(qi, k) * scale + bias[...] - total)
            dp = dot_nt(gi, v)
            inner = jnp.sum(dp * p, axis=1, keepdims=True)
            ds = (p * (dp - inner)).astype(bf16)
            dv = dv + dot_tn(p.astype(bf16), gi)
            dq = dq + dot(ds, ki)
            dk = dk + dot_tn(ds, qi)
        dq, dk = dq * scale, dk * scale
        dqkv[0, :, at] = (dq * cos[...] - swap_halves(dq) * sin[...]).astype(bf16)
        dqkv[1, :, at] = (dk * cos[...] - swap_halves(dk) * sin[...]).astype(bf16)
        dqkv[2, :, at] = dv.astype(bf16)

        return carry

    lax.fori_loop(0, HL // 128, attend, 0)
    loads[7].wait()
    loads[8].wait()

    dna[...] = (dot_nt(dqkv[0], wqkv[0]) + dot_nt(dqkv[1], wqkv[1]) + dot_nt(dqkv[2], wqkv[2])).astype(bf16)
    dna_copy = send(dna, dnar, s_x.at[1], r_x.at[1], partner)
    return_chunk(0)
    return_chunk(1)
    dna_copy.start()
    shp_copy = send(h_shp.at[:, theirs], shpr, s_x.at[0], r_x.at[0], partner)
    shp_copy.start()
    for i in range(9, 13):
        loads[i].wait()

    def fold_on(i):
        ys[i].wait()
        add_y(o1, b1, c1, halves[i])
        for s in range(1, zs):
            fold_z(i, c1, d1, halves[i], s).start()

    def gain_step(i, carry):
        at = pl.ds(pl.multiple_of(i * FOLD, FOLD), FOLD)
        x = tok[at, :].astype(f32)
        r = lax.rsqrt(jnp.mean(x * x, axis=1, keepdims=True) + epsilon)
        return carry + jnp.sum(dna[at, :].astype(f32) * x * r, axis=0, keepdims=True)

    gna[...] = jnp.broadcast_to(
        lax.fori_loop(0, T // FOLD, gain_step, jnp.zeros((1, D), f32)), gna.shape
    )
    gna_copy = send(gna, gnar, s_x.at[3], r_x.at[3], partner)
    gna_copy.start()
    return_chunk(2)

    turned[...] = normed_a[...].T
    for s in range(3):
        pay[:, :, :, :, s * HL : (s + 1) * HL] = dot(turned[...], dqkv[s]).astype(bf16).reshape(zs, 2, 2, share, HL)
    fold_on(0)
    return_chunk(3)
    turned[...] = dresb[...].T
    pay[:, :, :, :, 3 * HL : 4 * HL] = dot(turned[...], att_own[...]).astype(bf16).reshape(zs, 2, 2, share, HL)
    gna_copy.wait()
    row = lax.broadcasted_iota(jnp.int32, (128, D), 0)
    gains = jnp.where(row == 0, gnf[0:1, :], jnp.where(row == 1, gna[0:1, :] + gnar[0:1, :], 0.0))
    pay[:, :, :, :, 4 * HL :] = gains.T.astype(bf16).reshape(zs, 2, 2, share, 128)
    core2 = fold_core(2, pay, a2)
    core2.start()
    fold_on(1)
    core2.wait()
    add_core(pay, o2, a2)
    every = slice(0, gw2.shape[1])
    y2 = fold_y(2, o2, b2, every)
    y2.start()

    for i in range(13, 17):
        loads[i].wait()
    shp_copy.wait()
    mixed = shp[...].astype(f32) + shpr[...].astype(f32)
    for c in range(chunks):
        for k in range(c * per, (c + 1) * per):
            if k > 0:
                ret_copy(k).wait_recv()
            weights = gate[pl.ds(lax.rem(me + k, G), 1), :]
            gated[(k - c * per) * C : (k - c * per + 1) * C, :] = (
                plan[row_at(k), :].astype(f32) * weights
            ).astype(bf16)
        mixed = mixed + dot_tn(gated[...], ro[c * M : (c + 1) * M, :])
    ob[:, mine] = (resid[...] + mixed).astype(bf16)
    out_copy = send(ob.at[:, mine], ob.at[:, mine], s_x.at[2], r_x.at[2], partner)
    out_copy.start()
    y2.wait()
    add_y(o2, b2, c2, every)
    for s in range(1, zs):
        fold_z(2, c2, d2, every, s).start()
    for i in range(2):
        for s in range(1, zs):
            fold_z(i, c1, d1, halves[i], s).wait()
        add_z(c1, d1, gw1, halves[i])

    dna_copy.wait()

    def last_step(i, carry):
        at = pl.ds(pl.multiple_of(i * FOLD, FOLD), FOLD)
        x = tok[at, :].astype(f32)
        r = lax.rsqrt(jnp.mean(x * x, axis=1, keepdims=True) + epsilon)
        a = (dna[at, :].astype(f32) + dnar[at, :].astype(f32)) * na[...].reshape(1, D)
        inner = jnp.mean(a * x, axis=1, keepdims=True)
        gtok[at, :] = (dres[at, :] + r * a - x * (r * r * r * inner)).astype(bf16)
        return carry

    lax.fori_loop(0, T // FOLD, last_step, 0)
    out_copy.wait()
    out[...] = ob[...]
    for s in range(1, zs):
        fold_z(2, c2, d2, every, s).wait()
    add_z(c2, d2, gw2, every)
    for c in range(chunks):
        part_copy(c).wait_send()
    for k in range(1, G):
        ret_copy(k).wait_send()


def finish_kernel(
    HL, F, h_out, h_gtok, h_gw1, h_gw2, h_gein, h_geout,
    out, gtok, gqkv, gao, gna, gnf, gsi, gso, gein, geout,
):
    out[...] = h_out[...]
    gtok[...] = h_gtok[...]
    gein[...] = h_gein[...].astype(f32)
    geout[...] = h_geout[...].astype(f32)

    @pl.when(pl.program_id(0) == 0)
    def _():
        for s in range(3):
            gqkv[s] = h_gw2[:, s * HL : (s + 1) * HL]
        gao[...] = h_gw2[:, 3 * HL : 4 * HL].T
        gains = h_gw2[:, 4 * HL :].T
        gnf[...] = gains[0:1, :]
        gna[...] = gains[1:2, :]
        for s in range(2):
            gsi[s] = h_gw1[:, s * F : (s + 1) * F]
        gso[...] = h_gw1[:, 2 * F :].T


def fused(
    tokens, cont_lengths, routes, route_gates, w_qkv, w_attn_out, norm_attn, norm_ffn,
    shared_in, shared_out, expert_in, expert_out, cotangent,
):
    T, D = tokens.shape
    G = lax.axis_size("dp")
    HL, F, FX = w_qkv.shape[2], shared_in.shape[2], expert_in.shape[2]
    C = round_up(CAP, 16)
    S = G * C
    half, share, zs = D // 2, D // G, G // 4
    W1, W2 = 3 * F, 4 * HL + 128
    shape = jax.ShapeDtypeStruct
    dma = pltpu.SemaphoreType.DMA
    SM = pl.BlockSpec(memory_space=pltpu.SMEM)
    tile = 256
    kept = {
        "qkv": ((3, T, HL), bf16), "lse": ((T, 128), f32), "att": ((T, HL), bf16), "normed_a": ((T, D), bf16),
        "resid": ((T, D), f32), "plan": ((S, T), bf16), "gate": ((EXPERTS, T), f32), "cos": ((T, 128), f32),
        "sin": ((T, 128), f32), "part": ((S, D), bf16), "shp": ((T, D), bf16), "dres": ((T, D), f32),
        "gnf": ((8, D), f32),
    }

    def keep(*names):
        return [pltpu.VMEM(*kept[name]) for name in names]

    front = pl.pallas_call(
        functools.partial(front_kernel, G),
        out_shape=(
            *[shape(*k) for k in kept.values()],
            shape((D, W1), bf16), shape((2, D, FX), bf16), shape((FX, D), bf16),
        ),
        in_specs=[VM] * 2 + [SM] + [VM] * 2 + [ANY] * 8,
        out_specs=(ANY,) * (len(kept) + 3),
        scratch_shapes=[
            pltpu.VMEM((T, D), bf16),
            pltpu.VMEM((3, D, HL), bf16),
            pltpu.VMEM((HL, D), bf16),
            pltpu.VMEM((T, D), bf16),
            *keep("cos", "sin", "qkv", "lse", "att", "normed_a", "resid", "plan", "gate", "part", "shp", "dres", "gnf"),
            pltpu.VMEM((T, T), f32),
            pltpu.VMEM((T, HL), bf16),
            pltpu.VMEM((HL, D), bf16),
            pltpu.VMEM((EXPERTS, T), f32),
            pltpu.VMEM((S, D), bf16),
            pltpu.VMEM((T, D), bf16),
            pltpu.VMEM((S, D), bf16),
            pltpu.VMEM((2, D, F), bf16),
            pltpu.VMEM((F, D), bf16),
            pltpu.VMEM((2, D, FX), bf16),
            pltpu.VMEM((FX, D), bf16),
            pltpu.VMEM((T, F), bf16),
            pltpu.VMEM((2, T, F), bf16),
            pltpu.VMEM((S, FX), bf16),
            pltpu.VMEM((2, S, FX), bf16),
            pltpu.VMEM((T, D), bf16),
            pltpu.VMEM((T, half), bf16),
            pltpu.VMEM((S, D), bf16),
            pltpu.VMEM((S, half), bf16),
            pltpu.VMEM((S, half), bf16),
            pltpu.VMEM((S, half), bf16),
            pltpu.VMEM((T, D), bf16),
            pltpu.VMEM((D, S), bf16),
            pltpu.VMEM((2, D, tile), bf16),
            pltpu.VMEM((2, tile, D), bf16),
            pltpu.VMEM((2, D, tile), bf16),
            dma((7,)), dma((7,)), *[dma((G,))] * 8,
            dma((4,)), dma((4,)), dma((G,)), dma((G,)), dma((8,)), dma((4,)), dma((len(kept),)),
        ],
        compiler_params=pltpu.CompilerParams(
            collective_id=0, has_side_effects=True, vmem_limit_bytes=VMEM_BYTES
        ),
        name="front",
    )(
        norm_attn, norm_ffn, cont_lengths, routes.T, route_gates.T, tokens, w_qkv, w_attn_out, cotangent,
        shared_in, shared_out, expert_in, expert_out,
    )
    kept_out, (gsh, gein, geout) = front[: len(kept)], front[len(kept) :]
    fold = [(zs, 2, share), (zs, 2, share), (zs, share), (zs, share), (zs - 1, share)]
    raw = pl.pallas_call(
        functools.partial(back_kernel, G),
        out_shape=(
            shape((T, D), bf16), shape((T, D), bf16), shape((share, W1), f32), shape((share, W2), f32),
        ),
        in_specs=[VM, SM] + [ANY] * (4 + len(kept)),
        out_specs=(VM,) * 4,
        scratch_shapes=[
            pltpu.VMEM((T, D), bf16),
            pltpu.VMEM((3, D, HL), bf16),
            pltpu.VMEM((HL, D), bf16),
            *keep("qkv", "lse", "att", "normed_a"),
            pltpu.VMEM((T, half), f32),
            *keep("plan", "gate", "cos", "sin"),
            pltpu.VMEM((S, half), bf16),
            pltpu.VMEM((T, half), bf16),
            *keep("dres", "gnf"),
            pltpu.VMEM((T, T), f32),
            pltpu.VMEM((T, D), bf16),
            pltpu.VMEM((T, HL), bf16),
            pltpu.VMEM((3, T, HL), bf16),
            pltpu.VMEM((D, T), bf16),
            pltpu.VMEM((zs, 2, 2, share, W2), bf16),
            pltpu.VMEM((S, half), bf16),
            pltpu.VMEM((S, half), bf16),
            pltpu.VMEM((S, half), bf16),
            pltpu.VMEM((T, half), bf16),
            pltpu.VMEM((4 * C, T), bf16),
            pltpu.VMEM((T, D), bf16),
            pltpu.VMEM((T, D), bf16),
            pltpu.VMEM((8, D), f32),
            pltpu.VMEM((8, D), f32),
            pltpu.VMEM((T, D), bf16),
            *[pltpu.VMEM((*s, W1), bf16) for s in fold],
            *[pltpu.VMEM((*s, W2), bf16) for s in fold],
            dma((4,)), dma((4,)), dma((4,)), dma((4,)), dma((G,)), dma((G,)),
            dma((3, 1 + zs)), dma((3, 1 + zs)), dma((17,)),
        ],
        compiler_params=pltpu.CompilerParams(
            collective_id=1, has_side_effects=True, vmem_limit_bytes=VMEM_BYTES
        ),
        name="back",
    )(
        norm_attn, cont_lengths, tokens, w_qkv, w_attn_out, *kept_out, gsh.reshape(zs, 2, 2, share, W1),
    )
    steps = 4

    def rows_of(*dims):
        return pl.BlockSpec(dims, lambda i: (0,) * (len(dims) - 2) + (i, 0))

    def whole(*dims):
        return pl.BlockSpec(dims, lambda i: (0,) * len(dims))

    results = ((3, share, HL), (HL, share), (1, share), (1, share), (2, share, F), (F, share))
    out, gtok, gqkv, gao, gna, gnf, gsi, gso, gein, geout = pl.pallas_call(
        functools.partial(finish_kernel, HL, F),
        grid=(steps,),
        out_shape=(
            shape((T, D), bf16), shape((T, D), bf16), *[shape(r, f32) for r in results],
            shape((2, D, FX), f32), shape((FX, D), f32),
        ),
        in_specs=[
            rows_of(T // steps, D), rows_of(T // steps, D), whole(share, W1), whole(share, W2),
            rows_of(2, D // steps, FX), rows_of(FX // steps, D),
        ],
        out_specs=(
            rows_of(T // steps, D), rows_of(T // steps, D), *[whole(*r) for r in results],
            rows_of(2, D // steps, FX), rows_of(FX // steps, D),
        ),
        compiler_params=pltpu.CompilerParams(vmem_limit_bytes=VMEM_BYTES),
        name="finish",
    )(*raw, gein, geout)
    return (out, gtok, gqkv, gao, gna[0], gnf[0], gsi, gso, gein, geout)


def solution(mesh):
    placed = (
        P("dp", None),
        P("dp", None),
        P("dp", None),
        P("dp", None),
        P(None, None, "tensor"),
        P("tensor", None),
        P(),
        P(),
        P(None, None, "tensor"),
        P("tensor", None),
        P(None, None, ("dp", "tensor")),
        P(("dp", "tensor"), None),
        P("dp", None),
    )
    return jax.shard_map(
        fused if mesh.shape["dp"] == EXPERTS else local,
        mesh=mesh,
        in_specs=placed,
        out_specs=(
            P("dp", None),
            P("dp", None),
            P(None, "dp", "tensor"),
            P("tensor", "dp"),
            P("dp"),
            P("dp"),
            P(None, "dp", "tensor"),
            P("tensor", "dp"),
            P(None, None, ("dp", "tensor")),
            P(("dp", "tensor"), None),
        ),
        check_vma=False,
    )
```

```python
import functools
import math

import jax
import jax.numpy as jnp
from jax import lax
from jax.experimental import pallas as pl
from jax.experimental.pallas import tpu as pltpu
from jax.sharding import PartitionSpec as P

HD = 64
EXPERTS = 16
TOP = 2
PROMPT = 64
CAP = 92


epsilon = 1e-06


def rms_parts(values, gain):
    factor = lax.rsqrt(jnp.mean(values * values, axis=-1, keepdims=True) + epsilon)
    return (values * factor * gain, factor)


def rms_back(values, factor, gain, incoming):
    weighted = incoming * gain
    inner = jnp.mean(weighted * values, axis=-1, keepdims=True)
    return (
        factor * weighted - values * factor * factor * factor * inner,
        jnp.sum(incoming * values * factor, axis=0),
    )


def silu_act(values):
    return values * jax.nn.sigmoid(values)


def swiglu_back(gate_up, d_act):
    sigma = jax.nn.sigmoid(gate_up[0])
    d_gate = d_act * gate_up[1] * sigma * (1.0 + gate_up[0] * (1.0 - sigma))
    d_upper = d_act * gate_up[0] * sigma
    return jnp.stack([d_gate, d_upper]).astype(jnp.bfloat16)


def group_layout(lengths, rows_here):
    row_index = jnp.arange(rows_here, dtype=jnp.int32)
    cont_ends = PROMPT + jnp.cumsum(lengths, dtype=jnp.int32)
    begins = cont_ends - lengths
    later = jnp.sum(
        (row_index[:, None] >= cont_ends[None, :]).astype(jnp.int32), axis=1, dtype=jnp.int32
    )
    segment = jnp.where(row_index < PROMPT, 0, 1 + later)
    member = (
        segment[:, None] == jnp.arange(1, lengths.shape[0] + 1, dtype=jnp.int32)[None, :]
    ).astype(jnp.int32)
    offset = jnp.sum(member * begins[None, :], axis=1, dtype=jnp.int32)
    position = jnp.where(segment == 0, row_index, PROMPT + row_index - offset)
    allowed = (row_index[None, :] <= row_index[:, None]) & (
        (segment[None, :] == 0) | (segment[None, :] == segment[:, None])
    )
    return (position, allowed)


def rope_tables(position):
    half_size = HD // 2
    inv_freq = 10000.0 ** (-jnp.arange(half_size, dtype=jnp.float32) / half_size)
    angles = position.astype(jnp.float32)[:, None] * inv_freq[None, :]
    return (jnp.cos(angles)[:, None, :], jnp.sin(angles)[:, None, :])


def rotate_pairs(values, cosine, sine):
    half_size = values.shape[-1] // 2
    front_half = values[..., :half_size]
    back_half = values[..., half_size:]
    return jnp.concatenate(
        [front_half * cosine - back_half * sine, front_half * sine + back_half * cosine], axis=-1
    )


def dispatch_plan(routes):
    flat_routes = routes.reshape(-1)
    one_hot = (flat_routes[:, None] == jnp.arange(EXPERTS, dtype=jnp.int32)[None, :]).astype(
        jnp.int32
    )
    earlier = jnp.cumsum(one_hot, axis=0, dtype=jnp.int32) - one_hot
    place_in = jnp.sum(earlier * one_hot, axis=1, dtype=jnp.int32)
    target = flat_routes * CAP + place_in
    pair_count = flat_routes.shape[0]
    slot_table = (
        jnp.full((EXPERTS * CAP,), pair_count, jnp.int32)
        .at[target]
        .set(jnp.arange(pair_count, dtype=jnp.int32))
    )
    return (target, slot_table)


def spread_rows(padded, indices, copies):
    model_width = padded.shape[1]
    picked = jnp.take(padded, indices, axis=0).reshape(EXPERTS, 1, CAP, model_width)
    return jnp.broadcast_to(picked, (EXPERTS, copies, CAP, model_width)).reshape(
        EXPERTS * copies, CAP, model_width
    )


def collect_rows(returned, target, copies, rows_here):
    model_width = returned.shape[2]
    summed = jnp.sum(returned.reshape(EXPERTS, copies, CAP, model_width), axis=1, dtype=jnp.float32)
    summed = summed.reshape(EXPERTS * CAP, model_width)
    return jnp.take(summed, target, axis=0).reshape(rows_here, TOP, model_width)


def local(
    tokens,
    cont_lengths,
    routes,
    route_gates,
    w_qkv,
    w_attn_out,
    norm_attn,
    norm_ffn,
    shared_in,
    shared_out,
    expert_in,
    expert_out,
    cotangent,
):
    rows_here = tokens.shape[0]
    model_width = tokens.shape[1]
    groups = lax.axis_size("dp")
    copies = groups // EXPERTS
    head_count = w_qkv.shape[2] // HD
    score_scale = HD ** (-0.5)
    inputs = tokens.astype(jnp.float32)
    position, allowed = group_layout(cont_lengths[0], rows_here)
    cosine, sine = rope_tables(position)
    normed_a, factor_a = rms_parts(inputs, norm_attn)
    normed_attn = normed_a.astype(jnp.bfloat16)
    projected = jnp.einsum("td,sdf->stf", normed_attn, w_qkv, preferred_element_type=jnp.float32)
    query = rotate_pairs(projected[0].reshape(rows_here, head_count, HD), cosine, sine).astype(
        jnp.bfloat16
    )
    key_rows = rotate_pairs(projected[1].reshape(rows_here, head_count, HD), cosine, sine).astype(
        jnp.bfloat16
    )
    value_rows = projected[2].reshape(rows_here, head_count, HD).astype(jnp.bfloat16)
    score = (
        jnp.einsum("qhd,khd->hqk", query, key_rows, preferred_element_type=jnp.float32)
        * score_scale
    )
    score = jnp.where(allowed[None], score, -1000000000.0)
    row_max = jnp.max(score, axis=-1, keepdims=True)
    exponent = jnp.exp(score - row_max)
    row_total = jnp.sum(exponent, axis=-1, keepdims=True)
    log_total = row_max + jnp.log(row_total)
    weights_b = (exponent / row_total).astype(jnp.bfloat16)
    attended = jnp.einsum("hqk,khd->qhd", weights_b, value_rows, preferred_element_type=jnp.float32)
    attended = attended.reshape(rows_here, head_count * HD).astype(jnp.bfloat16)
    attn_part = jnp.dot(attended, w_attn_out, preferred_element_type=jnp.float32)
    resid = inputs + lax.psum(attn_part.astype(jnp.bfloat16), "tensor").astype(jnp.float32)
    normed_f, factor_f = rms_parts(resid, norm_ffn)
    normed_ffn = normed_f.astype(jnp.bfloat16)
    gate_up = jnp.einsum("td,sdf->stf", normed_ffn, shared_in, preferred_element_type=jnp.float32)
    shared_act = (silu_act(gate_up[0]) * gate_up[1]).astype(jnp.bfloat16)
    shared_part = jnp.dot(shared_act, shared_out, preferred_element_type=jnp.float32)
    target, slot_table = dispatch_plan(routes)
    padded_rows = jnp.concatenate([normed_ffn, jnp.zeros((1, model_width), jnp.bfloat16)], axis=0)
    send_rows = spread_rows(padded_rows, slot_table // TOP, copies)
    arrived = lax.all_to_all(send_rows, "dp", split_axis=0, concat_axis=0, tiled=True)
    expert_input = arrived.reshape(groups * CAP, model_width)
    expert_gu = jnp.einsum(
        "rd,sdf->srf", expert_input, expert_in, preferred_element_type=jnp.float32
    )
    expert_act = (silu_act(expert_gu[0]) * expert_gu[1]).astype(jnp.bfloat16)
    expert_part = jnp.dot(expert_act, expert_out, preferred_element_type=jnp.float32).astype(
        jnp.bfloat16
    )
    returned = lax.all_to_all(
        expert_part.reshape(groups, CAP, model_width), "dp", split_axis=0, concat_axis=0, tiled=True
    )
    picked = collect_rows(returned, target, copies, rows_here)
    mixed = jnp.sum(route_gates[:, :, None] * picked, axis=1)
    ffn_total = lax.psum((shared_part + mixed).astype(jnp.bfloat16), "tensor").astype(jnp.float32)
    output = (resid + ffn_total).astype(jnp.bfloat16)
    upstream = cotangent.astype(jnp.float32)
    d_shared_act = jnp.einsum(
        "td,fd->tf", cotangent, shared_out, preferred_element_type=jnp.float32
    )
    d_shared_gu = swiglu_back(gate_up, d_shared_act)
    d_normed = jnp.einsum("stf,sdf->td", d_shared_gu, shared_in, preferred_element_type=jnp.float32)
    g_shared_in = jnp.einsum(
        "td,stf->sdf", normed_ffn, d_shared_gu, preferred_element_type=jnp.float32
    )
    g_shared_out = jnp.einsum(
        "tf,td->fd", shared_act, cotangent, preferred_element_type=jnp.float32
    )
    pair_grad = (
        (route_gates[:, :, None] * upstream[:, None, :])
        .reshape(rows_here * TOP, model_width)
        .astype(jnp.bfloat16)
    )
    padded_grad = jnp.concatenate([pair_grad, jnp.zeros((1, model_width), jnp.bfloat16)], axis=0)
    send_grad = spread_rows(padded_grad, slot_table, copies)
    again_rows = spread_rows(padded_rows, slot_table // TOP, copies)
    grad_arrived, rows_arrived = (
        lax.all_to_all(send_grad, "dp", split_axis=0, concat_axis=0, tiled=True),
        lax.all_to_all(again_rows, "dp", split_axis=0, concat_axis=0, tiled=True),
    )
    rows_back = rows_arrived.reshape(groups * CAP, model_width)
    d_expert_rows = grad_arrived.reshape(groups * CAP, model_width)
    back_gu = jnp.einsum("rd,sdf->srf", rows_back, expert_in, preferred_element_type=jnp.float32)
    back_act = (silu_act(back_gu[0]) * back_gu[1]).astype(jnp.bfloat16)
    d_expert_act = jnp.einsum(
        "rd,fd->rf", d_expert_rows, expert_out, preferred_element_type=jnp.float32
    )
    d_expert_gu = swiglu_back(back_gu, d_expert_act)
    d_expert_in = jnp.einsum(
        "srf,sdf->rd", d_expert_gu, expert_in, preferred_element_type=jnp.float32
    ).astype(jnp.bfloat16)
    g_expert_in = jnp.einsum(
        "rd,srf->sdf", rows_back, d_expert_gu, preferred_element_type=jnp.float32
    )
    g_expert_out = jnp.einsum(
        "rf,rd->fd", back_act, d_expert_rows, preferred_element_type=jnp.float32
    )
    d_returned = lax.all_to_all(
        d_expert_in.reshape(groups, CAP, model_width), "dp", split_axis=0, concat_axis=0, tiled=True
    )
    d_normed = d_normed + jnp.sum(collect_rows(d_returned, target, copies, rows_here), axis=1)
    d_normed = lax.psum(d_normed.astype(jnp.bfloat16), "tensor").astype(jnp.float32)
    d_resid_norm, g_norm_ffn = rms_back(resid, factor_f, norm_ffn, d_normed)
    d_resid = upstream + d_resid_norm
    d_resid_b = d_resid.astype(jnp.bfloat16)
    g_attn_out = jnp.einsum("tf,td->fd", attended, d_resid_b, preferred_element_type=jnp.float32)
    d_attended = jnp.einsum("td,fd->tf", d_resid_b, w_attn_out, preferred_element_type=jnp.float32)
    d_attended = d_attended.astype(jnp.bfloat16).reshape(rows_here, head_count, HD)
    recomputed = (
        jnp.einsum("qhd,khd->hqk", query, key_rows, preferred_element_type=jnp.float32)
        * score_scale
    )
    recomputed = jnp.where(allowed[None], recomputed, -1000000000.0)
    probs = jnp.exp(recomputed - log_total)
    probs_b = probs.astype(jnp.bfloat16)
    d_probs = jnp.einsum("qhd,khd->hqk", d_attended, value_rows, preferred_element_type=jnp.float32)
    d_value = jnp.einsum("hqk,qhd->khd", probs_b, d_attended, preferred_element_type=jnp.float32)
    inner = jnp.sum(d_probs * probs, axis=-1, keepdims=True)
    d_score = (probs * (d_probs - inner)).astype(jnp.bfloat16)
    d_query = (
        jnp.einsum("hqk,khd->qhd", d_score, key_rows, preferred_element_type=jnp.float32)
        * score_scale
    )
    d_key = (
        jnp.einsum("hqk,qhd->khd", d_score, query, preferred_element_type=jnp.float32) * score_scale
    )
    d_query = rotate_pairs(d_query, cosine, -sine).reshape(rows_here, head_count * HD)
    d_key = rotate_pairs(d_key, cosine, -sine).reshape(rows_here, head_count * HD)
    d_qkv = jnp.stack([d_query, d_key, d_value.reshape(rows_here, head_count * HD)]).astype(
        jnp.bfloat16
    )
    g_qkv = jnp.einsum("td,stf->sdf", normed_attn, d_qkv, preferred_element_type=jnp.float32)
    d_normed_attn = jnp.einsum("stf,sdf->td", d_qkv, w_qkv, preferred_element_type=jnp.float32)
    d_normed_attn = lax.psum(d_normed_attn.astype(jnp.bfloat16), "tensor").astype(jnp.float32)
    d_input_norm, g_norm_attn = rms_back(inputs, factor_a, norm_attn, d_normed_attn)
    grad_tokens = (d_resid + d_input_norm).astype(jnp.bfloat16)
    summed_all = (
        lax.psum_scatter(g_qkv, "dp", scatter_dimension=1, tiled=True),
        lax.psum_scatter(g_attn_out, "dp", scatter_dimension=1, tiled=True),
        lax.psum_scatter(g_norm_attn, "dp", scatter_dimension=0, tiled=True),
        lax.psum_scatter(g_shared_in, "dp", scatter_dimension=1, tiled=True),
        lax.psum_scatter(g_shared_out, "dp", scatter_dimension=1, tiled=True),
        lax.psum_scatter(g_norm_ffn, "dp", scatter_dimension=0, tiled=True),
    )
    return (
        output,
        grad_tokens,
        summed_all[0],
        summed_all[1],
        summed_all[2],
        summed_all[5],
        summed_all[3],
        summed_all[4],
        g_expert_in,
        g_expert_out,
    )


VMEM_BYTES = 64000 * 1024
FOLD = 96
SPLIT = 7
EARLY = 2
MESH = pl.DeviceIdType.MESH
VM = pl.BlockSpec(memory_space=pltpu.VMEM)
ANY = pl.BlockSpec(memory_space=pl.ANY)
f32 = jnp.float32
bf16 = jnp.bfloat16


def round_up(value, unit):
    return (value + unit - 1) // unit * unit


def dot(a, b):
    return jnp.dot(a, b, preferred_element_type=f32)


def dot_nt(a, b):
    return lax.dot_general(a, b, (((1,), (1,)), ((), ())), preferred_element_type=f32)


def dot_tn(a, b):
    return lax.dot_general(a, b, (((0,), (0,)), ((), ())), preferred_element_type=f32)


def sigmoid(values):
    return 0.5 * jnp.tanh(0.5 * values) + 0.5


def swap_halves(values):
    lane = lax.broadcasted_iota(jnp.int32, values.shape, 1)
    ahead = pltpu.roll(values, values.shape[1] - HD // 2, 1)
    behind = pltpu.roll(values, HD // 2, 1)
    return jnp.where(lax.rem(lane, HD) < HD // 2, ahead, behind)


def hello(groups):
    me, t = lax.axis_index("dp"), lax.axis_index("tensor")
    barrier = pltpu.get_barrier_semaphore()

    def greet(k, carry):
        pl.semaphore_signal(
            barrier, inc=1, device_id=(lax.rem(me + k, groups), t), device_id_type=MESH
        )
        return carry

    lax.fori_loop(1, groups, greet, 0)
    pl.semaphore_signal(barrier, inc=1, device_id=(me, 1 - t), device_id_type=MESH)
    pl.semaphore_wait(barrier, groups)


def segment_of(index, lens):
    segment = jnp.where(index < PROMPT, 0, 1)
    end = PROMPT
    for c in range(lens.shape[1]):
        end = end + lens[0, c]
        segment = segment + jnp.where(index >= end, 1, 0)
    return segment


def position_of(index, lens):
    segment = segment_of(index, lens)
    position, end = index, PROMPT
    for c in range(lens.shape[1]):
        position = jnp.where(segment == c + 1, PROMPT + index - end, position)
        end = end + lens[0, c]
    return position


def fill_bias(bias, lens, rows):
    step = FOLD

    def body(i, carry):
        at = pl.ds(pl.multiple_of(i * step, step), step)
        row = lax.broadcasted_iota(jnp.int32, (step, rows), 0) + i * step
        col = lax.broadcasted_iota(jnp.int32, (step, rows), 1)
        own = segment_of(lax.broadcasted_iota(jnp.int32, (step, 1), 0) + i * step, lens)
        other = segment_of(lax.broadcasted_iota(jnp.int32, (1, rows), 1), lens)
        ok = (col <= row) & ((other == 0) | (other == own))
        bias[at, :] = jnp.where(ok, 0.0, -1000000000.0)
        return carry

    lax.fori_loop(0, rows // step, body, 0)


def fill_angles(cos, sin, lens, rows):
    step = FOLD

    def body(i, carry):
        at = pl.ds(pl.multiple_of(i * step, step), step)
        lane = lax.broadcasted_iota(jnp.int32, (step, 128), 1)
        row = lax.broadcasted_iota(jnp.int32, (step, 128), 0) + i * step
        power = lax.rem(lane, HD // 2).astype(f32) * (-math.log(10000.0) / (HD // 2))
        angle = position_of(row, lens).astype(f32) * jnp.exp(power)
        cos[at, :] = jnp.cos(angle)
        sine = jnp.sin(angle)
        sin[at, :] = jnp.where(lax.rem(lane, HD) < HD // 2, -sine, sine)
        return carry

    lax.fori_loop(0, rows // step, body, 0)


def send(src, dst, ssem, rsem, to):
    return pltpu.make_async_remote_copy(
        src_ref=src, dst_ref=dst, send_sem=ssem, recv_sem=rsem, device_id=to, device_id_type=MESH
    )


def layer_kernel(
    G, na, nf, lens, rT, gT, h_tok, h_wqkv, h_wo, h_cot, si, so, ei, eo,
    h_out, h_gtok, h_gw1, h_gw2, gein, geout,
    tok, wqkv, wo, cot, cos, sin, qkv, lse, att_own, normed_a, resid, plan, gate, slot, bias, att, wo2,
    csend, drows, rows, rets, ret, dxr, dnsh, dnsh_r, dnb, shp, partr, ro, shpr, gna, gnar,
    a1, b1, d1, a2, b2, d2,
    s_x, r_x, s_c, r_c, s_cf, r_cf, s_r, r_r, s_f, r_f, s_dx, r_dx, s_ret, r_ret, s_p, r_p, s_po, r_po,
    s_k, r_k, s_y, r_y, s_z, r_z, lsem, osem,
):
    T, D = tok.shape
    HL = wqkv.shape[2]
    F = si.shape[2]
    S = plan.shape[0]
    C = S // G
    half, share, zs = D // 2, D // G, G // 4
    W2 = a2.shape[3]
    scale = HD ** (-0.5)
    me, t = lax.axis_index("dp"), lax.axis_index("tensor")
    core, y, z = lax.rem(me, 2), lax.rem(me // 2, 2), me // 4
    mine = pl.ds(pl.multiple_of(t * half, 128), half)
    theirs = pl.ds(pl.multiple_of((1 - t) * half, 128), half)
    partner = (me, 1 - t)
    sibling = (me + 1 - 2 * core, t)
    neighbour = (me + 2 - 4 * y, t)
    per, tile = 4, 256
    M, chunks, tiles = per * C, G // per, F // tile

    loads = [
        pltpu.make_async_copy(a, b, lsem.at[i])
        for i, (a, b) in enumerate(((h_cot, cot), (h_tok, tok), (h_wqkv, wqkv), (h_wo, wo)))
    ]
    for c in loads:
        c.start()
    hello(G)
    part_wo = pl.ds(pl.multiple_of(core * (HL // 2), 16), HL // 2)
    wo_copy = send(h_wo.at[part_wo], wo2.at[part_wo], s_x.at[0], r_x.at[0], partner)
    wo_copy.start()
    wo_pass = send(wo2.at[part_wo], wo2.at[part_wo], s_x.at[6], r_x.at[6], sibling)

    def row_at(k):
        return pl.ds(pl.multiple_of(k * C, C), C)

    def chunk_at(c):
        return pl.ds(c * M, M)

    names = lax.broadcasted_iota(jnp.int32, (EXPERTS, T), 0)
    picks0, picks1 = rT[0:1, :] == names, rT[1:2, :] == names
    member = jnp.where(picks0 | picks1, 1.0, 0.0)
    upper = jnp.where(
        lax.broadcasted_iota(jnp.int32, (T, T), 0) < lax.broadcasted_iota(jnp.int32, (T, T), 1),
        1.0,
        0.0,
    ).astype(bf16)
    slot[...] = jnp.where(member > 0.0, dot(member.astype(bf16), upper), -1.0)
    gate[...] = jnp.where(picks0, gT[0:1, :], 0.0) + jnp.where(picks1, gT[1:2, :], 0.0)

    def cot_copy(k):
        return send(
            csend.at[row_at(k)], drows.at[row_at(k)], s_c.at[k], r_c.at[k], (lax.rem(me + k, G), t)
        )

    def cot_half(k):
        return send(
            csend.at[row_at(k), mine], drows.at[row_at(k), mine], s_c.at[k], r_c.at[k],
            (lax.rem(me + k, G), t),
        )

    def cot_pass(k):
        return send(
            drows.at[row_at(k), mine], drows.at[row_at(k), mine], s_cf.at[k], r_cf.at[k], partner
        )

    def cot_step(k, carry):
        e = lax.rem(me + k, G)
        at = row_at(k)
        place = lax.broadcasted_iota(jnp.int32, (C, T), 0).astype(f32)
        hit = slot[pl.ds(e, 1), :] == place
        picked = jnp.where(hit, 1.0, 0.0).astype(bf16)
        plan[at, :] = picked
        weight = jnp.sum(jnp.where(hit, gate[pl.ds(e, 1), :], 0.0), axis=1, keepdims=True)
        grad = (dot(picked, cot[...]) * weight).astype(bf16)
        csend[at, :] = grad

        @pl.when(k > SPLIT)
        def _():
            cot_copy(k).start()

        @pl.when((k > 0) & (k <= SPLIT))
        def _():
            cot_half(k).start()

        @pl.when(k == 0)
        def _():
            drows[at, :] = grad

        return carry

    loads[0].wait()
    lax.fori_loop(0, G, cot_step, 0)

    fill_angles(cos, sin, lens, T)
    fill_bias(bias, lens, T)
    loads[1].wait()

    def norm_step(i, carry):
        at = pl.ds(pl.multiple_of(i * FOLD, FOLD), FOLD)
        x = tok[at, :].astype(f32)
        r = lax.rsqrt(jnp.mean(x * x, axis=1, keepdims=True) + epsilon)
        normed_a[at, :] = (x * r * na[...].reshape(1, D)).astype(bf16)
        return carry

    lax.fori_loop(0, T // FOLD, norm_step, 0)
    loads[2].wait()
    loads[3].wait()

    def project(s, turned):
        full = dot(normed_a[...], wqkv[s])
        for j in range(HL // 128):
            x = full[:, j * 128 : (j + 1) * 128]
            if turned:
                x = x * cos[...] + swap_halves(x) * sin[...]
            qkv[s, :, j * 128 : (j + 1) * 128] = x.astype(bf16)

    project(0, True)
    project(1, True)
    project(2, False)
    lane = lax.broadcasted_iota(jnp.int32, (T, 128), 1)

    def att_copy(j):
        at = pl.ds(pl.multiple_of(j * 128, 128), 128)
        return send(att_own.at[:, at], att.at[:, at], s_x.at[1 + j], r_x.at[1 + j], partner)

    lse[...] = jnp.zeros_like(lse)

    def attend(j, carry):
        at = pl.ds(pl.multiple_of(j * 128, 128), 128)
        q, k, v = qkv[0, :, at], qkv[1, :, at], qkv[2, :, at]
        outs = []
        for i in range(2):
            inside = (lane < HD) if i == 0 else (lane >= HD)
            s = dot_nt(jnp.where(inside, q, jnp.zeros_like(q)), k) * scale + bias[...]
            top = jnp.max(s, axis=1, keepdims=True)
            e = jnp.exp(s - top)
            total = jnp.sum(e, axis=1, keepdims=True)
            p = (e * (1.0 / total)).astype(bf16)
            lse[...] = jnp.where(lane == 2 * j + i, top + jnp.log(total), lse[...])
            outs.append(dot(p, v))
        att_own[:, at] = jnp.where(lane < HD, outs[0], outs[1]).astype(bf16)
        att_copy(j).start()
        return carry

    wo_copy.wait()
    wo_pass.start()
    lax.fori_loop(0, HL // 128, attend, 0)
    own_out = dot(att_own[...], wo[...])
    wo_pass.wait()
    for j in range(HL // 128):
        att_copy(j).wait()
    for k in range(1, SPLIT + 1):
        cot_half(k).wait_recv()
        cot_pass(k).start()
    resid[...] = tok[...].astype(f32) + own_out + dot(att[...], wo2[...])

    def row_copy(k):
        return send(
            rets.at[row_at(k)], rows.at[row_at(k), mine], s_r.at[k], r_r.at[k], (lax.rem(me + k, G), t)
        )

    def row_pass(k):
        return send(
            rows.at[row_at(k), mine], rows.at[row_at(k), mine], s_f.at[k], r_f.at[k], partner
        )

    def hand_on(k):
        row_copy(k).wait_recv()
        row_pass(k).start()

    def dx_copy(c):
        return send(csend.at[chunk_at(c), theirs], dxr.at[chunk_at(c)], s_dx.at[c], r_dx.at[c], partner)

    def ret_copy(k):
        return send(
            rets.at[row_at(k)], ret.at[row_at(k)], s_ret.at[k], r_ret.at[k], (lax.rem(me - k + G, G), t)
        )

    def return_chunk(c):
        dx_copy(c).wait_recv()
        total = (csend[chunk_at(c), mine].astype(f32) + dxr[chunk_at(c), :].astype(f32)).astype(bf16)
        for k in range(c * per, (c + 1) * per):
            if k > 0:
                row_copy(k).wait_send()
        rets[chunk_at(c), :] = total
        for k in range(c * per, (c + 1) * per):
            if k > 0:
                ret_copy(k).start()
        if c == 0:
            ret[0:C, :] = total[0:C, :]

    def part_copy(c):
        return send(csend.at[chunk_at(c), theirs], partr.at[chunk_at(c)], s_p.at[c], r_p.at[c], partner)

    def po_copy(k):
        return send(
            rets.at[row_at(k)], ro.at[row_at(k)], s_po.at[k], r_po.at[k], (lax.rem(me - k + G, G), t)
        )

    def return_part(c):
        part_copy(c).wait_recv()
        total = (csend[chunk_at(c), mine].astype(f32) + partr[chunk_at(c), :].astype(f32)).astype(bf16)
        for k in range(c * per, (c + 1) * per):
            if k > 0:
                ret_copy(k).wait_send()
        rets[chunk_at(c), :] = total
        for k in range(c * per, (c + 1) * per):
            if k > 0:
                po_copy(k).start()
        if c == 0:
            ro[0:C, :] = total[0:C, :]

    dnsh_copy = send(dnsh.at[:, theirs], dnsh_r, s_x.at[4], r_x.at[4], partner)
    shp_copy = send(shp.at[:, theirs], shpr, s_x.at[7], r_x.at[7], partner)

    def columns(p):
        return slice(p * F, (p + 1) * F) if p < 3 else slice(0, W2)

    def fold_bufs(p):
        return (a1, b1, d1) if p < 3 else (a2, b2, d2)

    def fold_y(p):
        a, b, d = fold_bufs(p)
        return send(
            a.at[:, 1 - y, :, columns(p)], b.at[:, :, columns(p)], s_y.at[p], r_y.at[p], neighbour
        )

    def fold_z(p, k):
        a, b, d = fold_bufs(p)
        to = lax.rem(z + k, zs)
        return send(
            b.at[to, :, columns(p)], d.at[k - 1, :, columns(p)], s_z.at[p, k - 1], r_z.at[p, k - 1],
            (to * 4 + lax.rem(me, 4), t),
        )

    def fold_on(p):
        a, b, d = fold_bufs(p)
        fold_y(p).wait()

        def body(i, carry):
            b[i, :, columns(p)] = (
                b[i, :, columns(p)].astype(f32) + a[i, y, :, columns(p)].astype(f32)
            ).astype(bf16)
            return carry

        lax.fori_loop(0, zs, body, 0)
        for k in range(1, zs):
            fold_z(p, k).start()

    def fold_end(p, w):
        a, b, d = fold_bufs(p)
        total = b[z, :, columns(p)].astype(f32)
        for k in range(1, zs):
            fold_z(p, k).wait()
            total = total + d[k - 1, :, columns(p)].astype(f32)
        w[:, columns(p)] = total

    def experts(vsi, vso, vei, veo, act, dgu, normed, tall, wide):
        weights = [
            pltpu.make_async_copy(a, b, lsem.at[4 + i])
            for i, (a, b) in enumerate(((si, vsi), (so, vso), (ei, vei), (eo, veo)))
        ]
        for c in weights:
            c.start()

        def norm2_step(i, carry):
            at = pl.ds(pl.multiple_of(i * FOLD, FOLD), FOLD)
            x = resid[at, :]
            r = lax.rsqrt(jnp.mean(x * x, axis=1, keepdims=True) + epsilon)
            normed[at, :] = (x * r * nf[...].reshape(1, D)).astype(bf16)
            return carry

        lax.fori_loop(0, T // FOLD, norm2_step, 0)

        def row_step(k, carry):
            values = dot(plan[row_at(k), :], normed[:, mine]).astype(bf16)
            rets[row_at(k), :] = values

            @pl.when(k > 0)
            def _():
                row_copy(k).start()

            @pl.when(k == 0)
            def _():
                rows[row_at(k), mine] = values
                row_pass(k).start()

            return carry

        lax.fori_loop(0, G, row_step, 0)

        mid = slice(S - T, S)

        def shared_step(u, carry):
            at = pl.ds(pl.multiple_of(u * tile, tile), tile)
            pre = dot(normed[...], vsi[0, :, at])
            up = dot(normed[...], vsi[1, :, at])
            d_act = dot_nt(cot[...], vso[at, :])
            s = sigmoid(pre)
            gs = pre * s
            act[mid, at] = (gs * up).astype(bf16)
            dgu[0, mid, at] = (d_act * up * (s + gs * (1.0 - s))).astype(bf16)
            dgu[1, mid, at] = (d_act * gs).astype(bf16)
            return carry

        def tile_at(i):
            return pl.ds(pl.multiple_of(i * tile, tile), tile)

        def fold_core(i):
            return send(
                tall.at[lax.rem(i, 2), :, :, 1 - core], a1.at[:, :, :, tile_at(i)], s_k.at[i], r_k.at[i],
                sibling,
            )

        def core_end(i):
            fold_core(i).wait()

            def body(n, carry):
                u, v = n // 2, lax.rem(n, 2)
                a1[u, v, :, tile_at(i)] = (
                    a1[u, v, :, tile_at(i)].astype(f32) + tall[lax.rem(i, 2), u, v, core].astype(f32)
                ).astype(bf16)
                return carry

            lax.fori_loop(0, 2 * zs, body, 0)

        def shared_grads(p):
            def body(i, carry):
                at = tile_at(i - p * tiles)
                if p < 2:
                    grad = dot(vsi[0, :, 0:T], dgu[p, mid, at])
                else:
                    grad = dot(vsi[1, :, 0:T], act[mid, at])
                tall[lax.rem(i, 2)] = grad.astype(bf16).reshape(tall.shape[1:])
                fold_core(i).start()

                @pl.when(i > p * tiles)
                def _():
                    core_end(i - 1)

                return carry

            lax.fori_loop(p * tiles, (p + 1) * tiles, body, 0)
            core_end((p + 1) * tiles - 1)
            fold_y(p).start()

        def expert_chunk(c):
            for k in range(c * per, (c + 1) * per):
                row_pass(k).wait_recv()
                if k > SPLIT:
                    cot_copy(k).wait_recv()
                elif k > 0:
                    cot_pass(k).wait_recv()
            block = chunk_at(c)

            def unit_step(u, carry):
                at = pl.ds(pl.multiple_of(u * tile, tile), tile)
                pre = dot(rows[block, :], vei[0, :, at])
                up = dot(rows[block, :], vei[1, :, at])
                d_act = dot_nt(drows[block, :], veo[at, :])
                s = sigmoid(pre)
                gs = pre * s
                act[block, at] = (gs * up).astype(bf16)
                dgu[0, block, at] = (d_act * up * (s + gs * (1.0 - s))).astype(bf16)
                dgu[1, block, at] = (d_act * gs).astype(bf16)
                return carry

            lax.fori_loop(0, tiles, unit_step, 0)
            dx = dot_nt(dgu[0, block, :], vei[0]) + dot_nt(dgu[1, block, :], vei[1])
            for k in range(c * per, (c + 1) * per):
                if k > SPLIT:
                    cot_copy(k).wait_send()
                elif k > 0:
                    cot_half(k).wait_send()
            csend[block, :] = dx.astype(bf16)
            dx_copy(c).start()

        weights[0].wait()
        weights[1].wait()
        lax.fori_loop(0, tiles, shared_step, 0)
        for k in range(1, 4):
            hand_on(k)
        dnsh[...] = (dot_nt(dgu[0, mid, :], vsi[0]) + dot_nt(dgu[1, mid, :], vsi[1])).astype(bf16)
        dnsh_copy.start()
        weights[2].wait()
        weights[3].wait()
        for k in range(4, 6):
            hand_on(k)
        vsi[0, :, 0:T] = normed[...].T
        vsi[1, :, 0:T] = cot[...].T
        expert_chunk(0)
        for k in range(6, 8):
            hand_on(k)
        shp[...] = dot(act[mid, :], vso[...]).astype(bf16)
        shared_grads(0)
        return_chunk(0)
        expert_chunk(1)
        for k in range(8, 12):
            hand_on(k)
        shared_grads(1)
        shared_grads(2)
        return_chunk(1)
        expert_chunk(2)
        for k in range(12, G):
            hand_on(k)
        return_chunk(2)
        expert_chunk(3)

        def part_chunk(c):
            dx_copy(c).wait_send()
            csend[chunk_at(c), :] = dot(act[chunk_at(c), :], veo[...]).astype(bf16)

        for c in range(chunks - 1):
            part_chunk(c)
        return_chunk(3)
        for c in range(EARLY):
            part_copy(c).start()
        part_chunk(3)
        sides = [slice(0, S // 2), slice(S // 2, S)]
        for n in range(2):
            vsi[n, :, 0 : S // 2] = rows[sides[n], :].T

        def gein_copy(i):
            return pltpu.make_async_copy(
                tall.at[lax.rem(i, 2)], gein.at[i // tiles, :, :, :, :, tile_at(lax.rem(i, tiles))],
                osem.at[lax.rem(i, 2)],
            )

        def gein_step(i, carry):
            @pl.when(i > 1)
            def _():
                gein_copy(i - 2).wait()

            at = tile_at(lax.rem(i, tiles))
            grad = dot(vsi[0, :, 0 : S // 2], dgu[i // tiles, sides[0], at])
            grad = grad + dot(vsi[1, :, 0 : S // 2], dgu[i // tiles, sides[1], at])
            tall[lax.rem(i, 2)] = grad.astype(bf16).reshape(tall.shape[1:])
            gein_copy(i).start()
            return carry

        lax.fori_loop(0, 2 * tiles, gein_step, 0)
        for p in range(3):
            fold_on(p)

        def geout_copy(i):
            return pltpu.make_async_copy(
                wide.at[lax.rem(i, 2)], geout.at[tile_at(i), :], osem.at[2 + lax.rem(i, 2)]
            )

        def geout_step(i, carry):
            @pl.when(i > 1)
            def _():
                geout_copy(i - 2).wait()

            wide[lax.rem(i, 2)] = dot_tn(act[:, tile_at(i)], drows[...]).astype(bf16)
            geout_copy(i).start()
            return carry

        lax.fori_loop(0, tiles, geout_step, 0)
        for k in range(G):
            row_pass(k).wait_send()
        for k in range(1, SPLIT + 1):
            cot_pass(k).wait_send()
        gein_copy(2 * tiles - 2).wait()
        gein_copy(2 * tiles - 1).wait()
        geout_copy(tiles - 2).wait()
        geout_copy(tiles - 1).wait()

    pl.run_scoped(
        experts,
        pltpu.VMEM((2, D, F), bf16),
        pltpu.VMEM((F, D), bf16),
        pltpu.VMEM((2, D, F), bf16),
        pltpu.VMEM((F, D), bf16),
        pltpu.VMEM((S, F), bf16),
        pltpu.VMEM((2, S, F), bf16),
        pltpu.VMEM((T, D), bf16),
        pltpu.VMEM((2, zs, 2, 2, share, tile), bf16),
        pltpu.VMEM((2, tile, D), bf16),
    )

    dnsh_copy.wait()
    total = dnsh[:, mine].astype(f32) + dnsh_r[...].astype(f32)
    for c in range(chunks):
        for k in range(c * per, (c + 1) * per):
            if k > 0:
                ret_copy(k).wait_recv()
        total = total + dot_tn(plan[chunk_at(c), :], ret[chunk_at(c), :])
    dnb[:, mine] = total.astype(bf16)
    dnb_copy = send(dnb.at[:, mine], dnb.at[:, mine], s_x.at[5], r_x.at[5], partner)
    dnb_copy.start()

    dnar, ob = drows.at[0:T], rows.at[0:T]
    out_copy = send(ob.at[:, mine], ob.at[:, mine], s_x.at[8], r_x.at[8], partner)
    gna_copy = send(gna, gnar, s_x.at[9], r_x.at[9], partner)

    def attention_back(dres, dresb, da, dqkv, turned, pay, gated, dna, gtok, w1, w2):
        dna_copy = send(dna, dnar, s_x.at[10], r_x.at[10], partner)
        for c in range(min(2, EARLY)):
            return_part(c)
        dnb_copy.wait()
        for c in range(EARLY, chunks):
            part_copy(c).start()

        def dres_step(i, carry):
            at = pl.ds(pl.multiple_of(i * FOLD, FOLD), FOLD)
            y_ = dnb[at, :].astype(f32)
            x = resid[at, :]
            r = lax.rsqrt(jnp.mean(x * x, axis=1, keepdims=True) + epsilon)
            a = y_ * nf[...].reshape(1, D)
            inner = jnp.mean(a * x, axis=1, keepdims=True)
            xr = x * r
            value = cot[at, :].astype(f32) + r * a - xr * (r * r * inner)
            dres[at, :] = value
            dresb[at, :] = value.astype(bf16)
            return carry + jnp.sum(y_ * xr, axis=0, keepdims=True)

        gnf = lax.fori_loop(0, T // FOLD, dres_step, jnp.zeros((1, D), f32))
        da[...] = dot_nt(dresb[...], wo[...]).astype(bf16)

        def attend_back(j, carry):
            at = pl.ds(pl.multiple_of(j * 128, 128), 128)
            q, k, v, g = qkv[0, :, at], qkv[1, :, at], qkv[2, :, at], da[:, at]
            none = jnp.zeros_like(q)
            dq = dk = dv = jnp.zeros((T, 128), f32)
            for i in range(2):
                inside = (lane < HD) if i == 0 else (lane >= HD)
                qi, ki, gi = (jnp.where(inside, x, none) for x in (q, k, g))
                total = jnp.sum(jnp.where(lane == 2 * j + i, lse[...], 0.0), axis=1, keepdims=True)
                p = jnp.exp(dot_nt(qi, k) * scale + bias[...] - total)
                dp = dot_nt(gi, v)
                inner = jnp.sum(dp * p, axis=1, keepdims=True)
                ds = (p * (dp - inner)).astype(bf16)
                dv = dv + dot_tn(p.astype(bf16), gi)
                dq = dq + dot(ds, ki)
                dk = dk + dot_tn(ds, qi)
            dq, dk = dq * scale, dk * scale
            dqkv[0, :, at] = (dq * cos[...] - swap_halves(dq) * sin[...]).astype(bf16)
            dqkv[1, :, at] = (dk * cos[...] - swap_halves(dk) * sin[...]).astype(bf16)
            dqkv[2, :, at] = dv.astype(bf16)
            return carry

        lax.fori_loop(0, HL // 128, attend_back, 0)

        dna[...] = (
            dot_nt(dqkv[0], wqkv[0]) + dot_nt(dqkv[1], wqkv[1]) + dot_nt(dqkv[2], wqkv[2])
        ).astype(bf16)
        dna_copy.start()
        shp_copy.start()

        def gain_step(i, carry):
            at = pl.ds(pl.multiple_of(i * FOLD, FOLD), FOLD)
            x = tok[at, :].astype(f32)
            r = lax.rsqrt(jnp.mean(x * x, axis=1, keepdims=True) + epsilon)
            return carry + jnp.sum(dna[at, :].astype(f32) * x * r, axis=0, keepdims=True)

        gna[...] = jnp.broadcast_to(
            lax.fori_loop(0, T // FOLD, gain_step, jnp.zeros((1, D), f32)), gna.shape
        )
        gna_copy.start()
        for c in range(min(2, EARLY), chunks):
            return_part(c)

        turned[...] = normed_a[...].T
        for s in range(3):
            pay[:, :, :, :, s * HL : (s + 1) * HL] = (
                dot(turned[...], dqkv[s]).astype(bf16).reshape(zs, 2, 2, share, HL)
            )
        turned[...] = dresb[...].T
        pay[:, :, :, :, 3 * HL : 4 * HL] = (
            dot(turned[...], att_own[...]).astype(bf16).reshape(zs, 2, 2, share, HL)
        )
        gna_copy.wait()
        row = lax.broadcasted_iota(jnp.int32, (128, D), 0)
        gains = jnp.where(row == 0, gnf, jnp.where(row == 1, gna[0:1, :] + gnar[0:1, :], 0.0))
        pay[:, :, :, :, 4 * HL :] = gains.T.astype(bf16).reshape(zs, 2, 2, share, 128)
        core_copy = send(pay.at[:, :, 1 - core], a2, s_x.at[11], r_x.at[11], sibling)
        core_copy.start()
        core_copy.wait()

        def body(n, carry):
            u, v = n // 2, lax.rem(n, 2)
            a2[u, v] = (a2[u, v].astype(f32) + pay[u, v, core].astype(f32)).astype(bf16)
            return carry

        lax.fori_loop(0, 2 * zs, body, 0)
        fold_y(3).start()
        for p in range(3):
            fold_end(p, w1)
        fold_on(3)

        shp_copy.wait()
        mixed = shp[:, mine].astype(f32) + shpr[...].astype(f32)
        for c in range(chunks):
            for k in range(c * per, (c + 1) * per):
                if k > 0:
                    po_copy(k).wait_recv()
                weights = gate[pl.ds(lax.rem(me + k, G), 1), :]
                gated[(k - c * per) * C : (k - c * per + 1) * C, :] = (
                    plan[row_at(k), :].astype(f32) * weights
                ).astype(bf16)
            mixed = mixed + dot_tn(gated[...], ro[chunk_at(c), :])
        ob[:, mine] = (resid[:, mine] + mixed).astype(bf16)
        out_copy.start()
        dna_copy.wait()

        def last_step(i, carry):
            at = pl.ds(pl.multiple_of(i * FOLD, FOLD), FOLD)
            x = tok[at, :].astype(f32)
            r = lax.rsqrt(jnp.mean(x * x, axis=1, keepdims=True) + epsilon)
            a = (dna[at, :].astype(f32) + dnar[at, :].astype(f32)) * na[...].reshape(1, D)
            inner = jnp.mean(a * x, axis=1, keepdims=True)
            gtok[at, :] = (dres[at, :] + r * a - x * (r * r * r * inner)).astype(bf16)
            return carry

        lax.fori_loop(0, T // FOLD, last_step, 0)
        fold_end(3, w2)
        ends = [
            pltpu.make_async_copy(a, b, osem.at[i])
            for i, (a, b) in enumerate(((gtok, h_gtok), (w1, h_gw1), (w2, h_gw2), (ob, h_out)))
        ]
        for c in ends[:3]:
            c.start()
        out_copy.wait()
        ends[3].start()
        for c in ends:
            c.wait()

    pl.run_scoped(
        attention_back,
        pltpu.VMEM((T, D), f32),
        pltpu.VMEM((T, D), bf16),
        pltpu.VMEM((T, HL), bf16),
        pltpu.VMEM((3, T, HL), bf16),
        pltpu.VMEM((D, T), bf16),
        pltpu.VMEM((zs, 2, 2, share, W2), bf16),
        pltpu.VMEM((M, T), bf16),
        pltpu.VMEM((T, D), bf16),
        pltpu.VMEM((T, D), bf16),
        pltpu.VMEM((share, 3 * F), f32),
        pltpu.VMEM((share, W2), f32),
    )
    for c in range(chunks):
        part_copy(c).wait_send()
    for k in range(1, G):
        po_copy(k).wait_send()


def finish_kernel(
    HL, F, h_out, h_gtok, h_gw1, h_gw2, h_gein, h_geout,
    out, gtok, gqkv, gao, gna, gnf, gsi, gso, gein, geout,
):
    out[...] = h_out[...]
    gtok[...] = h_gtok[...]
    gein[...] = h_gein[...].astype(f32)
    geout[...] = h_geout[...].astype(f32)

    @pl.when(pl.program_id(0) == 0)
    def _():
        for s in range(3):
            gqkv[s] = h_gw2[:, s * HL : (s + 1) * HL]
        gao[...] = h_gw2[:, 3 * HL : 4 * HL].T
        gains = h_gw2[:, 4 * HL :].T
        gnf[...] = gains[0:1, :]
        gna[...] = gains[1:2, :]
        for s in range(2):
            gsi[s] = h_gw1[:, s * F : (s + 1) * F]
        gso[...] = h_gw1[:, 2 * F :].T


def fused(
    tokens, cont_lengths, routes, route_gates, w_qkv, w_attn_out, norm_attn, norm_ffn,
    shared_in, shared_out, expert_in, expert_out, cotangent,
):
    T, D = tokens.shape
    G = lax.axis_size("dp")
    HL, F = w_qkv.shape[2], shared_in.shape[2]
    C = round_up(CAP, 16)
    S = G * C
    half, share, zs = D // 2, D // G, G // 4
    W1, W2 = 3 * F, 4 * HL + 128
    shape = jax.ShapeDtypeStruct
    dma = pltpu.SemaphoreType.DMA
    SM = pl.BlockSpec(memory_space=pltpu.SMEM)
    out, gtok, gw1, gw2, gein, geout = pl.pallas_call(
        functools.partial(layer_kernel, G),
        out_shape=(
            shape((T, D), bf16), shape((T, D), bf16), shape((share, W1), f32), shape((share, W2), f32),
            shape((2, zs, 2, 2, share, F), bf16), shape((F, D), bf16),
        ),
        in_specs=[VM] * 2 + [SM] + [VM] * 2 + [ANY] * 8,
        out_specs=(ANY,) * 6,
        scratch_shapes=[
            pltpu.VMEM((T, D), bf16),
            pltpu.VMEM((3, D, HL), bf16),
            pltpu.VMEM((HL, D), bf16),
            pltpu.VMEM((T, D), bf16),
            pltpu.VMEM((T, 128), f32),
            pltpu.VMEM((T, 128), f32),
            pltpu.VMEM((3, T, HL), bf16),
            pltpu.VMEM((T, 128), f32),
            pltpu.VMEM((T, HL), bf16),
            pltpu.VMEM((T, D), bf16),
            pltpu.VMEM((T, D), f32),
            pltpu.VMEM((S, T), bf16),
            pltpu.VMEM((EXPERTS, T), f32),
            pltpu.VMEM((EXPERTS, T), f32),
            pltpu.VMEM((T, T), f32),
            pltpu.VMEM((T, HL), bf16),
            pltpu.VMEM((HL, D), bf16),
            pltpu.VMEM((S, D), bf16),
            pltpu.VMEM((S, D), bf16),
            pltpu.VMEM((S, D), bf16),
            pltpu.VMEM((S, half), bf16),
            pltpu.VMEM((S, half), bf16),
            pltpu.VMEM((S, half), bf16),
            pltpu.VMEM((T, D), bf16),
            pltpu.VMEM((T, half), bf16),
            pltpu.VMEM((T, D), bf16),
            pltpu.VMEM((T, D), bf16),
            pltpu.VMEM((S, half), bf16),
            pltpu.VMEM((S, half), bf16),
            pltpu.VMEM((T, half), bf16),
            pltpu.VMEM((8, D), f32),
            pltpu.VMEM((8, D), f32),
            *[
                pltpu.VMEM((*dims, share, width), bf16)
                for width in (W1, W2)
                for dims in ((zs, 2), (zs,), (zs - 1,))
            ],
            dma((12,)), dma((12,)), *[dma((G,))] * 8, dma((4,)), dma((4,)), dma((G,)), dma((G,)),
            dma((4,)), dma((4,)), dma((G,)), dma((G,)), dma((12,)), dma((12,)), dma((4,)), dma((4,)),
            dma((4, zs - 1)), dma((4, zs - 1)), dma((8,)), dma((4,)),
        ],
        compiler_params=pltpu.CompilerParams(
            collective_id=0, has_side_effects=True, vmem_limit_bytes=VMEM_BYTES
        ),
        name="layer",
    )(
        norm_attn, norm_ffn, cont_lengths, routes.T, route_gates.T, tokens, w_qkv, w_attn_out, cotangent,
        shared_in, shared_out, expert_in, expert_out,
    )
    steps = 4

    def rows_of(*dims):
        return pl.BlockSpec(dims, lambda i: (0,) * (len(dims) - 2) + (i, 0))

    def whole(*dims):
        return pl.BlockSpec(dims, lambda i: (0,) * len(dims))

    results = ((3, share, HL), (HL, share), (1, share), (1, share), (2, share, F), (F, share))
    out, gtok, gqkv, gao, gna, gnf, gsi, gso, gein, geout = pl.pallas_call(
        functools.partial(finish_kernel, HL, F),
        grid=(steps,),
        out_shape=(
            shape((T, D), bf16), shape((T, D), bf16), *[shape(r, f32) for r in results],
            shape((2, D, F), f32), shape((F, D), f32),
        ),
        in_specs=[
            rows_of(T // steps, D), rows_of(T // steps, D), whole(share, W1), whole(share, W2),
            rows_of(2, D // steps, F), rows_of(F // steps, D),
        ],
        out_specs=(
            rows_of(T // steps, D), rows_of(T // steps, D), *[whole(*r) for r in results],
            rows_of(2, D // steps, F), rows_of(F // steps, D),
        ),
        compiler_params=pltpu.CompilerParams(vmem_limit_bytes=VMEM_BYTES),
        name="finish",
    )(out, gtok, gw1, gw2, gein.reshape(2, D, F), geout)
    return (out, gtok, gqkv, gao, gna[0], gnf[0], gsi, gso, gein, geout)


def solution(mesh):
    placed = (
        P("dp", None),
        P("dp", None),
        P("dp", None),
        P("dp", None),
        P(None, None, "tensor"),
        P("tensor", None),
        P(),
        P(),
        P(None, None, "tensor"),
        P("tensor", None),
        P(None, None, ("dp", "tensor")),
        P(("dp", "tensor"), None),
        P("dp", None),
    )
    return jax.shard_map(
        fused if mesh.shape["dp"] == EXPERTS else local,
        mesh=mesh,
        in_specs=placed,
        out_specs=(
            P("dp", None),
            P("dp", None),
            P(None, "dp", "tensor"),
            P("tensor", "dp"),
            P("dp"),
            P("dp"),
            P(None, "dp", "tensor"),
            P("tensor", "dp"),
            P(None, None, ("dp", "tensor")),
            P(("dp", "tensor"), None),
        ),
        check_vma=False,
    )
```

```python
import functools
import math

import jax
import jax.numpy as jnp
from jax import lax
from jax.experimental import pallas as pl
from jax.experimental.pallas import tpu as pltpu
from jax.sharding import PartitionSpec as P

HD = 64
EXPERTS = 16
TOP = 2
PROMPT = 64
CAP = 92


epsilon = 1e-06


def rms_parts(values, gain):
    factor = lax.rsqrt(jnp.mean(values * values, axis=-1, keepdims=True) + epsilon)
    return (values * factor * gain, factor)


def rms_back(values, factor, gain, incoming):
    weighted = incoming * gain
    inner = jnp.mean(weighted * values, axis=-1, keepdims=True)
    return (
        factor * weighted - values * factor * factor * factor * inner,
        jnp.sum(incoming * values * factor, axis=0),
    )


def silu_act(values):
    return values * jax.nn.sigmoid(values)


def swiglu_back(gate_up, d_act):
    sigma = jax.nn.sigmoid(gate_up[0])
    d_gate = d_act * gate_up[1] * sigma * (1.0 + gate_up[0] * (1.0 - sigma))
    d_upper = d_act * gate_up[0] * sigma
    return jnp.stack([d_gate, d_upper]).astype(jnp.bfloat16)


def group_layout(lengths, rows_here):
    row_index = jnp.arange(rows_here, dtype=jnp.int32)
    cont_ends = PROMPT + jnp.cumsum(lengths, dtype=jnp.int32)
    begins = cont_ends - lengths
    later = jnp.sum(
        (row_index[:, None] >= cont_ends[None, :]).astype(jnp.int32), axis=1, dtype=jnp.int32
    )
    segment = jnp.where(row_index < PROMPT, 0, 1 + later)
    member = (
        segment[:, None] == jnp.arange(1, lengths.shape[0] + 1, dtype=jnp.int32)[None, :]
    ).astype(jnp.int32)
    offset = jnp.sum(member * begins[None, :], axis=1, dtype=jnp.int32)
    position = jnp.where(segment == 0, row_index, PROMPT + row_index - offset)
    allowed = (row_index[None, :] <= row_index[:, None]) & (
        (segment[None, :] == 0) | (segment[None, :] == segment[:, None])
    )
    return (position, allowed)


def rope_tables(position):
    half_size = HD // 2
    inv_freq = 10000.0 ** (-jnp.arange(half_size, dtype=jnp.float32) / half_size)
    angles = position.astype(jnp.float32)[:, None] * inv_freq[None, :]
    return (jnp.cos(angles)[:, None, :], jnp.sin(angles)[:, None, :])


def rotate_pairs(values, cosine, sine):
    half_size = values.shape[-1] // 2
    front_half = values[..., :half_size]
    back_half = values[..., half_size:]
    return jnp.concatenate(
        [front_half * cosine - back_half * sine, front_half * sine + back_half * cosine], axis=-1
    )


def dispatch_plan(routes):
    flat_routes = routes.reshape(-1)
    one_hot = (flat_routes[:, None] == jnp.arange(EXPERTS, dtype=jnp.int32)[None, :]).astype(
        jnp.int32
    )
    earlier = jnp.cumsum(one_hot, axis=0, dtype=jnp.int32) - one_hot
    place_in = jnp.sum(earlier * one_hot, axis=1, dtype=jnp.int32)
    target = flat_routes * CAP + place_in
    pair_count = flat_routes.shape[0]
    slot_table = (
        jnp.full((EXPERTS * CAP,), pair_count, jnp.int32)
        .at[target]
        .set(jnp.arange(pair_count, dtype=jnp.int32))
    )
    return (target, slot_table)


def spread_rows(padded, indices, copies):
    model_width = padded.shape[1]
    picked = jnp.take(padded, indices, axis=0).reshape(EXPERTS, 1, CAP, model_width)
    return jnp.broadcast_to(picked, (EXPERTS, copies, CAP, model_width)).reshape(
        EXPERTS * copies, CAP, model_width
    )


def collect_rows(returned, target, copies, rows_here):
    model_width = returned.shape[2]
    summed = jnp.sum(returned.reshape(EXPERTS, copies, CAP, model_width), axis=1, dtype=jnp.float32)
    summed = summed.reshape(EXPERTS * CAP, model_width)
    return jnp.take(summed, target, axis=0).reshape(rows_here, TOP, model_width)


def local(
    tokens,
    cont_lengths,
    routes,
    route_gates,
    w_qkv,
    w_attn_out,
    norm_attn,
    norm_ffn,
    shared_in,
    shared_out,
    expert_in,
    expert_out,
    cotangent,
):
    rows_here = tokens.shape[0]
    model_width = tokens.shape[1]
    groups = lax.axis_size("dp")
    copies = groups // EXPERTS
    head_count = w_qkv.shape[2] // HD
    score_scale = HD ** (-0.5)
    inputs = tokens.astype(jnp.float32)
    position, allowed = group_layout(cont_lengths[0], rows_here)
    cosine, sine = rope_tables(position)
    normed_a, factor_a = rms_parts(inputs, norm_attn)
    normed_attn = normed_a.astype(jnp.bfloat16)
    projected = jnp.einsum("td,sdf->stf", normed_attn, w_qkv, preferred_element_type=jnp.float32)
    query = rotate_pairs(projected[0].reshape(rows_here, head_count, HD), cosine, sine).astype(
        jnp.bfloat16
    )
    key_rows = rotate_pairs(projected[1].reshape(rows_here, head_count, HD), cosine, sine).astype(
        jnp.bfloat16
    )
    value_rows = projected[2].reshape(rows_here, head_count, HD).astype(jnp.bfloat16)
    score = (
        jnp.einsum("qhd,khd->hqk", query, key_rows, preferred_element_type=jnp.float32)
        * score_scale
    )
    score = jnp.where(allowed[None], score, -1000000000.0)
    row_max = jnp.max(score, axis=-1, keepdims=True)
    exponent = jnp.exp(score - row_max)
    row_total = jnp.sum(exponent, axis=-1, keepdims=True)
    log_total = row_max + jnp.log(row_total)
    weights_b = (exponent / row_total).astype(jnp.bfloat16)
    attended = jnp.einsum("hqk,khd->qhd", weights_b, value_rows, preferred_element_type=jnp.float32)
    attended = attended.reshape(rows_here, head_count * HD).astype(jnp.bfloat16)
    attn_part = jnp.dot(attended, w_attn_out, preferred_element_type=jnp.float32)
    resid = inputs + lax.psum(attn_part.astype(jnp.bfloat16), "tensor").astype(jnp.float32)
    normed_f, factor_f = rms_parts(resid, norm_ffn)
    normed_ffn = normed_f.astype(jnp.bfloat16)
    gate_up = jnp.einsum("td,sdf->stf", normed_ffn, shared_in, preferred_element_type=jnp.float32)
    shared_act = (silu_act(gate_up[0]) * gate_up[1]).astype(jnp.bfloat16)
    shared_part = jnp.dot(shared_act, shared_out, preferred_element_type=jnp.float32)
    target, slot_table = dispatch_plan(routes)
    padded_rows = jnp.concatenate([normed_ffn, jnp.zeros((1, model_width), jnp.bfloat16)], axis=0)
    send_rows = spread_rows(padded_rows, slot_table // TOP, copies)
    arrived = lax.all_to_all(send_rows, "dp", split_axis=0, concat_axis=0, tiled=True)
    expert_input = arrived.reshape(groups * CAP, model_width)
    expert_gu = jnp.einsum(
        "rd,sdf->srf", expert_input, expert_in, preferred_element_type=jnp.float32
    )
    expert_act = (silu_act(expert_gu[0]) * expert_gu[1]).astype(jnp.bfloat16)
    expert_part = jnp.dot(expert_act, expert_out, preferred_element_type=jnp.float32).astype(
        jnp.bfloat16
    )
    returned = lax.all_to_all(
        expert_part.reshape(groups, CAP, model_width), "dp", split_axis=0, concat_axis=0, tiled=True
    )
    picked = collect_rows(returned, target, copies, rows_here)
    mixed = jnp.sum(route_gates[:, :, None] * picked, axis=1)
    ffn_total = lax.psum((shared_part + mixed).astype(jnp.bfloat16), "tensor").astype(jnp.float32)
    output = (resid + ffn_total).astype(jnp.bfloat16)
    upstream = cotangent.astype(jnp.float32)
    d_shared_act = jnp.einsum(
        "td,fd->tf", cotangent, shared_out, preferred_element_type=jnp.float32
    )
    d_shared_gu = swiglu_back(gate_up, d_shared_act)
    d_normed = jnp.einsum("stf,sdf->td", d_shared_gu, shared_in, preferred_element_type=jnp.float32)
    g_shared_in = jnp.einsum(
        "td,stf->sdf", normed_ffn, d_shared_gu, preferred_element_type=jnp.float32
    )
    g_shared_out = jnp.einsum(
        "tf,td->fd", shared_act, cotangent, preferred_element_type=jnp.float32
    )
    pair_grad = (
        (route_gates[:, :, None] * upstream[:, None, :])
        .reshape(rows_here * TOP, model_width)
        .astype(jnp.bfloat16)
    )
    padded_grad = jnp.concatenate([pair_grad, jnp.zeros((1, model_width), jnp.bfloat16)], axis=0)
    send_grad = spread_rows(padded_grad, slot_table, copies)
    again_rows = spread_rows(padded_rows, slot_table // TOP, copies)
    grad_arrived, rows_arrived = (
        lax.all_to_all(send_grad, "dp", split_axis=0, concat_axis=0, tiled=True),
        lax.all_to_all(again_rows, "dp", split_axis=0, concat_axis=0, tiled=True),
    )
    rows_back = rows_arrived.reshape(groups * CAP, model_width)
    d_expert_rows = grad_arrived.reshape(groups * CAP, model_width)
    back_gu = jnp.einsum("rd,sdf->srf", rows_back, expert_in, preferred_element_type=jnp.float32)
    back_act = (silu_act(back_gu[0]) * back_gu[1]).astype(jnp.bfloat16)
    d_expert_act = jnp.einsum(
        "rd,fd->rf", d_expert_rows, expert_out, preferred_element_type=jnp.float32
    )
    d_expert_gu = swiglu_back(back_gu, d_expert_act)
    d_expert_in = jnp.einsum(
        "srf,sdf->rd", d_expert_gu, expert_in, preferred_element_type=jnp.float32
    ).astype(jnp.bfloat16)
    g_expert_in = jnp.einsum(
        "rd,srf->sdf", rows_back, d_expert_gu, preferred_element_type=jnp.float32
    )
    g_expert_out = jnp.einsum(
        "rf,rd->fd", back_act, d_expert_rows, preferred_element_type=jnp.float32
    )
    d_returned = lax.all_to_all(
        d_expert_in.reshape(groups, CAP, model_width), "dp", split_axis=0, concat_axis=0, tiled=True
    )
    d_normed = d_normed + jnp.sum(collect_rows(d_returned, target, copies, rows_here), axis=1)
    d_normed = lax.psum(d_normed.astype(jnp.bfloat16), "tensor").astype(jnp.float32)
    d_resid_norm, g_norm_ffn = rms_back(resid, factor_f, norm_ffn, d_normed)
    d_resid = upstream + d_resid_norm
    d_resid_b = d_resid.astype(jnp.bfloat16)
    g_attn_out = jnp.einsum("tf,td->fd", attended, d_resid_b, preferred_element_type=jnp.float32)
    d_attended = jnp.einsum("td,fd->tf", d_resid_b, w_attn_out, preferred_element_type=jnp.float32)
    d_attended = d_attended.astype(jnp.bfloat16).reshape(rows_here, head_count, HD)
    recomputed = (
        jnp.einsum("qhd,khd->hqk", query, key_rows, preferred_element_type=jnp.float32)
        * score_scale
    )
    recomputed = jnp.where(allowed[None], recomputed, -1000000000.0)
    probs = jnp.exp(recomputed - log_total)
    probs_b = probs.astype(jnp.bfloat16)
    d_probs = jnp.einsum("qhd,khd->hqk", d_attended, value_rows, preferred_element_type=jnp.float32)
    d_value = jnp.einsum("hqk,qhd->khd", probs_b, d_attended, preferred_element_type=jnp.float32)
    inner = jnp.sum(d_probs * probs, axis=-1, keepdims=True)
    d_score = (probs * (d_probs - inner)).astype(jnp.bfloat16)
    d_query = (
        jnp.einsum("hqk,khd->qhd", d_score, key_rows, preferred_element_type=jnp.float32)
        * score_scale
    )
    d_key = (
        jnp.einsum("hqk,qhd->khd", d_score, query, preferred_element_type=jnp.float32) * score_scale
    )
    d_query = rotate_pairs(d_query, cosine, -sine).reshape(rows_here, head_count * HD)
    d_key = rotate_pairs(d_key, cosine, -sine).reshape(rows_here, head_count * HD)
    d_qkv = jnp.stack([d_query, d_key, d_value.reshape(rows_here, head_count * HD)]).astype(
        jnp.bfloat16
    )
    g_qkv = jnp.einsum("td,stf->sdf", normed_attn, d_qkv, preferred_element_type=jnp.float32)
    d_normed_attn = jnp.einsum("stf,sdf->td", d_qkv, w_qkv, preferred_element_type=jnp.float32)
    d_normed_attn = lax.psum(d_normed_attn.astype(jnp.bfloat16), "tensor").astype(jnp.float32)
    d_input_norm, g_norm_attn = rms_back(inputs, factor_a, norm_attn, d_normed_attn)
    grad_tokens = (d_resid + d_input_norm).astype(jnp.bfloat16)
    summed_all = (
        lax.psum_scatter(g_qkv, "dp", scatter_dimension=1, tiled=True),
        lax.psum_scatter(g_attn_out, "dp", scatter_dimension=1, tiled=True),
        lax.psum_scatter(g_norm_attn, "dp", scatter_dimension=0, tiled=True),
        lax.psum_scatter(g_shared_in, "dp", scatter_dimension=1, tiled=True),
        lax.psum_scatter(g_shared_out, "dp", scatter_dimension=1, tiled=True),
        lax.psum_scatter(g_norm_ffn, "dp", scatter_dimension=0, tiled=True),
    )
    return (
        output,
        grad_tokens,
        summed_all[0],
        summed_all[1],
        summed_all[2],
        summed_all[5],
        summed_all[3],
        summed_all[4],
        g_expert_in,
        g_expert_out,
    )


VMEM_BYTES = 64000 * 1024
FOLD = 96
SPLIT = 7
MESH = pl.DeviceIdType.MESH
VM = pl.BlockSpec(memory_space=pltpu.VMEM)
ANY = pl.BlockSpec(memory_space=pl.ANY)
f32 = jnp.float32
bf16 = jnp.bfloat16


def round_up(value, unit):
    return (value + unit - 1) // unit * unit


def dot(a, b):
    return jnp.dot(a, b, preferred_element_type=f32)


def dot_nt(a, b):
    return lax.dot_general(a, b, (((1,), (1,)), ((), ())), preferred_element_type=f32)


def dot_tn(a, b):
    return lax.dot_general(a, b, (((0,), (0,)), ((), ())), preferred_element_type=f32)


def sigmoid(values):
    return 0.5 * jnp.tanh(0.5 * values) + 0.5


def swap_halves(values):
    lane = lax.broadcasted_iota(jnp.int32, values.shape, 1)
    ahead = pltpu.roll(values, values.shape[1] - HD // 2, 1)
    behind = pltpu.roll(values, HD // 2, 1)
    return jnp.where(lax.rem(lane, HD) < HD // 2, ahead, behind)


def hello(groups):
    me, t = lax.axis_index("dp"), lax.axis_index("tensor")
    barrier = pltpu.get_barrier_semaphore()

    def greet(k, carry):
        pl.semaphore_signal(
            barrier, inc=1, device_id=(lax.rem(me + k, groups), t), device_id_type=MESH
        )
        return carry

    lax.fori_loop(1, groups, greet, 0)
    pl.semaphore_signal(barrier, inc=1, device_id=(me, 1 - t), device_id_type=MESH)
    pl.semaphore_wait(barrier, groups)


def segment_of(index, lens):
    segment = jnp.where(index < PROMPT, 0, 1)
    end = PROMPT
    for c in range(lens.shape[1]):
        end = end + lens[0, c]
        segment = segment + jnp.where(index >= end, 1, 0)
    return segment


def position_of(index, lens):
    segment = segment_of(index, lens)
    position, end = index, PROMPT
    for c in range(lens.shape[1]):
        position = jnp.where(segment == c + 1, PROMPT + index - end, position)
        end = end + lens[0, c]
    return position


def fill_bias(bias, lens, rows):
    step = FOLD

    def body(i, carry):
        at = pl.ds(pl.multiple_of(i * step, step), step)
        row = lax.broadcasted_iota(jnp.int32, (step, rows), 0) + i * step
        col = lax.broadcasted_iota(jnp.int32, (step, rows), 1)
        own = segment_of(lax.broadcasted_iota(jnp.int32, (step, 1), 0) + i * step, lens)
        other = segment_of(lax.broadcasted_iota(jnp.int32, (1, rows), 1), lens)
        ok = (col <= row) & ((other == 0) | (other == own))
        bias[at, :] = jnp.where(ok, 0.0, -1000000000.0)
        return carry

    lax.fori_loop(0, rows // step, body, 0)


def fill_angles(cos, sin, lens, rows):
    step = FOLD

    def body(i, carry):
        at = pl.ds(pl.multiple_of(i * step, step), step)
        lane = lax.broadcasted_iota(jnp.int32, (step, 128), 1)
        row = lax.broadcasted_iota(jnp.int32, (step, 128), 0) + i * step
        power = lax.rem(lane, HD // 2).astype(f32) * (-math.log(10000.0) / (HD // 2))
        angle = position_of(row, lens).astype(f32) * jnp.exp(power)
        cos[at, :] = jnp.cos(angle)
        sine = jnp.sin(angle)
        sin[at, :] = jnp.where(lax.rem(lane, HD) < HD // 2, -sine, sine)
        return carry

    lax.fori_loop(0, rows // step, body, 0)


def send(src, dst, ssem, rsem, to):
    return pltpu.make_async_remote_copy(
        src_ref=src, dst_ref=dst, send_sem=ssem, recv_sem=rsem, device_id=to, device_id_type=MESH
    )


def layer_kernel(
    G, na, nf, lens, rT, gT, h_tok, h_wqkv, h_wo, h_cot, si, so, ei, eo,
    h_out, h_gtok, h_gw1, h_gw2, gein, geout,
    tok, wqkv, wo, cot, cos, sin, qkv, lse, att_own, normed_a, resid, plan, gate, slot, bias, att, wo2,
    csend, drows, rows, rets, ret, dxr, dnsh, dnsh_r, dnb, shp, partr, ro, shpr, gna, gnar,
    a1, b1, d1, a2, b2, d2,
    s_x, r_x, s_c, r_c, s_cf, r_cf, s_r, r_r, s_f, r_f, s_dx, r_dx, s_ret, r_ret, s_p, r_p, s_po, r_po,
    s_k, r_k, s_y, r_y, s_z, r_z, lsem, osem,
):
    T, D = tok.shape
    HL = wqkv.shape[2]
    F = si.shape[2]
    S = plan.shape[0]
    C = S // G
    half, share, zs = D // 2, D // G, G // 4
    W2 = a2.shape[3]
    scale = HD ** (-0.5)
    me, t = lax.axis_index("dp"), lax.axis_index("tensor")
    core, y, z = lax.rem(me, 2), lax.rem(me // 2, 2), me // 4
    mine = pl.ds(pl.multiple_of(t * half, 128), half)
    theirs = pl.ds(pl.multiple_of((1 - t) * half, 128), half)
    partner = (me, 1 - t)
    sibling = (me + 1 - 2 * core, t)
    neighbour = (me + 2 - 4 * y, t)
    per, tile = 4, 256
    M, chunks, tiles = per * C, G // per, F // tile

    loads = [
        pltpu.make_async_copy(a, b, lsem.at[i])
        for i, (a, b) in enumerate(((h_cot, cot), (h_tok, tok), (h_wqkv, wqkv), (h_wo, wo)))
    ]
    for c in loads:
        c.start()
    hello(G)
    part_wo = pl.ds(pl.multiple_of(core * (HL // 2), 16), HL // 2)
    wo_copy = send(h_wo.at[part_wo], wo2.at[part_wo], s_x.at[0], r_x.at[0], partner)
    wo_copy.start()
    wo_pass = send(wo2.at[part_wo], wo2.at[part_wo], s_x.at[6], r_x.at[6], sibling)

    def row_at(k):
        return pl.ds(pl.multiple_of(k * C, C), C)

    def chunk_at(c):
        return pl.ds(c * M, M)

    names = lax.broadcasted_iota(jnp.int32, (EXPERTS, T), 0)
    picks0, picks1 = rT[0:1, :] == names, rT[1:2, :] == names
    member = jnp.where(picks0 | picks1, 1.0, 0.0)
    upper = jnp.where(
        lax.broadcasted_iota(jnp.int32, (T, T), 0) < lax.broadcasted_iota(jnp.int32, (T, T), 1),
        1.0,
        0.0,
    ).astype(bf16)
    slot[...] = jnp.where(member > 0.0, dot(member.astype(bf16), upper), -1.0)
    gate[...] = jnp.where(picks0, gT[0:1, :], 0.0) + jnp.where(picks1, gT[1:2, :], 0.0)

    def cot_copy(k):
        return send(
            csend.at[row_at(k)], drows.at[row_at(k)], s_c.at[k], r_c.at[k], (lax.rem(me + k, G), t)
        )

    def cot_half(k):
        return send(
            csend.at[row_at(k), mine], drows.at[row_at(k), mine], s_c.at[k], r_c.at[k],
            (lax.rem(me + k, G), t),
        )

    def cot_pass(k):
        return send(
            drows.at[row_at(k), mine], drows.at[row_at(k), mine], s_cf.at[k], r_cf.at[k], partner
        )

    def cot_hand_on(k):
        cot_half(k).wait_recv()
        cot_pass(k).start()

    def cot_step(k, carry):
        e = lax.rem(me + k, G)
        at = row_at(k)
        place = lax.broadcasted_iota(jnp.int32, (C, T), 0).astype(f32)
        hit = slot[pl.ds(e, 1), :] == place
        picked = jnp.where(hit, 1.0, 0.0).astype(bf16)
        plan[at, :] = picked
        weight = jnp.sum(jnp.where(hit, gate[pl.ds(e, 1), :], 0.0), axis=1, keepdims=True)
        grad = (dot(picked, cot[...]) * weight).astype(bf16)
        csend[at, :] = grad

        @pl.when(k > SPLIT)
        def _():
            cot_copy(k).start()

        @pl.when((k > 0) & (k <= SPLIT))
        def _():
            cot_half(k).start()

        @pl.when(k == 0)
        def _():
            drows[at, :] = grad

        return carry

    loads[0].wait()
    lax.fori_loop(0, G, cot_step, 0)

    fill_angles(cos, sin, lens, T)
    fill_bias(bias, lens, T)
    cot_hand_on(1)
    loads[1].wait()

    def norm_step(i, carry):
        at = pl.ds(pl.multiple_of(i * FOLD, FOLD), FOLD)
        x = tok[at, :].astype(f32)
        r = lax.rsqrt(jnp.mean(x * x, axis=1, keepdims=True) + epsilon)
        normed_a[at, :] = (x * r * na[...].reshape(1, D)).astype(bf16)
        return carry

    lax.fori_loop(0, T // FOLD, norm_step, 0)
    cot_hand_on(2)
    loads[2].wait()
    loads[3].wait()

    def project(s, turned):
        full = dot(normed_a[...], wqkv[s])
        for j in range(HL // 128):
            x = full[:, j * 128 : (j + 1) * 128]
            if turned:
                x = x * cos[...] + swap_halves(x) * sin[...]
            qkv[s, :, j * 128 : (j + 1) * 128] = x.astype(bf16)

    project(0, True)
    project(1, True)
    project(2, False)
    cot_hand_on(3)
    lane = lax.broadcasted_iota(jnp.int32, (T, 128), 1)

    def att_copy(j):
        at = pl.ds(pl.multiple_of(j * 128, 128), 128)
        return send(att_own.at[:, at], att.at[:, at], s_x.at[1 + j], r_x.at[1 + j], partner)

    lse[...] = jnp.zeros_like(lse)

    def attend(j, carry):
        at = pl.ds(pl.multiple_of(j * 128, 128), 128)
        q, k, v = qkv[0, :, at], qkv[1, :, at], qkv[2, :, at]
        outs = []
        for i in range(2):
            inside = (lane < HD) if i == 0 else (lane >= HD)
            s = dot_nt(jnp.where(inside, q, jnp.zeros_like(q)), k) * scale + bias[...]
            top = jnp.max(s, axis=1, keepdims=True)
            e = jnp.exp(s - top)
            total = jnp.sum(e, axis=1, keepdims=True)
            p = (e * (1.0 / total)).astype(bf16)
            lse[...] = jnp.where(lane == 2 * j + i, top + jnp.log(total), lse[...])
            outs.append(dot(p, v))
        att_own[:, at] = jnp.where(lane < HD, outs[0], outs[1]).astype(bf16)
        att_copy(j).start()
        return carry

    wo_copy.wait()
    wo_pass.start()
    lax.fori_loop(0, HL // 128, attend, 0)
    own_out = dot(att_own[...], wo[...])
    wo_pass.wait()
    for j in range(HL // 128):
        att_copy(j).wait()
    for k in range(4, SPLIT + 1):
        cot_hand_on(k)
    resid[...] = tok[...].astype(f32) + own_out + dot(att[...], wo2[...])

    def row_copy(k):
        return send(
            rets.at[row_at(k)], rows.at[row_at(k), mine], s_r.at[k], r_r.at[k], (lax.rem(me + k, G), t)
        )

    def row_pass(k):
        return send(
            rows.at[row_at(k), mine], rows.at[row_at(k), mine], s_f.at[k], r_f.at[k], partner
        )

    def hand_on(k):
        row_copy(k).wait_recv()
        row_pass(k).start()

    def dx_copy(c):
        return send(csend.at[chunk_at(c), theirs], dxr.at[chunk_at(c)], s_dx.at[c], r_dx.at[c], partner)

    def ret_copy(k):
        return send(
            rets.at[row_at(k)], ret.at[row_at(k)], s_ret.at[k], r_ret.at[k], (lax.rem(me - k + G, G), t)
        )

    def return_chunk(c):
        dx_copy(c).wait_recv()
        total = (csend[chunk_at(c), mine].astype(f32) + dxr[chunk_at(c), :].astype(f32)).astype(bf16)
        for k in range(c * per, (c + 1) * per):
            if k > 0:
                row_copy(k).wait_send()
        rets[chunk_at(c), :] = total
        for k in range(c * per, (c + 1) * per):
            if k > 0:
                ret_copy(k).start()
        if c == 0:
            ret[0:C, :] = total[0:C, :]

    def part_copy(c):
        return send(csend.at[chunk_at(c), theirs], partr.at[chunk_at(c)], s_p.at[c], r_p.at[c], partner)

    def po_copy(k):
        return send(
            rets.at[row_at(k)], ro.at[row_at(k)], s_po.at[k], r_po.at[k], (lax.rem(me - k + G, G), t)
        )

    def return_part(c):
        part_copy(c).wait_recv()
        total = (csend[chunk_at(c), mine].astype(f32) + partr[chunk_at(c), :].astype(f32)).astype(bf16)
        for k in range(c * per, (c + 1) * per):
            if k > 0:
                ret_copy(k).wait_send()
        rets[chunk_at(c), :] = total
        for k in range(c * per, (c + 1) * per):
            if k > 0:
                po_copy(k).start()
        if c == 0:
            ro[0:C, :] = total[0:C, :]

    dnar, ob = rows.at[0:T], rows.at[T : 2 * T]
    out_copy = send(ob.at[:, mine], ob.at[:, mine], s_x.at[8], r_x.at[8], partner)
    gna_copy = send(gna, gnar, s_x.at[9], r_x.at[9], partner)
    dnb_copy = send(dnb.at[:, mine], dnb.at[:, mine], s_x.at[5], r_x.at[5], partner)
    dnsh_copy = send(dnsh.at[:, theirs], dnsh_r, s_x.at[4], r_x.at[4], partner)
    shp_copy = send(shp.at[:, theirs], shpr, s_x.at[7], r_x.at[7], partner)

    def columns(p):
        return slice(p * F, (p + 1) * F) if p < 3 else (slice(0, HL), slice(HL, W2))[p - 3]

    def fold_bufs(p):
        return (a1, b1, d1) if p < 3 else (a2, b2, d2)

    def fold_y(p):
        a, b, d = fold_bufs(p)
        return send(
            a.at[:, 1 - y, :, columns(p)], b.at[:, :, columns(p)], s_y.at[p], r_y.at[p], neighbour
        )

    def fold_z(p, k):
        a, b, d = fold_bufs(p)
        to = lax.rem(z + k, zs)
        return send(
            b.at[to, :, columns(p)], d.at[k - 1, :, columns(p)], s_z.at[p, k - 1], r_z.at[p, k - 1],
            (to * 4 + lax.rem(me, 4), t),
        )

    def fold_on(p):
        a, b, d = fold_bufs(p)
        fold_y(p).wait()

        def body(i, carry):
            b[i, :, columns(p)] = (
                b[i, :, columns(p)].astype(f32) + a[i, y, :, columns(p)].astype(f32)
            ).astype(bf16)
            return carry

        lax.fori_loop(0, zs, body, 0)
        for k in range(1, zs):
            fold_z(p, k).start()

    def fold_end(p, w):
        a, b, d = fold_bufs(p)
        total = b[z, :, columns(p)].astype(f32)
        for k in range(1, zs):
            fold_z(p, k).wait()
            total = total + d[k - 1, :, columns(p)].astype(f32)
        w[:, columns(p)] = total

    def experts(vsi, vso, vei, veo, act, dgu, normed, tall, wide):
        weights = [
            pltpu.make_async_copy(a, b, lsem.at[4 + i])
            for i, (a, b) in enumerate(((si, vsi), (so, vso), (ei, vei), (eo, veo)))
        ]
        for c in weights:
            c.start()

        def norm2_step(i, carry):
            at = pl.ds(pl.multiple_of(i * FOLD, FOLD), FOLD)
            x = resid[at, :]
            r = lax.rsqrt(jnp.mean(x * x, axis=1, keepdims=True) + epsilon)
            normed[at, :] = (x * r * nf[...].reshape(1, D)).astype(bf16)
            return carry

        lax.fori_loop(0, T // FOLD, norm2_step, 0)

        def row_step(k, carry):
            values = dot(plan[row_at(k), :], normed[:, mine]).astype(bf16)
            rets[row_at(k), :] = values

            @pl.when(k > 0)
            def _():
                row_copy(k).start()

            @pl.when(k == 0)
            def _():
                rows[row_at(k), mine] = values
                row_pass(k).start()

            return carry

        lax.fori_loop(0, G, row_step, 0)

        mid = slice(S - T, S)

        def shared_step(u, carry):
            at = pl.ds(pl.multiple_of(u * tile, tile), tile)
            pre = dot(normed[...], vsi[0, :, at])
            up = dot(normed[...], vsi[1, :, at])
            d_act = dot_nt(cot[...], vso[at, :])
            s = sigmoid(pre)
            gs = pre * s
            act[mid, at] = (gs * up).astype(bf16)
            dgu[0, mid, at] = (d_act * up * (s + gs * (1.0 - s))).astype(bf16)
            dgu[1, mid, at] = (d_act * gs).astype(bf16)
            return carry

        def tile_at(i):
            return pl.ds(pl.multiple_of(i * tile, tile), tile)

        def fold_core(i):
            return send(
                tall.at[lax.rem(i, 2), :, :, 1 - core], a1.at[:, :, :, tile_at(i)], s_k.at[i], r_k.at[i],
                sibling,
            )

        def core_end(i):
            fold_core(i).wait()

            def body(n, carry):
                u, v = n // 2, lax.rem(n, 2)
                a1[u, v, :, tile_at(i)] = (
                    a1[u, v, :, tile_at(i)].astype(f32) + tall[lax.rem(i, 2), u, v, core].astype(f32)
                ).astype(bf16)
                return carry

            lax.fori_loop(0, 2 * zs, body, 0)

        def shared_grads(p):
            def body(i, carry):
                at = tile_at(i - p * tiles)
                if p < 2:
                    grad = dot(vsi[0, :, 0:T], dgu[p, mid, at])
                else:
                    grad = dot(vsi[1, :, 0:T], act[mid, at])
                tall[lax.rem(i, 2)] = grad.astype(bf16).reshape(tall.shape[1:])
                fold_core(i).start()

                @pl.when(i > p * tiles)
                def _():
                    core_end(i - 1)

                return carry

            lax.fori_loop(p * tiles, (p + 1) * tiles, body, 0)
            core_end((p + 1) * tiles - 1)
            fold_y(p).start()

        def expert_chunk(c):
            for k in range(c * per, (c + 1) * per):
                row_pass(k).wait_recv()
                if k > SPLIT:
                    cot_copy(k).wait_recv()
                elif k > 0:
                    cot_pass(k).wait_recv()
            block = chunk_at(c)

            def unit_step(u, carry):
                at = pl.ds(pl.multiple_of(u * tile, tile), tile)
                pre = dot(rows[block, :], vei[0, :, at])
                up = dot(rows[block, :], vei[1, :, at])
                d_act = dot_nt(drows[block, :], veo[at, :])
                s = sigmoid(pre)
                gs = pre * s
                act[block, at] = (gs * up).astype(bf16)
                dgu[0, block, at] = (d_act * up * (s + gs * (1.0 - s))).astype(bf16)
                dgu[1, block, at] = (d_act * gs).astype(bf16)
                return carry

            lax.fori_loop(0, tiles, unit_step, 0)
            dx = dot_nt(dgu[0, block, :], vei[0]) + dot_nt(dgu[1, block, :], vei[1])
            for k in range(c * per, (c + 1) * per):
                if k > SPLIT:
                    cot_copy(k).wait_send()
                elif k > 0:
                    cot_half(k).wait_send()
            csend[block, :] = dx.astype(bf16)
            dx_copy(c).start()

        weights[0].wait()
        weights[1].wait()
        lax.fori_loop(0, tiles, shared_step, 0)
        for k in range(1, 4):
            hand_on(k)
        dnsh[...] = (dot_nt(dgu[0, mid, :], vsi[0]) + dot_nt(dgu[1, mid, :], vsi[1])).astype(bf16)
        dnsh_copy.start()
        weights[2].wait()
        weights[3].wait()
        vsi[0, :, 0:T] = normed[...].T
        vsi[1, :, 0:T] = cot[...].T
        shp[...] = dot(act[mid, :], vso[...]).astype(bf16)
        shared_grads(0)
        for k in range(4, 8):
            hand_on(k)
        expert_chunk(0)
        shared_grads(1)
        for k in range(8, 10):
            hand_on(k)
        expert_chunk(1)
        return_chunk(0)
        for k in range(10, 12):
            hand_on(k)
        shared_grads(2)
        for k in range(12, 14):
            hand_on(k)
        expert_chunk(2)
        return_chunk(1)
        for k in range(14, G):
            hand_on(k)
        expert_chunk(3)
        return_chunk(2)

        def part_chunk(c):
            dx_copy(c).wait_send()
            csend[chunk_at(c), :] = dot(act[chunk_at(c), :], veo[...]).astype(bf16)

        for c in range(chunks - 1):
            part_chunk(c)
        return_chunk(3)
        part_copy(0).start()
        part_copy(1).start()
        part_chunk(3)
        sides = [slice(0, S // 2), slice(S // 2, S)]
        for n in range(2):
            vsi[n, :, 0 : S // 2] = rows[sides[n], :].T

        def gein_copy(i):
            return pltpu.make_async_copy(
                tall.at[lax.rem(i, 2)], gein.at[i // tiles, :, :, :, :, tile_at(lax.rem(i, tiles))],
                osem.at[lax.rem(i, 2)],
            )

        def gein_step(i, carry):
            @pl.when(i > 1)
            def _():
                gein_copy(i - 2).wait()

            at = tile_at(lax.rem(i, tiles))
            grad = dot(vsi[0, :, 0 : S // 2], dgu[i // tiles, sides[0], at])
            grad = grad + dot(vsi[1, :, 0 : S // 2], dgu[i // tiles, sides[1], at])
            tall[lax.rem(i, 2)] = grad.astype(bf16).reshape(tall.shape[1:])
            gein_copy(i).start()
            return carry

        first = 2
        lax.fori_loop(0, first, gein_step, 0)
        for k in range(G):
            row_pass(k).wait_send()

        dnsh_copy.wait()
        total = dnsh[:, mine].astype(f32) + dnsh_r[...].astype(f32)
        for c in range(chunks):
            for k in range(c * per, (c + 1) * per):
                if k > 0:
                    ret_copy(k).wait_recv()
            total = total + dot_tn(plan[chunk_at(c), :], ret[chunk_at(c), :])
        dnb[:, mine] = total.astype(bf16)
        dnb_copy.start()
        part_copy(2).start()
        for p in range(3):
            fold_on(p)
        lax.fori_loop(first, 2 * tiles, gein_step, 0)
        return_part(0)
        return_part(1)

        def geout_copy(i):
            return pltpu.make_async_copy(
                wide.at[lax.rem(i, 2)], geout.at[tile_at(i), :], osem.at[2 + lax.rem(i, 2)]
            )

        def geout_step(i, carry):
            @pl.when(i > 1)
            def _():
                geout_copy(i - 2).wait()

            wide[lax.rem(i, 2)] = dot_tn(act[:, tile_at(i)], drows[...]).astype(bf16)
            geout_copy(i).start()
            return carry

        lax.fori_loop(0, tiles, geout_step, 0)
        gein_copy(2 * tiles - 2).wait()
        gein_copy(2 * tiles - 1).wait()
        geout_copy(tiles - 2).wait()
        geout_copy(tiles - 1).wait()

    pl.run_scoped(
        experts,
        pltpu.VMEM((2, D, F), bf16),
        pltpu.VMEM((F, D), bf16),
        pltpu.VMEM((2, D, F), bf16),
        pltpu.VMEM((F, D), bf16),
        pltpu.VMEM((S, F), bf16),
        pltpu.VMEM((2, S, F), bf16),
        pltpu.VMEM((T, D), bf16),
        pltpu.VMEM((2, zs, 2, 2, share, tile), bf16),
        pltpu.VMEM((2, tile, D), bf16),
    )

    def attention_back(dres, dresb, da, dqkv, turned, turned2, pay, gated, dna, gtok, w1, w2):
        dna_copy = send(dna, dnar, s_x.at[10], r_x.at[10], partner)
        turned[...] = normed_a[...].T
        dnb_copy.wait()
        part_copy(3).start()
        shp_copy.start()

        def dres_step(i, carry):
            at = pl.ds(pl.multiple_of(i * FOLD, FOLD), FOLD)
            y_ = dnb[at, :].astype(f32)
            x = resid[at, :]
            r = lax.rsqrt(jnp.mean(x * x, axis=1, keepdims=True) + epsilon)
            a = y_ * nf[...].reshape(1, D)
            inner = jnp.mean(a * x, axis=1, keepdims=True)
            xr = x * r
            value = cot[at, :].astype(f32) + r * a - xr * (r * r * inner)
            dres[at, :] = value
            dresb[at, :] = value.astype(bf16)
            return carry + jnp.sum(y_ * xr, axis=0, keepdims=True)

        gnf = lax.fori_loop(0, T // FOLD, dres_step, jnp.zeros((1, D), f32))
        da[...] = dot_nt(dresb[...], wo[...]).astype(bf16)
        turned2[...] = dresb[...].T
        pay[:, :, :, :, 0:HL] = dot(turned2[...], att_own[...]).astype(bf16).reshape(zs, 2, 2, share, HL)

        def pay_core(p):
            return send(
                pay.at[:, :, 1 - core, :, columns(p)], a2.at[:, :, :, columns(p)], s_x.at[8 + p], r_x.at[8 + p],
                sibling,
            )

        def pay_on(p):
            pay_core(p).wait()

            def body(n, carry):
                u, v = n // 2, lax.rem(n, 2)
                a2[u, v, :, columns(p)] = (
                    a2[u, v, :, columns(p)].astype(f32) + pay[u, v, core, :, columns(p)].astype(f32)
                ).astype(bf16)
                return carry

            lax.fori_loop(0, 2 * zs, body, 0)
            fold_y(p).start()

        pay_core(3).start()

        def attend_back(j, carry):
            at = pl.ds(pl.multiple_of(j * 128, 128), 128)
            q, k, v, g = qkv[0, :, at], qkv[1, :, at], qkv[2, :, at], da[:, at]
            none = jnp.zeros_like(q)
            dq = dk = dv = jnp.zeros((T, 128), f32)
            for i in range(2):
                inside = (lane < HD) if i == 0 else (lane >= HD)
                qi, ki, gi = (jnp.where(inside, x, none) for x in (q, k, g))
                total = jnp.sum(jnp.where(lane == 2 * j + i, lse[...], 0.0), axis=1, keepdims=True)
                p = jnp.exp(dot_nt(qi, k) * scale + bias[...] - total)
                dp = dot_nt(gi, v)
                inner = jnp.sum(dp * p, axis=1, keepdims=True)
                ds = (p * (dp - inner)).astype(bf16)
                dv = dv + dot_tn(p.astype(bf16), gi)
                dq = dq + dot(ds, ki)
                dk = dk + dot_tn(ds, qi)
            dq, dk = dq * scale, dk * scale
            dqkv[0, :, at] = (dq * cos[...] - swap_halves(dq) * sin[...]).astype(bf16)
            dqkv[1, :, at] = (dk * cos[...] - swap_halves(dk) * sin[...]).astype(bf16)
            dqkv[2, :, at] = dv.astype(bf16)
            return carry

        lax.fori_loop(0, HL // 128, attend_back, 0)
        pay_on(3)

        dna[...] = (
            dot_nt(dqkv[0], wqkv[0]) + dot_nt(dqkv[1], wqkv[1]) + dot_nt(dqkv[2], wqkv[2])
        ).astype(bf16)

        def gain_step(i, carry):
            at = pl.ds(pl.multiple_of(i * FOLD, FOLD), FOLD)
            x = tok[at, :].astype(f32)
            r = lax.rsqrt(jnp.mean(x * x, axis=1, keepdims=True) + epsilon)
            return carry + jnp.sum(dna[at, :].astype(f32) * x * r, axis=0, keepdims=True)

        gna[...] = jnp.broadcast_to(
            lax.fori_loop(0, T // FOLD, gain_step, jnp.zeros((1, D), f32)), gna.shape
        )
        gna_copy.start()
        dna_copy.start()
        return_part(2)
        return_part(3)
        for s in range(3):
            pay[:, :, :, :, (s + 1) * HL : (s + 2) * HL] = (
                dot(turned[...], dqkv[s]).astype(bf16).reshape(zs, 2, 2, share, HL)
            )
        gna_copy.wait()
        row = lax.broadcasted_iota(jnp.int32, (128, D), 0)
        gains = jnp.where(row == 0, gnf, jnp.where(row == 1, gna[0:1, :] + gnar[0:1, :], 0.0))
        pay[:, :, :, :, 4 * HL :] = gains.T.astype(bf16).reshape(zs, 2, 2, share, 128)
        pay_core(4).start()
        fold_on(3)
        pay_on(4)
        for p in range(3):
            fold_end(p, w1)
        fold_on(4)

        shp_copy.wait()
        mixed = shp[:, mine].astype(f32) + shpr[...].astype(f32)
        for c in range(chunks):
            for k in range(c * per, (c + 1) * per):
                if k > 0:
                    po_copy(k).wait_recv()
                weights = gate[pl.ds(lax.rem(me + k, G), 1), :]
                gated[(k - c * per) * C : (k - c * per + 1) * C, :] = (
                    plan[row_at(k), :].astype(f32) * weights
                ).astype(bf16)
            mixed = mixed + dot_tn(gated[...], ro[chunk_at(c), :])
        ob[:, mine] = (resid[:, mine] + mixed).astype(bf16)
        out_copy.start()
        dna_copy.wait()

        def last_step(i, carry):
            at = pl.ds(pl.multiple_of(i * FOLD, FOLD), FOLD)
            x = tok[at, :].astype(f32)
            r = lax.rsqrt(jnp.mean(x * x, axis=1, keepdims=True) + epsilon)
            a = (dna[at, :].astype(f32) + dnar[at, :].astype(f32)) * na[...].reshape(1, D)
            inner = jnp.mean(a * x, axis=1, keepdims=True)
            gtok[at, :] = (dres[at, :] + r * a - x * (r * r * r * inner)).astype(bf16)
            return carry

        lax.fori_loop(0, T // FOLD, last_step, 0)
        fold_end(3, w2)
        fold_end(4, w2)
        ends = [
            pltpu.make_async_copy(a, b, osem.at[i])
            for i, (a, b) in enumerate(((gtok, h_gtok), (w1, h_gw1), (w2, h_gw2), (ob, h_out)))
        ]
        for c in ends[:3]:
            c.start()
        out_copy.wait()
        ends[3].start()
        for c in ends:
            c.wait()

    pl.run_scoped(
        attention_back,
        pltpu.VMEM((T, D), f32),
        pltpu.VMEM((T, D), bf16),
        pltpu.VMEM((T, HL), bf16),
        pltpu.VMEM((3, T, HL), bf16),
        pltpu.VMEM((D, T), bf16),
        pltpu.VMEM((D, T), bf16),
        pltpu.VMEM((zs, 2, 2, share, W2), bf16),
        pltpu.VMEM((M, T), bf16),
        pltpu.VMEM((T, D), bf16),
        pltpu.VMEM((T, D), bf16),
        pltpu.VMEM((share, 3 * F), f32),
        pltpu.VMEM((share, W2), f32),
    )
    for k in range(1, SPLIT + 1):
        cot_pass(k).wait_send()
    for c in range(chunks):
        part_copy(c).wait_send()
    for k in range(1, G):
        po_copy(k).wait_send()


def finish_kernel(
    HL, F, h_out, h_gtok, h_gw1, h_gw2, h_gein, h_geout,
    out, gtok, gqkv, gao, gna, gnf, gsi, gso, gein, geout,
):
    out[...] = h_out[...]
    gtok[...] = h_gtok[...]
    gein[...] = h_gein[...].astype(f32)
    geout[...] = h_geout[...].astype(f32)

    @pl.when(pl.program_id(0) == 0)
    def _():
        for s in range(3):
            gqkv[s] = h_gw2[:, (s + 1) * HL : (s + 2) * HL]
        gao[...] = h_gw2[:, 0:HL]
        gains = h_gw2[:, 4 * HL :].T
        gnf[...] = gains[0:1, :]
        gna[...] = gains[1:2, :]
        for s in range(2):
            gsi[s] = h_gw1[:, s * F : (s + 1) * F]
        gso[...] = h_gw1[:, 2 * F :]


def fused(
    tokens, cont_lengths, routes, route_gates, w_qkv, w_attn_out, norm_attn, norm_ffn,
    shared_in, shared_out, expert_in, expert_out, cotangent,
):
    T, D = tokens.shape
    G = lax.axis_size("dp")
    HL, F = w_qkv.shape[2], shared_in.shape[2]
    C = round_up(CAP, 16)
    S = G * C
    half, share, zs = D // 2, D // G, G // 4
    W1, W2 = 3 * F, 4 * HL + 128
    shape = jax.ShapeDtypeStruct
    dma = pltpu.SemaphoreType.DMA
    SM = pl.BlockSpec(memory_space=pltpu.SMEM)
    out, gtok, gw1, gw2, gein, geout = pl.pallas_call(
        functools.partial(layer_kernel, G),
        out_shape=(
            shape((T, D), bf16), shape((T, D), bf16), shape((share, W1), f32), shape((share, W2), f32),
            shape((2, zs, 2, 2, share, F), bf16), shape((F, D), bf16),
        ),
        in_specs=[VM] * 2 + [SM] + [VM] * 2 + [ANY] * 8,
        out_specs=(ANY,) * 6,
        scratch_shapes=[
            pltpu.VMEM((T, D), bf16),
            pltpu.VMEM((3, D, HL), bf16),
            pltpu.VMEM((HL, D), bf16),
            pltpu.VMEM((T, D), bf16),
            pltpu.VMEM((T, 128), f32),
            pltpu.VMEM((T, 128), f32),
            pltpu.VMEM((3, T, HL), bf16),
            pltpu.VMEM((T, 128), f32),
            pltpu.VMEM((T, HL), bf16),
            pltpu.VMEM((T, D), bf16),
            pltpu.VMEM((T, D), f32),
            pltpu.VMEM((S, T), bf16),
            pltpu.VMEM((EXPERTS, T), f32),
            pltpu.VMEM((EXPERTS, T), f32),
            pltpu.VMEM((T, T), f32),
            pltpu.VMEM((T, HL), bf16),
            pltpu.VMEM((HL, D), bf16),
            pltpu.VMEM((S, D), bf16),
            pltpu.VMEM((S, D), bf16),
            pltpu.VMEM((S, D), bf16),
            pltpu.VMEM((S, half), bf16),
            pltpu.VMEM((S, half), bf16),
            pltpu.VMEM((S, half), bf16),
            pltpu.VMEM((T, D), bf16),
            pltpu.VMEM((T, half), bf16),
            pltpu.VMEM((T, D), bf16),
            pltpu.VMEM((T, D), bf16),
            pltpu.VMEM((S, half), bf16),
            pltpu.VMEM((S, half), bf16),
            pltpu.VMEM((T, half), bf16),
            pltpu.VMEM((8, D), f32),
            pltpu.VMEM((8, D), f32),
            *[
                pltpu.VMEM((*dims, share, width), bf16)
                for width in (W1, W2)
                for dims in ((zs, 2), (zs,), (zs - 1,))
            ],
            dma((13,)), dma((13,)), *[dma((G,))] * 8, dma((4,)), dma((4,)), dma((G,)), dma((G,)),
            dma((4,)), dma((4,)), dma((G,)), dma((G,)), dma((12,)), dma((12,)), dma((5,)), dma((5,)),
            dma((5, zs - 1)), dma((5, zs - 1)), dma((8,)), dma((4,)),
        ],
        compiler_params=pltpu.CompilerParams(
            collective_id=0, has_side_effects=True, vmem_limit_bytes=VMEM_BYTES
        ),
        name="layer",
    )(
        norm_attn, norm_ffn, cont_lengths, routes.T, route_gates.T, tokens, w_qkv, w_attn_out, cotangent,
        shared_in, shared_out, expert_in, expert_out,
    )
    steps = 4

    def rows_of(*dims):
        return pl.BlockSpec(dims, lambda i: (0,) * (len(dims) - 2) + (i, 0))

    def whole(*dims):
        return pl.BlockSpec(dims, lambda i: (0,) * len(dims))

    results = ((3, share, HL), (share, HL), (1, share), (1, share), (2, share, F), (share, F))
    out, gtok, gqkv, gao, gna, gnf, gsi, gso, gein, geout = pl.pallas_call(
        functools.partial(finish_kernel, HL, F),
        grid=(steps,),
        out_shape=(
            shape((T, D), bf16), shape((T, D), bf16), *[shape(r, f32) for r in results],
            shape((2, D, F), f32), shape((F, D), f32),
        ),
        in_specs=[
            rows_of(T // steps, D), rows_of(T // steps, D), whole(share, W1), whole(share, W2),
            rows_of(2, D // steps, F), rows_of(F // steps, D),
        ],
        out_specs=(
            rows_of(T // steps, D), rows_of(T // steps, D), *[whole(*r) for r in results],
            rows_of(2, D // steps, F), rows_of(F // steps, D),
        ),
        compiler_params=pltpu.CompilerParams(vmem_limit_bytes=VMEM_BYTES),
        name="finish",
    )(out, gtok, gw1, gw2, gein.reshape(2, D, F), geout)
    return (out, gtok, gqkv, gao.T, gna[0], gnf[0], gsi, gso.T, gein, geout)


def solution(mesh):
    placed = (
        P("dp", None),
        P("dp", None),
        P("dp", None),
        P("dp", None),
        P(None, None, "tensor"),
        P("tensor", None),
        P(),
        P(),
        P(None, None, "tensor"),
        P("tensor", None),
        P(None, None, ("dp", "tensor")),
        P(("dp", "tensor"), None),
        P("dp", None),
    )
    return jax.shard_map(
        fused if mesh.shape["dp"] == EXPERTS else local,
        mesh=mesh,
        in_specs=placed,
        out_specs=(
            P("dp", None),
            P("dp", None),
            P(None, "dp", "tensor"),
            P("tensor", "dp"),
            P("dp"),
            P("dp"),
            P(None, "dp", "tensor"),
            P("tensor", "dp"),
            P(None, None, ("dp", "tensor")),
            P(("dp", "tensor"), None),
        ),
        check_vma=False,
    )
```

```python
import functools
import math

import jax
import jax.numpy as jnp
from jax import lax
from jax.experimental import pallas as pl
from jax.experimental.pallas import tpu as pltpu
from jax.sharding import PartitionSpec as P

HD = 64
EXPERTS = 16
TOP = 2
PROMPT = 64
CAP = 92


epsilon = 1e-06


def rms_parts(values, gain):
    factor = lax.rsqrt(jnp.mean(values * values, axis=-1, keepdims=True) + epsilon)
    return (values * factor * gain, factor)


def rms_back(values, factor, gain, incoming):
    weighted = incoming * gain
    inner = jnp.mean(weighted * values, axis=-1, keepdims=True)
    return (
        factor * weighted - values * factor * factor * factor * inner,
        jnp.sum(incoming * values * factor, axis=0),
    )


def silu_act(values):
    return values * jax.nn.sigmoid(values)


def swiglu_back(gate_up, d_act):
    sigma = jax.nn.sigmoid(gate_up[0])
    d_gate = d_act * gate_up[1] * sigma * (1.0 + gate_up[0] * (1.0 - sigma))
    d_upper = d_act * gate_up[0] * sigma
    return jnp.stack([d_gate, d_upper]).astype(jnp.bfloat16)


def group_layout(lengths, rows_here):
    row_index = jnp.arange(rows_here, dtype=jnp.int32)
    cont_ends = PROMPT + jnp.cumsum(lengths, dtype=jnp.int32)
    begins = cont_ends - lengths
    later = jnp.sum(
        (row_index[:, None] >= cont_ends[None, :]).astype(jnp.int32), axis=1, dtype=jnp.int32
    )
    segment = jnp.where(row_index < PROMPT, 0, 1 + later)
    member = (
        segment[:, None] == jnp.arange(1, lengths.shape[0] + 1, dtype=jnp.int32)[None, :]
    ).astype(jnp.int32)
    offset = jnp.sum(member * begins[None, :], axis=1, dtype=jnp.int32)
    position = jnp.where(segment == 0, row_index, PROMPT + row_index - offset)
    allowed = (row_index[None, :] <= row_index[:, None]) & (
        (segment[None, :] == 0) | (segment[None, :] == segment[:, None])
    )
    return (position, allowed)


def rope_tables(position):
    half_size = HD // 2
    inv_freq = 10000.0 ** (-jnp.arange(half_size, dtype=jnp.float32) / half_size)
    angles = position.astype(jnp.float32)[:, None] * inv_freq[None, :]
    return (jnp.cos(angles)[:, None, :], jnp.sin(angles)[:, None, :])


def rotate_pairs(values, cosine, sine):
    half_size = values.shape[-1] // 2
    front_half = values[..., :half_size]
    back_half = values[..., half_size:]
    return jnp.concatenate(
        [front_half * cosine - back_half * sine, front_half * sine + back_half * cosine], axis=-1
    )


def dispatch_plan(routes):
    flat_routes = routes.reshape(-1)
    one_hot = (flat_routes[:, None] == jnp.arange(EXPERTS, dtype=jnp.int32)[None, :]).astype(
        jnp.int32
    )
    earlier = jnp.cumsum(one_hot, axis=0, dtype=jnp.int32) - one_hot
    place_in = jnp.sum(earlier * one_hot, axis=1, dtype=jnp.int32)
    target = flat_routes * CAP + place_in
    pair_count = flat_routes.shape[0]
    slot_table = (
        jnp.full((EXPERTS * CAP,), pair_count, jnp.int32)
        .at[target]
        .set(jnp.arange(pair_count, dtype=jnp.int32))
    )
    return (target, slot_table)


def spread_rows(padded, indices, copies):
    model_width = padded.shape[1]
    picked = jnp.take(padded, indices, axis=0).reshape(EXPERTS, 1, CAP, model_width)
    return jnp.broadcast_to(picked, (EXPERTS, copies, CAP, model_width)).reshape(
        EXPERTS * copies, CAP, model_width
    )


def collect_rows(returned, target, copies, rows_here):
    model_width = returned.shape[2]
    summed = jnp.sum(returned.reshape(EXPERTS, copies, CAP, model_width), axis=1, dtype=jnp.float32)
    summed = summed.reshape(EXPERTS * CAP, model_width)
    return jnp.take(summed, target, axis=0).reshape(rows_here, TOP, model_width)


def local(
    tokens,
    cont_lengths,
    routes,
    route_gates,
    w_qkv,
    w_attn_out,
    norm_attn,
    norm_ffn,
    shared_in,
    shared_out,
    expert_in,
    expert_out,
    cotangent,
):
    rows_here = tokens.shape[0]
    model_width = tokens.shape[1]
    groups = lax.axis_size("dp")
    copies = groups // EXPERTS
    head_count = w_qkv.shape[2] // HD
    score_scale = HD ** (-0.5)
    inputs = tokens.astype(jnp.float32)
    position, allowed = group_layout(cont_lengths[0], rows_here)
    cosine, sine = rope_tables(position)
    normed_a, factor_a = rms_parts(inputs, norm_attn)
    normed_attn = normed_a.astype(jnp.bfloat16)
    projected = jnp.einsum("td,sdf->stf", normed_attn, w_qkv, preferred_element_type=jnp.float32)
    query = rotate_pairs(projected[0].reshape(rows_here, head_count, HD), cosine, sine).astype(
        jnp.bfloat16
    )
    key_rows = rotate_pairs(projected[1].reshape(rows_here, head_count, HD), cosine, sine).astype(
        jnp.bfloat16
    )
    value_rows = projected[2].reshape(rows_here, head_count, HD).astype(jnp.bfloat16)
    score = (
        jnp.einsum("qhd,khd->hqk", query, key_rows, preferred_element_type=jnp.float32)
        * score_scale
    )
    score = jnp.where(allowed[None], score, -1000000000.0)
    row_max = jnp.max(score, axis=-1, keepdims=True)
    exponent = jnp.exp(score - row_max)
    row_total = jnp.sum(exponent, axis=-1, keepdims=True)
    log_total = row_max + jnp.log(row_total)
    weights_b = (exponent / row_total).astype(jnp.bfloat16)
    attended = jnp.einsum("hqk,khd->qhd", weights_b, value_rows, preferred_element_type=jnp.float32)
    attended = attended.reshape(rows_here, head_count * HD).astype(jnp.bfloat16)
    attn_part = jnp.dot(attended, w_attn_out, preferred_element_type=jnp.float32)
    resid = inputs + lax.psum(attn_part.astype(jnp.bfloat16), "tensor").astype(jnp.float32)
    normed_f, factor_f = rms_parts(resid, norm_ffn)
    normed_ffn = normed_f.astype(jnp.bfloat16)
    gate_up = jnp.einsum("td,sdf->stf", normed_ffn, shared_in, preferred_element_type=jnp.float32)
    shared_act = (silu_act(gate_up[0]) * gate_up[1]).astype(jnp.bfloat16)
    shared_part = jnp.dot(shared_act, shared_out, preferred_element_type=jnp.float32)
    target, slot_table = dispatch_plan(routes)
    padded_rows = jnp.concatenate([normed_ffn, jnp.zeros((1, model_width), jnp.bfloat16)], axis=0)
    send_rows = spread_rows(padded_rows, slot_table // TOP, copies)
    arrived = lax.all_to_all(send_rows, "dp", split_axis=0, concat_axis=0, tiled=True)
    expert_input = arrived.reshape(groups * CAP, model_width)
    expert_gu = jnp.einsum(
        "rd,sdf->srf", expert_input, expert_in, preferred_element_type=jnp.float32
    )
    expert_act = (silu_act(expert_gu[0]) * expert_gu[1]).astype(jnp.bfloat16)
    expert_part = jnp.dot(expert_act, expert_out, preferred_element_type=jnp.float32).astype(
        jnp.bfloat16
    )
    returned = lax.all_to_all(
        expert_part.reshape(groups, CAP, model_width), "dp", split_axis=0, concat_axis=0, tiled=True
    )
    picked = collect_rows(returned, target, copies, rows_here)
    mixed = jnp.sum(route_gates[:, :, None] * picked, axis=1)
    ffn_total = lax.psum((shared_part + mixed).astype(jnp.bfloat16), "tensor").astype(jnp.float32)
    output = (resid + ffn_total).astype(jnp.bfloat16)
    upstream = cotangent.astype(jnp.float32)
    d_shared_act = jnp.einsum(
        "td,fd->tf", cotangent, shared_out, preferred_element_type=jnp.float32
    )
    d_shared_gu = swiglu_back(gate_up, d_shared_act)
    d_normed = jnp.einsum("stf,sdf->td", d_shared_gu, shared_in, preferred_element_type=jnp.float32)
    g_shared_in = jnp.einsum(
        "td,stf->sdf", normed_ffn, d_shared_gu, preferred_element_type=jnp.float32
    )
    g_shared_out = jnp.einsum(
        "tf,td->fd", shared_act, cotangent, preferred_element_type=jnp.float32
    )
    pair_grad = (
        (route_gates[:, :, None] * upstream[:, None, :])
        .reshape(rows_here * TOP, model_width)
        .astype(jnp.bfloat16)
    )
    padded_grad = jnp.concatenate([pair_grad, jnp.zeros((1, model_width), jnp.bfloat16)], axis=0)
    send_grad = spread_rows(padded_grad, slot_table, copies)
    again_rows = spread_rows(padded_rows, slot_table // TOP, copies)
    grad_arrived, rows_arrived = (
        lax.all_to_all(send_grad, "dp", split_axis=0, concat_axis=0, tiled=True),
        lax.all_to_all(again_rows, "dp", split_axis=0, concat_axis=0, tiled=True),
    )
    rows_back = rows_arrived.reshape(groups * CAP, model_width)
    d_expert_rows = grad_arrived.reshape(groups * CAP, model_width)
    back_gu = jnp.einsum("rd,sdf->srf", rows_back, expert_in, preferred_element_type=jnp.float32)
    back_act = (silu_act(back_gu[0]) * back_gu[1]).astype(jnp.bfloat16)
    d_expert_act = jnp.einsum(
        "rd,fd->rf", d_expert_rows, expert_out, preferred_element_type=jnp.float32
    )
    d_expert_gu = swiglu_back(back_gu, d_expert_act)
    d_expert_in = jnp.einsum(
        "srf,sdf->rd", d_expert_gu, expert_in, preferred_element_type=jnp.float32
    ).astype(jnp.bfloat16)
    g_expert_in = jnp.einsum(
        "rd,srf->sdf", rows_back, d_expert_gu, preferred_element_type=jnp.float32
    )
    g_expert_out = jnp.einsum(
        "rf,rd->fd", back_act, d_expert_rows, preferred_element_type=jnp.float32
    )
    d_returned = lax.all_to_all(
        d_expert_in.reshape(groups, CAP, model_width), "dp", split_axis=0, concat_axis=0, tiled=True
    )
    d_normed = d_normed + jnp.sum(collect_rows(d_returned, target, copies, rows_here), axis=1)
    d_normed = lax.psum(d_normed.astype(jnp.bfloat16), "tensor").astype(jnp.float32)
    d_resid_norm, g_norm_ffn = rms_back(resid, factor_f, norm_ffn, d_normed)
    d_resid = upstream + d_resid_norm
    d_resid_b = d_resid.astype(jnp.bfloat16)
    g_attn_out = jnp.einsum("tf,td->fd", attended, d_resid_b, preferred_element_type=jnp.float32)
    d_attended = jnp.einsum("td,fd->tf", d_resid_b, w_attn_out, preferred_element_type=jnp.float32)
    d_attended = d_attended.astype(jnp.bfloat16).reshape(rows_here, head_count, HD)
    recomputed = (
        jnp.einsum("qhd,khd->hqk", query, key_rows, preferred_element_type=jnp.float32)
        * score_scale
    )
    recomputed = jnp.where(allowed[None], recomputed, -1000000000.0)
    probs = jnp.exp(recomputed - log_total)
    probs_b = probs.astype(jnp.bfloat16)
    d_probs = jnp.einsum("qhd,khd->hqk", d_attended, value_rows, preferred_element_type=jnp.float32)
    d_value = jnp.einsum("hqk,qhd->khd", probs_b, d_attended, preferred_element_type=jnp.float32)
    inner = jnp.sum(d_probs * probs, axis=-1, keepdims=True)
    d_score = (probs * (d_probs - inner)).astype(jnp.bfloat16)
    d_query = (
        jnp.einsum("hqk,khd->qhd", d_score, key_rows, preferred_element_type=jnp.float32)
        * score_scale
    )
    d_key = (
        jnp.einsum("hqk,qhd->khd", d_score, query, preferred_element_type=jnp.float32) * score_scale
    )
    d_query = rotate_pairs(d_query, cosine, -sine).reshape(rows_here, head_count * HD)
    d_key = rotate_pairs(d_key, cosine, -sine).reshape(rows_here, head_count * HD)
    d_qkv = jnp.stack([d_query, d_key, d_value.reshape(rows_here, head_count * HD)]).astype(
        jnp.bfloat16
    )
    g_qkv = jnp.einsum("td,stf->sdf", normed_attn, d_qkv, preferred_element_type=jnp.float32)
    d_normed_attn = jnp.einsum("stf,sdf->td", d_qkv, w_qkv, preferred_element_type=jnp.float32)
    d_normed_attn = lax.psum(d_normed_attn.astype(jnp.bfloat16), "tensor").astype(jnp.float32)
    d_input_norm, g_norm_attn = rms_back(inputs, factor_a, norm_attn, d_normed_attn)
    grad_tokens = (d_resid + d_input_norm).astype(jnp.bfloat16)
    summed_all = (
        lax.psum_scatter(g_qkv, "dp", scatter_dimension=1, tiled=True),
        lax.psum_scatter(g_attn_out, "dp", scatter_dimension=1, tiled=True),
        lax.psum_scatter(g_norm_attn, "dp", scatter_dimension=0, tiled=True),
        lax.psum_scatter(g_shared_in, "dp", scatter_dimension=1, tiled=True),
        lax.psum_scatter(g_shared_out, "dp", scatter_dimension=1, tiled=True),
        lax.psum_scatter(g_norm_ffn, "dp", scatter_dimension=0, tiled=True),
    )
    return (
        output,
        grad_tokens,
        summed_all[0],
        summed_all[1],
        summed_all[2],
        summed_all[5],
        summed_all[3],
        summed_all[4],
        g_expert_in,
        g_expert_out,
    )


VMEM_BYTES = 64000 * 1024
FOLD = 96
MESH = pl.DeviceIdType.MESH
VM = pl.BlockSpec(memory_space=pltpu.VMEM)
ANY = pl.BlockSpec(memory_space=pl.ANY)
f32 = jnp.float32
bf16 = jnp.bfloat16


def round_up(value, unit):
    return (value + unit - 1) // unit * unit


def dot(a, b):
    return jnp.dot(a, b, preferred_element_type=f32)


def dot_nt(a, b):
    return lax.dot_general(a, b, (((1,), (1,)), ((), ())), preferred_element_type=f32)


def dot_tn(a, b):
    return lax.dot_general(a, b, (((0,), (0,)), ((), ())), preferred_element_type=f32)


def sigmoid(values):
    return 0.5 * jnp.tanh(0.5 * values) + 0.5


def swap_halves(values):
    lane = lax.broadcasted_iota(jnp.int32, values.shape, 1)
    ahead = pltpu.roll(values, values.shape[1] - HD // 2, 1)
    behind = pltpu.roll(values, HD // 2, 1)
    return jnp.where(lax.rem(lane, HD) < HD // 2, ahead, behind)


def hello(groups):
    me, t = lax.axis_index("dp"), lax.axis_index("tensor")
    barrier = pltpu.get_barrier_semaphore()

    def greet(k, carry):
        pl.semaphore_signal(
            barrier, inc=1, device_id=(lax.rem(me + k, groups), t), device_id_type=MESH
        )
        return carry

    lax.fori_loop(1, groups, greet, 0)
    pl.semaphore_signal(barrier, inc=1, device_id=(me, 1 - t), device_id_type=MESH)
    pl.semaphore_wait(barrier, groups)


def segment_of(index, lens):
    segment = jnp.where(index < PROMPT, 0, 1)
    end = PROMPT
    for c in range(lens.shape[1]):
        end = end + lens[0, c]
        segment = segment + jnp.where(index >= end, 1, 0)
    return segment


def position_of(index, lens):
    segment = segment_of(index, lens)
    position, end = index, PROMPT
    for c in range(lens.shape[1]):
        position = jnp.where(segment == c + 1, PROMPT + index - end, position)
        end = end + lens[0, c]
    return position


def fill_bias(bias, lens, rows):
    step = FOLD

    def body(i, carry):
        at = pl.ds(pl.multiple_of(i * step, step), step)
        row = lax.broadcasted_iota(jnp.int32, (step, rows), 0) + i * step
        col = lax.broadcasted_iota(jnp.int32, (step, rows), 1)
        own = segment_of(lax.broadcasted_iota(jnp.int32, (step, 1), 0) + i * step, lens)
        other = segment_of(lax.broadcasted_iota(jnp.int32, (1, rows), 1), lens)
        ok = (col <= row) & ((other == 0) | (other == own))
        bias[at, :] = jnp.where(ok, 0.0, -1000000000.0)
        return carry

    lax.fori_loop(0, rows // step, body, 0)


def fill_angles(cos, sin, lens, rows):
    step = FOLD

    def body(i, carry):
        at = pl.ds(pl.multiple_of(i * step, step), step)
        lane = lax.broadcasted_iota(jnp.int32, (step, 128), 1)
        row = lax.broadcasted_iota(jnp.int32, (step, 128), 0) + i * step
        power = lax.rem(lane, HD // 2).astype(f32) * (-math.log(10000.0) / (HD // 2))
        angle = position_of(row, lens).astype(f32) * jnp.exp(power)
        cos[at, :] = jnp.cos(angle)
        sine = jnp.sin(angle)
        sin[at, :] = jnp.where(lax.rem(lane, HD) < HD // 2, -sine, sine)
        return carry

    lax.fori_loop(0, rows // step, body, 0)


def send(src, dst, ssem, rsem, to):
    return pltpu.make_async_remote_copy(
        src_ref=src, dst_ref=dst, send_sem=ssem, recv_sem=rsem, device_id=to, device_id_type=MESH
    )


def layer_kernel(
    G, na, nf, lens, rT, gT, h_tok, h_wqkv, h_wo, h_cot, si, so, ei, eo,
    h_out, h_gtok, h_gw1, h_gw2, gein, geout,
    tok, wqkv, wo, cot, cos, sin, qkv, lse, att_own, normed_a, resid, plan, gate, slot, bias, att, wo2,
    csend, drows, rows, near_send, rets, near_ret, ret, dxr, dnsh, dnsh_r, dnb, shp, partr, near_ro, ro, shpr, gna, gnar,
    a1, b1, d1, a2, b2, d2,
    s_x, r_x, s_c, r_c, s_cf, r_cf, s_r, r_r, s_f, r_f, s_dx, r_dx, s_ret, r_ret, s_p, r_p, s_po, r_po,
    s_k, r_k, s_y, r_y, s_z, r_z, lsem, osem,
):
    T, D = tok.shape
    HL = wqkv.shape[2]
    F = si.shape[2]
    S = plan.shape[0]
    C = S // G
    half, share, zs = D // 2, D // G, G // 4
    W2 = a2.shape[3]
    scale = HD ** (-0.5)
    me, t = lax.axis_index("dp"), lax.axis_index("tensor")
    core, y, z = lax.rem(me, 2), lax.rem(me // 2, 2), me // 4
    mine = pl.ds(pl.multiple_of(t * half, 128), half)
    theirs = pl.ds(pl.multiple_of((1 - t) * half, 128), half)
    partner = (me, 1 - t)
    sibling = (me + 1 - 2 * core, t)
    neighbour = (me + 2 - 4 * y, t)
    per, tile = 4, 256
    M, chunks, tiles = per * C, G // per, F // tile

    loads = [
        pltpu.make_async_copy(a, b, lsem.at[i])
        for i, (a, b) in enumerate(((h_cot, cot), (h_tok, tok), (h_wqkv, wqkv), (h_wo, wo)))
    ]
    for c in loads:
        c.start()
    hello(G)
    part_wo = pl.ds(pl.multiple_of(core * (HL // 2), 16), HL // 2)
    wo_copy = send(h_wo.at[part_wo], wo2.at[part_wo], s_x.at[0], r_x.at[0], partner)
    wo_copy.start()
    wo_pass = send(wo2.at[part_wo], wo2.at[part_wo], s_x.at[6], r_x.at[6], sibling)

    def row_at(k):
        return pl.ds(pl.multiple_of(k * C, C), C)

    def chunk_at(c):
        return pl.ds(c * M, M)

    near = G // 2

    def peer(k):
        to, weight = me, 1
        while weight < G:
            bit = lax.rem(k // weight, 2)
            to = to + weight * bit * (1 - 2 * lax.rem(me // weight, 2))
            weight = weight * 2
        return to

    def far_at(k):
        return pl.ds(pl.multiple_of((k - per) * C, C), C)

    def out_at(k):
        return pl.ds(pl.multiple_of((k - near) * C, C), C)

    def far_chunk(c):
        return pl.ds((c - 1) * M, M)

    def out_chunk(c):
        return pl.ds((c - near // per) * M, M)

    names = lax.broadcasted_iota(jnp.int32, (EXPERTS, T), 0)
    picks0, picks1 = rT[0:1, :] == names, rT[1:2, :] == names
    member = jnp.where(picks0 | picks1, 1.0, 0.0)
    upper = jnp.where(
        lax.broadcasted_iota(jnp.int32, (T, T), 0) < lax.broadcasted_iota(jnp.int32, (T, T), 1),
        1.0,
        0.0,
    ).astype(bf16)
    slot[...] = jnp.where(member > 0.0, dot(member.astype(bf16), upper), -1.0)
    gate[...] = jnp.where(picks0, gT[0:1, :], 0.0) + jnp.where(picks1, gT[1:2, :], 0.0)

    def cot_copy(k):
        return send(csend.at[row_at(k)], drows.at[row_at(k)], s_c.at[k], r_c.at[k], (peer(k), t))

    def cot_half(k):
        return send(
            csend.at[row_at(k), mine], drows.at[row_at(k), mine], s_c.at[k], r_c.at[k], (peer(k), t)
        )

    def cot_pass(k):
        return send(
            drows.at[row_at(k), mine], drows.at[row_at(k), mine], s_cf.at[k], r_cf.at[k], partner
        )

    def cot_hand_on(k):
        cot_half(k).wait_recv()
        cot_pass(k).start()

    def cot_step(i, carry):
        k = G - 1 - i
        e = peer(k)
        at = row_at(k)
        place = lax.broadcasted_iota(jnp.int32, (C, T), 0).astype(f32)
        hit = slot[pl.ds(e, 1), :] == place
        picked = jnp.where(hit, 1.0, 0.0).astype(bf16)
        plan[at, :] = picked
        weight = jnp.sum(jnp.where(hit, gate[pl.ds(e, 1), :], 0.0), axis=1, keepdims=True)
        grad = (dot(picked, cot[...]) * weight).astype(bf16)
        csend[at, :] = grad

        @pl.when(k >= near)
        def _():
            cot_half(k).start()

        @pl.when((k > 0) & (k < near))
        def _():
            cot_copy(k).start()

        @pl.when(k == 0)
        def _():
            drows[at, :] = grad

        return carry

    loads[0].wait()
    lax.fori_loop(0, G, cot_step, 0)

    fill_angles(cos, sin, lens, T)
    fill_bias(bias, lens, T)
    cot_hand_on(G - 1)
    loads[1].wait()

    def norm_step(i, carry):
        at = pl.ds(pl.multiple_of(i * FOLD, FOLD), FOLD)
        x = tok[at, :].astype(f32)
        r = lax.rsqrt(jnp.mean(x * x, axis=1, keepdims=True) + epsilon)
        normed_a[at, :] = (x * r * na[...].reshape(1, D)).astype(bf16)
        return carry

    lax.fori_loop(0, T // FOLD, norm_step, 0)
    cot_hand_on(G - 2)
    loads[2].wait()
    loads[3].wait()

    def project(s, turned):
        full = dot(normed_a[...], wqkv[s])
        for j in range(HL // 128):
            x = full[:, j * 128 : (j + 1) * 128]
            if turned:
                x = x * cos[...] + swap_halves(x) * sin[...]
            qkv[s, :, j * 128 : (j + 1) * 128] = x.astype(bf16)

    project(0, True)
    project(1, True)
    project(2, False)
    cot_hand_on(G - 3)
    lane = lax.broadcasted_iota(jnp.int32, (T, 128), 1)

    def att_copy(j):
        at = pl.ds(pl.multiple_of(j * 128, 128), 128)
        return send(att_own.at[:, at], att.at[:, at], s_x.at[1 + j], r_x.at[1 + j], partner)

    lse[...] = jnp.zeros_like(lse)

    def attend(j, carry):
        at = pl.ds(pl.multiple_of(j * 128, 128), 128)
        q, k, v = qkv[0, :, at], qkv[1, :, at], qkv[2, :, at]
        outs = []
        for i in range(2):
            inside = (lane < HD) if i == 0 else (lane >= HD)
            s = dot_nt(jnp.where(inside, q, jnp.zeros_like(q)), k) * scale + bias[...]
            top = jnp.max(s, axis=1, keepdims=True)
            e = jnp.exp(s - top)
            total = jnp.sum(e, axis=1, keepdims=True)
            p = (e * (1.0 / total)).astype(bf16)
            lse[...] = jnp.where(lane == 2 * j + i, top + jnp.log(total), lse[...])
            outs.append(dot(p, v))
        att_own[:, at] = jnp.where(lane < HD, outs[0], outs[1]).astype(bf16)
        att_copy(j).start()
        return carry

    wo_copy.wait()
    wo_pass.start()
    lax.fori_loop(0, HL // 128, attend, 0)
    own_out = dot(att_own[...], wo[...])
    wo_pass.wait()
    for j in range(HL // 128):
        att_copy(j).wait()
    for k in range(G - 4, near - 1, -1):
        cot_hand_on(k)
    resid[...] = tok[...].astype(f32) + own_out + dot(att[...], wo2[...])

    def row_copy(k):
        return send(near_send.at[row_at(k)], rows.at[row_at(k)], s_r.at[k], r_r.at[k], (peer(k), t))

    def row_half(k):
        return send(rets.at[far_at(k)], rows.at[row_at(k), mine], s_r.at[k], r_r.at[k], (peer(k), t))

    def row_pass(k):
        return send(
            rows.at[row_at(k), mine], rows.at[row_at(k), mine], s_f.at[k], r_f.at[k], partner
        )

    def hand_on(k):
        row_half(k).wait_recv()
        row_pass(k).start()

    def dx_copy(c):
        return send(csend.at[chunk_at(c), theirs], dxr.at[far_chunk(c)], s_dx.at[c], r_dx.at[c], partner)

    def ret_copy(k):
        return send(csend.at[row_at(k)], near_ret.at[row_at(k)], s_ret.at[k], r_ret.at[k], (peer(k), t))

    def ret_half(k):
        return send(rets.at[far_at(k)], ret.at[far_at(k)], s_ret.at[k], r_ret.at[k], (peer(k), t))

    def return_chunk(c):
        dx_copy(c).wait_recv()
        total = (csend[chunk_at(c), mine].astype(f32) + dxr[far_chunk(c), :].astype(f32)).astype(bf16)
        for k in range(c * per, (c + 1) * per):
            if k >= near:
                row_half(k).wait_send()
        rets[far_chunk(c), :] = total
        for k in range(c * per, (c + 1) * per):
            ret_half(k).start()

    def part_copy(c):
        return send(csend.at[chunk_at(c), theirs], partr.at[out_chunk(c)], s_p.at[c], r_p.at[c], partner)

    def po_copy(k):
        return send(csend.at[row_at(k)], near_ro.at[row_at(k)], s_po.at[k], r_po.at[k], (peer(k), t))

    def po_half(k):
        return send(rets.at[far_at(k)], ro.at[out_at(k)], s_po.at[k], r_po.at[k], (peer(k), t))

    def return_part(c):
        part_copy(c).wait_recv()
        total = (csend[chunk_at(c), mine].astype(f32) + partr[out_chunk(c), :].astype(f32)).astype(bf16)
        for k in range(c * per, (c + 1) * per):
            ret_half(k).wait_send()
        rets[far_chunk(c), :] = total
        for k in range(c * per, (c + 1) * per):
            po_half(k).start()

    dnar, ob = rows.at[0:T], rows.at[T : 2 * T]
    out_copy = send(ob.at[:, mine], ob.at[:, mine], s_x.at[8], r_x.at[8], partner)
    gna_copy = send(gna, gnar, s_x.at[9], r_x.at[9], partner)
    dnb_copy = send(dnb.at[:, mine], dnb.at[:, mine], s_x.at[5], r_x.at[5], partner)
    dnsh_copy = send(dnsh.at[:, theirs], dnsh_r, s_x.at[4], r_x.at[4], partner)
    shp_copy = send(shp.at[:, theirs], shpr, s_x.at[7], r_x.at[7], partner)

    def columns(p):
        return slice(p * F, (p + 1) * F) if p < 3 else (slice(0, HL), slice(HL, W2))[p - 3]

    def fold_bufs(p):
        return (a1, b1, d1) if p < 3 else (a2, b2, d2)

    def fold_y(p):
        a, b, d = fold_bufs(p)
        return send(
            a.at[:, 1 - y, :, columns(p)], b.at[:, :, columns(p)], s_y.at[p], r_y.at[p], neighbour
        )

    def fold_z(p, k):
        a, b, d = fold_bufs(p)
        to = lax.rem(z + k, zs)
        return send(
            b.at[to, :, columns(p)], d.at[k - 1, :, columns(p)], s_z.at[p, k - 1], r_z.at[p, k - 1],
            (to * 4 + lax.rem(me, 4), t),
        )

    def fold_on(p):
        a, b, d = fold_bufs(p)
        fold_y(p).wait()

        def body(i, carry):
            b[i, :, columns(p)] = (
                b[i, :, columns(p)].astype(f32) + a[i, y, :, columns(p)].astype(f32)
            ).astype(bf16)
            return carry

        lax.fori_loop(0, zs, body, 0)
        for k in range(1, zs):
            fold_z(p, k).start()

    def fold_end(p, w):
        a, b, d = fold_bufs(p)
        total = b[z, :, columns(p)].astype(f32)
        for k in range(1, zs):
            fold_z(p, k).wait()
            total = total + d[k - 1, :, columns(p)].astype(f32)
        w[:, columns(p)] = total

    def experts(vsi, vso, vei, veo, act, dgu, normed, tall, wide):
        weights = [
            pltpu.make_async_copy(a, b, lsem.at[4 + i])
            for i, (a, b) in enumerate(((si, vsi), (so, vso), (ei, vei), (eo, veo)))
        ]
        for c in weights:
            c.start()

        def norm2_step(i, carry):
            at = pl.ds(pl.multiple_of(i * FOLD, FOLD), FOLD)
            x = resid[at, :]
            r = lax.rsqrt(jnp.mean(x * x, axis=1, keepdims=True) + epsilon)
            normed[at, :] = (x * r * nf[...].reshape(1, D)).astype(bf16)
            return carry

        lax.fori_loop(0, T // FOLD, norm2_step, 0)

        def near_step(k, carry):
            values = dot(plan[row_at(k), :], normed[...]).astype(bf16)

            @pl.when(k > 0)
            def _():
                near_send[row_at(k), :] = values
                row_copy(k).start()

            @pl.when(k == 0)
            def _():
                rows[row_at(k), :] = values

            return carry

        def far_step(i, carry):
            k = G - 1 - i
            rets[far_at(k), :] = dot(plan[row_at(k), :], normed[:, mine]).astype(bf16)
            row_half(k).start()
            return carry

        lax.fori_loop(0, G - near, far_step, 0)
        lax.fori_loop(0, near, near_step, 0)

        mid = slice(M, M + T)

        def shared_step(u, carry):
            at = pl.ds(pl.multiple_of(u * tile, tile), tile)
            pre = dot(normed[...], vsi[0, :, at])
            up = dot(normed[...], vsi[1, :, at])
            d_act = dot_nt(cot[...], vso[at, :])
            s = sigmoid(pre)
            gs = pre * s
            act[mid, at] = (gs * up).astype(bf16)
            dgu[0, mid, at] = (d_act * up * (s + gs * (1.0 - s))).astype(bf16)
            dgu[1, mid, at] = (d_act * gs).astype(bf16)
            return carry

        def tile_at(i):
            return pl.ds(pl.multiple_of(i * tile, tile), tile)

        def fold_core(i):
            return send(
                tall.at[lax.rem(i, 2), :, :, 1 - core], a1.at[:, :, :, tile_at(i)], s_k.at[i], r_k.at[i],
                sibling,
            )

        def core_end(i):
            fold_core(i).wait()

            def body(n, carry):
                u, v = n // 2, lax.rem(n, 2)
                a1[u, v, :, tile_at(i)] = (
                    a1[u, v, :, tile_at(i)].astype(f32) + tall[lax.rem(i, 2), u, v, core].astype(f32)
                ).astype(bf16)
                return carry

            lax.fori_loop(0, 2 * zs, body, 0)

        def shared_grads(p):
            def body(i, carry):
                at = tile_at(i - p * tiles)
                if p < 2:
                    grad = dot(vsi[0, :, 0:T], dgu[p, mid, at])
                else:
                    grad = dot(vsi[1, :, 0:T], act[mid, at])
                tall[lax.rem(i, 2)] = grad.astype(bf16).reshape(tall.shape[1:])
                fold_core(i).start()

                @pl.when(i > p * tiles)
                def _():
                    core_end(i - 1)

                return carry

            lax.fori_loop(p * tiles, (p + 1) * tiles, body, 0)
            core_end((p + 1) * tiles - 1)
            fold_y(p).start()

        def expert_chunk(c):
            for k in range(c * per, (c + 1) * per):
                if k >= near:
                    row_pass(k).wait_recv()
                    cot_pass(k).wait_recv()
                elif k > 0:
                    row_copy(k).wait_recv()
                    cot_copy(k).wait_recv()
            block = chunk_at(c)

            def unit_step(u, carry):
                at = pl.ds(pl.multiple_of(u * tile, tile), tile)
                pre = dot(rows[block, :], vei[0, :, at])
                up = dot(rows[block, :], vei[1, :, at])
                d_act = dot_nt(drows[block, :], veo[at, :])
                s = sigmoid(pre)
                gs = pre * s
                act[block, at] = (gs * up).astype(bf16)
                dgu[0, block, at] = (d_act * up * (s + gs * (1.0 - s))).astype(bf16)
                dgu[1, block, at] = (d_act * gs).astype(bf16)
                return carry

            lax.fori_loop(0, tiles, unit_step, 0)
            dx = dot_nt(dgu[0, block, :], vei[0]) + dot_nt(dgu[1, block, :], vei[1])
            for k in range(c * per, (c + 1) * per):
                if k >= near:
                    cot_half(k).wait_send()
                elif k > 0:
                    cot_copy(k).wait_send()
            csend[block, :] = dx.astype(bf16)
            if c > 0:
                dx_copy(c).start()
                return
            for k in range(c * per, (c + 1) * per):
                if k > 0:
                    ret_copy(k).start()
                else:
                    near_ret[0:C, :] = csend[0:C, :]

        weights[0].wait()
        weights[1].wait()
        lax.fori_loop(0, tiles, shared_step, 0)
        dnsh[...] = (dot_nt(dgu[0, mid, :], vsi[0]) + dot_nt(dgu[1, mid, :], vsi[1])).astype(bf16)
        weights[2].wait()
        weights[3].wait()
        vsi[0, :, 0:T] = normed[...].T
        vsi[1, :, 0:T] = cot[...].T
        shp[...] = dot(act[mid, :], vso[...]).astype(bf16)
        expert_chunk(0)
        for k in range(G - 1, G - 5, -1):
            hand_on(k)
        shared_grads(0)
        expert_chunk(3)
        for k in range(G - 5, G - 7, -1):
            hand_on(k)
        shared_grads(1)
        for k in range(G - 7, near - 1, -1):
            hand_on(k)
        shared_grads(2)
        return_chunk(3)

        expert_chunk(2)
        expert_chunk(1)
        for k in range(1, per):
            ret_copy(k).wait_recv()
        dnsh[...] = (dnsh[...].astype(f32) + dot_tn(plan[0:M, :], near_ret[...])).astype(bf16)
        dnsh_copy.start()
        return_chunk(2)

        def part_chunk(c):
            if c > 0:
                dx_copy(c).wait_send()
            else:
                for k in range(1, per):
                    ret_copy(k).wait_send()
            csend[chunk_at(c), :] = dot(act[chunk_at(c), :], veo[...]).astype(bf16)

        part_chunk(0)
        near_ro[0:C, :] = csend[0:C, :]
        part_chunk(3)
        return_chunk(1)
        part_copy(3).start()
        part_chunk(2)
        part_chunk(1)
        for k in range(1, near):
            po_copy(k).start()
        sides = [slice(0, S // 2), slice(S // 2, S)]
        for n in range(2):
            vsi[n, :, 0 : S // 2] = rows[sides[n], :].T

        def gein_copy(i):
            return pltpu.make_async_copy(
                tall.at[lax.rem(i, 2)], gein.at[i // tiles, :, :, :, :, tile_at(lax.rem(i, tiles))],
                osem.at[lax.rem(i, 2)],
            )

        def gein_step(i, carry):
            @pl.when(i > 1)
            def _():
                gein_copy(i - 2).wait()

            at = tile_at(lax.rem(i, tiles))
            grad = dot(vsi[0, :, 0 : S // 2], dgu[i // tiles, sides[0], at])
            grad = grad + dot(vsi[1, :, 0 : S // 2], dgu[i // tiles, sides[1], at])
            tall[lax.rem(i, 2)] = grad.astype(bf16).reshape(tall.shape[1:])
            gein_copy(i).start()
            return carry

        first = 2
        lax.fori_loop(0, first, gein_step, 0)
        for k in range(near, G):
            row_pass(k).wait_send()

        dnsh_copy.wait()
        total = dnsh[:, mine].astype(f32) + dnsh_r[...].astype(f32)
        for k in range(per, G):
            ret_half(k).wait_recv()
        total = total + dot_tn(plan[M:S, :], ret[...])
        dnb[:, mine] = total.astype(bf16)
        dnb_copy.start()
        part_copy(2).start()
        for p in range(3):
            fold_on(p)
        lax.fori_loop(first, 2 * tiles, gein_step, 0)
        return_part(3)

        def geout_copy(i):
            return pltpu.make_async_copy(
                wide.at[lax.rem(i, 2)], geout.at[tile_at(i), :], osem.at[2 + lax.rem(i, 2)]
            )

        def geout_step(i, carry):
            @pl.when(i > 1)
            def _():
                geout_copy(i - 2).wait()

            wide[lax.rem(i, 2)] = dot_tn(act[:, tile_at(i)], drows[...]).astype(bf16)
            geout_copy(i).start()
            return carry

        lax.fori_loop(0, tiles, geout_step, 0)
        gein_copy(2 * tiles - 2).wait()
        gein_copy(2 * tiles - 1).wait()
        geout_copy(tiles - 2).wait()
        geout_copy(tiles - 1).wait()

    pl.run_scoped(
        experts,
        pltpu.VMEM((2, D, F), bf16),
        pltpu.VMEM((F, D), bf16),
        pltpu.VMEM((2, D, F), bf16),
        pltpu.VMEM((F, D), bf16),
        pltpu.VMEM((S, F), bf16),
        pltpu.VMEM((2, S, F), bf16),
        pltpu.VMEM((T, D), bf16),
        pltpu.VMEM((2, zs, 2, 2, share, tile), bf16),
        pltpu.VMEM((2, tile, D), bf16),
    )

    def attention_back(dres, dresb, da, dqkv, turned, turned2, pay, gated, dna, gtok, w1, w2):
        dna_copy = send(dna, dnar, s_x.at[10], r_x.at[10], partner)
        turned[...] = normed_a[...].T
        dnb_copy.wait()

        def gated_rows(c):
            for k in range(c * per, (c + 1) * per):
                gated[(k - c * per) * C : (k - c * per + 1) * C, :] = (
                    plan[row_at(k), :].astype(f32) * gate[pl.ds(peer(k), 1), :]
                ).astype(bf16)
            return gated[...]

        def dres_step(i, carry):
            at = pl.ds(pl.multiple_of(i * FOLD, FOLD), FOLD)
            y_ = dnb[at, :].astype(f32)
            x = resid[at, :]
            r = lax.rsqrt(jnp.mean(x * x, axis=1, keepdims=True) + epsilon)
            a = y_ * nf[...].reshape(1, D)
            inner = jnp.mean(a * x, axis=1, keepdims=True)
            xr = x * r
            value = cot[at, :].astype(f32) + r * a - xr * (r * r * inner)
            dres[at, :] = value
            dresb[at, :] = value.astype(bf16)
            return carry + jnp.sum(y_ * xr, axis=0, keepdims=True)

        gnf = lax.fori_loop(0, T // FOLD, dres_step, jnp.zeros((1, D), f32))
        da[...] = dot_nt(dresb[...], wo[...]).astype(bf16)
        turned2[...] = dresb[...].T
        pay[:, :, :, :, 0:HL] = dot(turned2[...], att_own[...]).astype(bf16).reshape(zs, 2, 2, share, HL)

        def pay_core(p):
            return send(
                pay.at[:, :, 1 - core, :, columns(p)], a2.at[:, :, :, columns(p)], s_x.at[8 + p], r_x.at[8 + p],
                sibling,
            )

        def pay_on(p):
            pay_core(p).wait()

            def body(n, carry):
                u, v = n // 2, lax.rem(n, 2)
                a2[u, v, :, columns(p)] = (
                    a2[u, v, :, columns(p)].astype(f32) + pay[u, v, core, :, columns(p)].astype(f32)
                ).astype(bf16)
                return carry

            lax.fori_loop(0, 2 * zs, body, 0)
            fold_y(p).start()

        pay_core(3).start()

        def attend_back(j, carry):
            at = pl.ds(pl.multiple_of(j * 128, 128), 128)
            q, k, v, g = qkv[0, :, at], qkv[1, :, at], qkv[2, :, at], da[:, at]
            none = jnp.zeros_like(q)
            dq = dk = dv = jnp.zeros((T, 128), f32)
            for i in range(2):
                inside = (lane < HD) if i == 0 else (lane >= HD)
                qi, ki, gi = (jnp.where(inside, x, none) for x in (q, k, g))
                total = jnp.sum(jnp.where(lane == 2 * j + i, lse[...], 0.0), axis=1, keepdims=True)
                p = jnp.exp(dot_nt(qi, k) * scale + bias[...] - total)
                dp = dot_nt(gi, v)
                inner = jnp.sum(dp * p, axis=1, keepdims=True)
                ds = (p * (dp - inner)).astype(bf16)
                dv = dv + dot_tn(p.astype(bf16), gi)
                dq = dq + dot(ds, ki)
                dk = dk + dot_tn(ds, qi)
            dq, dk = dq * scale, dk * scale
            dqkv[0, :, at] = (dq * cos[...] - swap_halves(dq) * sin[...]).astype(bf16)
            dqkv[1, :, at] = (dk * cos[...] - swap_halves(dk) * sin[...]).astype(bf16)
            dqkv[2, :, at] = dv.astype(bf16)
            return carry

        lax.fori_loop(0, HL // 128, attend_back, 0)
        pay_on(3)

        dna[...] = (
            dot_nt(dqkv[0], wqkv[0]) + dot_nt(dqkv[1], wqkv[1]) + dot_nt(dqkv[2], wqkv[2])
        ).astype(bf16)

        def gain_step(i, carry):
            at = pl.ds(pl.multiple_of(i * FOLD, FOLD), FOLD)
            x = tok[at, :].astype(f32)
            r = lax.rsqrt(jnp.mean(x * x, axis=1, keepdims=True) + epsilon)
            return carry + jnp.sum(dna[at, :].astype(f32) * x * r, axis=0, keepdims=True)

        gna[...] = jnp.broadcast_to(
            lax.fori_loop(0, T // FOLD, gain_step, jnp.zeros((1, D), f32)), gna.shape
        )
        gna_copy.start()
        dna_copy.start()
        return_part(2)
        mixed = shp[...].astype(f32)
        for c in range(near // per):
            for k in range(max(1, c * per), (c + 1) * per):
                po_copy(k).wait_recv()
            mixed = mixed + dot_tn(gated_rows(c), near_ro[chunk_at(c), :])
        shp[...] = mixed.astype(bf16)
        shp_copy.start()
        for s in range(3):
            pay[:, :, :, :, (s + 1) * HL : (s + 2) * HL] = (
                dot(turned[...], dqkv[s]).astype(bf16).reshape(zs, 2, 2, share, HL)
            )
        gna_copy.wait()
        row = lax.broadcasted_iota(jnp.int32, (128, D), 0)
        gains = jnp.where(row == 0, gnf, jnp.where(row == 1, gna[0:1, :] + gnar[0:1, :], 0.0))
        pay[:, :, :, :, 4 * HL :] = gains.T.astype(bf16).reshape(zs, 2, 2, share, 128)
        pay_core(4).start()
        fold_on(3)
        pay_on(4)
        for p in range(3):
            fold_end(p, w1)
        fold_on(4)

        shp_copy.wait()
        mixed = shp[:, mine].astype(f32) + shpr[...].astype(f32)
        for c in range(near // per, chunks):
            for k in range(c * per, (c + 1) * per):
                po_half(k).wait_recv()
            mixed = mixed + dot_tn(gated_rows(c), ro[out_chunk(c), :])
        ob[:, mine] = (resid[:, mine] + mixed).astype(bf16)
        out_copy.start()
        dna_copy.wait()

        def last_step(i, carry):
            at = pl.ds(pl.multiple_of(i * FOLD, FOLD), FOLD)
            x = tok[at, :].astype(f32)
            r = lax.rsqrt(jnp.mean(x * x, axis=1, keepdims=True) + epsilon)
            a = (dna[at, :].astype(f32) + dnar[at, :].astype(f32)) * na[...].reshape(1, D)
            inner = jnp.mean(a * x, axis=1, keepdims=True)
            gtok[at, :] = (dres[at, :] + r * a - x * (r * r * r * inner)).astype(bf16)
            return carry

        lax.fori_loop(0, T // FOLD, last_step, 0)
        fold_end(3, w2)
        fold_end(4, w2)
        ends = [
            pltpu.make_async_copy(a, b, osem.at[i])
            for i, (a, b) in enumerate(((gtok, h_gtok), (w1, h_gw1), (w2, h_gw2), (ob, h_out)))
        ]
        for c in ends[:3]:
            c.start()
        out_copy.wait()
        ends[3].start()
        for c in ends:
            c.wait()

    pl.run_scoped(
        attention_back,
        pltpu.VMEM((T, D), f32),
        pltpu.VMEM((T, D), bf16),
        pltpu.VMEM((T, HL), bf16),
        pltpu.VMEM((3, T, HL), bf16),
        pltpu.VMEM((D, T), bf16),
        pltpu.VMEM((D, T), bf16),
        pltpu.VMEM((zs, 2, 2, share, W2), bf16),
        pltpu.VMEM((M, T), bf16),
        pltpu.VMEM((T, D), bf16),
        pltpu.VMEM((T, D), bf16),
        pltpu.VMEM((share, 3 * F), f32),
        pltpu.VMEM((share, W2), f32),
    )
    for k in range(near, G):
        cot_pass(k).wait_send()
        po_half(k).wait_send()
    for k in range(1, near):
        row_copy(k).wait_send()
        po_copy(k).wait_send()
    for k in range(per, near):
        ret_half(k).wait_send()
    for c in range(near // per, chunks):
        part_copy(c).wait_send()


def finish_kernel(
    HL, F, h_out, h_gtok, h_gw1, h_gw2, h_gein, h_geout,
    out, gtok, gqkv, gao, gna, gnf, gsi, gso, gein, geout,
):
    out[...] = h_out[...]
    gtok[...] = h_gtok[...]
    gein[...] = h_gein[...].astype(f32)
    geout[...] = h_geout[...].astype(f32)

    @pl.when(pl.program_id(0) == 0)
    def _():
        for s in range(3):
            gqkv[s] = h_gw2[:, (s + 1) * HL : (s + 2) * HL]
        gao[...] = h_gw2[:, 0:HL]
        gains = h_gw2[:, 4 * HL :].T
        gnf[...] = gains[0:1, :]
        gna[...] = gains[1:2, :]
        for s in range(2):
            gsi[s] = h_gw1[:, s * F : (s + 1) * F]
        gso[...] = h_gw1[:, 2 * F :]


def fused(
    tokens, cont_lengths, routes, route_gates, w_qkv, w_attn_out, norm_attn, norm_ffn,
    shared_in, shared_out, expert_in, expert_out, cotangent,
):
    T, D = tokens.shape
    G = lax.axis_size("dp")
    HL, F = w_qkv.shape[2], shared_in.shape[2]
    C = round_up(CAP, 16)
    S = G * C
    half, share, zs = D // 2, D // G, G // 4
    W1, W2 = 3 * F, 4 * HL + 128
    shape = jax.ShapeDtypeStruct
    dma = pltpu.SemaphoreType.DMA
    SM = pl.BlockSpec(memory_space=pltpu.SMEM)
    out, gtok, gw1, gw2, gein, geout = pl.pallas_call(
        functools.partial(layer_kernel, G),
        out_shape=(
            shape((T, D), bf16), shape((T, D), bf16), shape((share, W1), f32), shape((share, W2), f32),
            shape((2, zs, 2, 2, share, F), bf16), shape((F, D), bf16),
        ),
        in_specs=[VM] * 2 + [SM] + [VM] * 2 + [ANY] * 8,
        out_specs=(ANY,) * 6,
        scratch_shapes=[
            pltpu.VMEM((T, D), bf16),
            pltpu.VMEM((3, D, HL), bf16),
            pltpu.VMEM((HL, D), bf16),
            pltpu.VMEM((T, D), bf16),
            pltpu.VMEM((T, 128), f32),
            pltpu.VMEM((T, 128), f32),
            pltpu.VMEM((3, T, HL), bf16),
            pltpu.VMEM((T, 128), f32),
            pltpu.VMEM((T, HL), bf16),
            pltpu.VMEM((T, D), bf16),
            pltpu.VMEM((T, D), f32),
            pltpu.VMEM((S, T), bf16),
            pltpu.VMEM((EXPERTS, T), f32),
            pltpu.VMEM((EXPERTS, T), f32),
            pltpu.VMEM((T, T), f32),
            pltpu.VMEM((T, HL), bf16),
            pltpu.VMEM((HL, D), bf16),
            pltpu.VMEM((S, D), bf16),
            pltpu.VMEM((S, D), bf16),
            pltpu.VMEM((S, D), bf16),
            pltpu.VMEM((S // 2, D), bf16),
            pltpu.VMEM((S - 4 * C, half), bf16),
            pltpu.VMEM((4 * C, D), bf16),
            pltpu.VMEM((S - 4 * C, half), bf16),
            pltpu.VMEM((S - 4 * C, half), bf16),
            pltpu.VMEM((T, D), bf16),
            pltpu.VMEM((T, half), bf16),
            pltpu.VMEM((T, D), bf16),
            pltpu.VMEM((T, D), bf16),
            pltpu.VMEM((S // 2, half), bf16),
            pltpu.VMEM((S // 2, D), bf16),
            pltpu.VMEM((S // 2, half), bf16),
            pltpu.VMEM((T, half), bf16),
            pltpu.VMEM((8, D), f32),
            pltpu.VMEM((8, D), f32),
            *[
                pltpu.VMEM((*dims, share, width), bf16)
                for width in (W1, W2)
                for dims in ((zs, 2), (zs,), (zs - 1,))
            ],
            dma((13,)), dma((13,)), *[dma((G,))] * 8, dma((4,)), dma((4,)), dma((G,)), dma((G,)),
            dma((4,)), dma((4,)), dma((G,)), dma((G,)), dma((12,)), dma((12,)), dma((5,)), dma((5,)),
            dma((5, zs - 1)), dma((5, zs - 1)), dma((8,)), dma((4,)),
        ],
        compiler_params=pltpu.CompilerParams(
            collective_id=0, has_side_effects=True, vmem_limit_bytes=VMEM_BYTES
        ),
        name="layer",
    )(
        norm_attn, norm_ffn, cont_lengths, routes.T, route_gates.T, tokens, w_qkv, w_attn_out, cotangent,
        shared_in, shared_out, expert_in, expert_out,
    )
    steps = 4

    def rows_of(*dims):
        return pl.BlockSpec(dims, lambda i: (0,) * (len(dims) - 2) + (i, 0))

    def whole(*dims):
        return pl.BlockSpec(dims, lambda i: (0,) * len(dims))

    results = ((3, share, HL), (share, HL), (1, share), (1, share), (2, share, F), (share, F))
    out, gtok, gqkv, gao, gna, gnf, gsi, gso, gein, geout = pl.pallas_call(
        functools.partial(finish_kernel, HL, F),
        grid=(steps,),
        out_shape=(
            shape((T, D), bf16), shape((T, D), bf16), *[shape(r, f32) for r in results],
            shape((2, D, F), f32), shape((F, D), f32),
        ),
        in_specs=[
            rows_of(T // steps, D), rows_of(T // steps, D), whole(share, W1), whole(share, W2),
            rows_of(2, D // steps, F), rows_of(F // steps, D),
        ],
        out_specs=(
            rows_of(T // steps, D), rows_of(T // steps, D), *[whole(*r) for r in results],
            rows_of(2, D // steps, F), rows_of(F // steps, D),
        ),
        compiler_params=pltpu.CompilerParams(vmem_limit_bytes=VMEM_BYTES),
        name="finish",
    )(out, gtok, gw1, gw2, gein.reshape(2, D, F), geout)
    return (out, gtok, gqkv, gao.T, gna[0], gnf[0], gsi, gso.T, gein, geout)


def solution(mesh):
    placed = (
        P("dp", None),
        P("dp", None),
        P("dp", None),
        P("dp", None),
        P(None, None, "tensor"),
        P("tensor", None),
        P(),
        P(),
        P(None, None, "tensor"),
        P("tensor", None),
        P(None, None, ("dp", "tensor")),
        P(("dp", "tensor"), None),
        P("dp", None),
    )
    return jax.shard_map(
        fused if mesh.shape["dp"] == EXPERTS else local,
        mesh=mesh,
        in_specs=placed,
        out_specs=(
            P("dp", None),
            P("dp", None),
            P(None, "dp", "tensor"),
            P("tensor", "dp"),
            P("dp"),
            P("dp"),
            P(None, "dp", "tensor"),
            P("tensor", "dp"),
            P(None, None, ("dp", "tensor")),
            P(("dp", "tensor"), None),
        ),
        check_vma=False,
    )
```

```python
import functools
import math

import jax
import jax.numpy as jnp
from jax import lax
from jax.experimental import pallas as pl
from jax.experimental.pallas import tpu as pltpu
from jax.sharding import PartitionSpec as P

HD = 64
EXPERTS = 16
TOP = 2
PROMPT = 64
CAP = 92


epsilon = 1e-06


def rms_parts(values, gain):
    factor = lax.rsqrt(jnp.mean(values * values, axis=-1, keepdims=True) + epsilon)
    return (values * factor * gain, factor)


def rms_back(values, factor, gain, incoming):
    weighted = incoming * gain
    inner = jnp.mean(weighted * values, axis=-1, keepdims=True)
    return (
        factor * weighted - values * factor * factor * factor * inner,
        jnp.sum(incoming * values * factor, axis=0),
    )


def silu_act(values):
    return values * jax.nn.sigmoid(values)


def swiglu_back(gate_up, d_act):
    sigma = jax.nn.sigmoid(gate_up[0])
    d_gate = d_act * gate_up[1] * sigma * (1.0 + gate_up[0] * (1.0 - sigma))
    d_upper = d_act * gate_up[0] * sigma
    return jnp.stack([d_gate, d_upper]).astype(jnp.bfloat16)


def group_layout(lengths, rows_here):
    row_index = jnp.arange(rows_here, dtype=jnp.int32)
    cont_ends = PROMPT + jnp.cumsum(lengths, dtype=jnp.int32)
    begins = cont_ends - lengths
    later = jnp.sum(
        (row_index[:, None] >= cont_ends[None, :]).astype(jnp.int32), axis=1, dtype=jnp.int32
    )
    segment = jnp.where(row_index < PROMPT, 0, 1 + later)
    member = (
        segment[:, None] == jnp.arange(1, lengths.shape[0] + 1, dtype=jnp.int32)[None, :]
    ).astype(jnp.int32)
    offset = jnp.sum(member * begins[None, :], axis=1, dtype=jnp.int32)
    position = jnp.where(segment == 0, row_index, PROMPT + row_index - offset)
    allowed = (row_index[None, :] <= row_index[:, None]) & (
        (segment[None, :] == 0) | (segment[None, :] == segment[:, None])
    )
    return (position, allowed)


def rope_tables(position):
    half_size = HD // 2
    inv_freq = 10000.0 ** (-jnp.arange(half_size, dtype=jnp.float32) / half_size)
    angles = position.astype(jnp.float32)[:, None] * inv_freq[None, :]
    return (jnp.cos(angles)[:, None, :], jnp.sin(angles)[:, None, :])


def rotate_pairs(values, cosine, sine):
    half_size = values.shape[-1] // 2
    front_half = values[..., :half_size]
    back_half = values[..., half_size:]
    return jnp.concatenate(
        [front_half * cosine - back_half * sine, front_half * sine + back_half * cosine], axis=-1
    )


def dispatch_plan(routes):
    flat_routes = routes.reshape(-1)
    one_hot = (flat_routes[:, None] == jnp.arange(EXPERTS, dtype=jnp.int32)[None, :]).astype(
        jnp.int32
    )
    earlier = jnp.cumsum(one_hot, axis=0, dtype=jnp.int32) - one_hot
    place_in = jnp.sum(earlier * one_hot, axis=1, dtype=jnp.int32)
    target = flat_routes * CAP + place_in
    pair_count = flat_routes.shape[0]
    slot_table = (
        jnp.full((EXPERTS * CAP,), pair_count, jnp.int32)
        .at[target]
        .set(jnp.arange(pair_count, dtype=jnp.int32))
    )
    return (target, slot_table)


def spread_rows(padded, indices, copies):
    model_width = padded.shape[1]
    picked = jnp.take(padded, indices, axis=0).reshape(EXPERTS, 1, CAP, model_width)
    return jnp.broadcast_to(picked, (EXPERTS, copies, CAP, model_width)).reshape(
        EXPERTS * copies, CAP, model_width
    )


def collect_rows(returned, target, copies, rows_here):
    model_width = returned.shape[2]
    summed = jnp.sum(returned.reshape(EXPERTS, copies, CAP, model_width), axis=1, dtype=jnp.float32)
    summed = summed.reshape(EXPERTS * CAP, model_width)
    return jnp.take(summed, target, axis=0).reshape(rows_here, TOP, model_width)


def local(
    tokens,
    cont_lengths,
    routes,
    route_gates,
    w_qkv,
    w_attn_out,
    norm_attn,
    norm_ffn,
    shared_in,
    shared_out,
    expert_in,
    expert_out,
    cotangent,
):
    rows_here = tokens.shape[0]
    model_width = tokens.shape[1]
    groups = lax.axis_size("dp")
    copies = groups // EXPERTS
    head_count = w_qkv.shape[2] // HD
    score_scale = HD ** (-0.5)
    inputs = tokens.astype(jnp.float32)
    position, allowed = group_layout(cont_lengths[0], rows_here)
    cosine, sine = rope_tables(position)
    normed_a, factor_a = rms_parts(inputs, norm_attn)
    normed_attn = normed_a.astype(jnp.bfloat16)
    projected = jnp.einsum("td,sdf->stf", normed_attn, w_qkv, preferred_element_type=jnp.float32)
    query = rotate_pairs(projected[0].reshape(rows_here, head_count, HD), cosine, sine).astype(
        jnp.bfloat16
    )
    key_rows = rotate_pairs(projected[1].reshape(rows_here, head_count, HD), cosine, sine).astype(
        jnp.bfloat16
    )
    value_rows = projected[2].reshape(rows_here, head_count, HD).astype(jnp.bfloat16)
    score = (
        jnp.einsum("qhd,khd->hqk", query, key_rows, preferred_element_type=jnp.float32)
        * score_scale
    )
    score = jnp.where(allowed[None], score, -1000000000.0)
    row_max = jnp.max(score, axis=-1, keepdims=True)
    exponent = jnp.exp(score - row_max)
    row_total = jnp.sum(exponent, axis=-1, keepdims=True)
    log_total = row_max + jnp.log(row_total)
    weights_b = (exponent / row_total).astype(jnp.bfloat16)
    attended = jnp.einsum("hqk,khd->qhd", weights_b, value_rows, preferred_element_type=jnp.float32)
    attended = attended.reshape(rows_here, head_count * HD).astype(jnp.bfloat16)
    attn_part = jnp.dot(attended, w_attn_out, preferred_element_type=jnp.float32)
    resid = inputs + lax.psum(attn_part.astype(jnp.bfloat16), "tensor").astype(jnp.float32)
    normed_f, factor_f = rms_parts(resid, norm_ffn)
    normed_ffn = normed_f.astype(jnp.bfloat16)
    gate_up = jnp.einsum("td,sdf->stf", normed_ffn, shared_in, preferred_element_type=jnp.float32)
    shared_act = (silu_act(gate_up[0]) * gate_up[1]).astype(jnp.bfloat16)
    shared_part = jnp.dot(shared_act, shared_out, preferred_element_type=jnp.float32)
    target, slot_table = dispatch_plan(routes)
    padded_rows = jnp.concatenate([normed_ffn, jnp.zeros((1, model_width), jnp.bfloat16)], axis=0)
    send_rows = spread_rows(padded_rows, slot_table // TOP, copies)
    arrived = lax.all_to_all(send_rows, "dp", split_axis=0, concat_axis=0, tiled=True)
    expert_input = arrived.reshape(groups * CAP, model_width)
    expert_gu = jnp.einsum(
        "rd,sdf->srf", expert_input, expert_in, preferred_element_type=jnp.float32
    )
    expert_act = (silu_act(expert_gu[0]) * expert_gu[1]).astype(jnp.bfloat16)
    expert_part = jnp.dot(expert_act, expert_out, preferred_element_type=jnp.float32).astype(
        jnp.bfloat16
    )
    returned = lax.all_to_all(
        expert_part.reshape(groups, CAP, model_width), "dp", split_axis=0, concat_axis=0, tiled=True
    )
    picked = collect_rows(returned, target, copies, rows_here)
    mixed = jnp.sum(route_gates[:, :, None] * picked, axis=1)
    ffn_total = lax.psum((shared_part + mixed).astype(jnp.bfloat16), "tensor").astype(jnp.float32)
    output = (resid + ffn_total).astype(jnp.bfloat16)
    upstream = cotangent.astype(jnp.float32)
    d_shared_act = jnp.einsum(
        "td,fd->tf", cotangent, shared_out, preferred_element_type=jnp.float32
    )
    d_shared_gu = swiglu_back(gate_up, d_shared_act)
    d_normed = jnp.einsum("stf,sdf->td", d_shared_gu, shared_in, preferred_element_type=jnp.float32)
    g_shared_in = jnp.einsum(
        "td,stf->sdf", normed_ffn, d_shared_gu, preferred_element_type=jnp.float32
    )
    g_shared_out = jnp.einsum(
        "tf,td->fd", shared_act, cotangent, preferred_element_type=jnp.float32
    )
    pair_grad = (
        (route_gates[:, :, None] * upstream[:, None, :])
        .reshape(rows_here * TOP, model_width)
        .astype(jnp.bfloat16)
    )
    padded_grad = jnp.concatenate([pair_grad, jnp.zeros((1, model_width), jnp.bfloat16)], axis=0)
    send_grad = spread_rows(padded_grad, slot_table, copies)
    again_rows = spread_rows(padded_rows, slot_table // TOP, copies)
    grad_arrived, rows_arrived = (
        lax.all_to_all(send_grad, "dp", split_axis=0, concat_axis=0, tiled=True),
        lax.all_to_all(again_rows, "dp", split_axis=0, concat_axis=0, tiled=True),
    )
    rows_back = rows_arrived.reshape(groups * CAP, model_width)
    d_expert_rows = grad_arrived.reshape(groups * CAP, model_width)
    back_gu = jnp.einsum("rd,sdf->srf", rows_back, expert_in, preferred_element_type=jnp.float32)
    back_act = (silu_act(back_gu[0]) * back_gu[1]).astype(jnp.bfloat16)
    d_expert_act = jnp.einsum(
        "rd,fd->rf", d_expert_rows, expert_out, preferred_element_type=jnp.float32
    )
    d_expert_gu = swiglu_back(back_gu, d_expert_act)
    d_expert_in = jnp.einsum(
        "srf,sdf->rd", d_expert_gu, expert_in, preferred_element_type=jnp.float32
    ).astype(jnp.bfloat16)
    g_expert_in = jnp.einsum(
        "rd,srf->sdf", rows_back, d_expert_gu, preferred_element_type=jnp.float32
    )
    g_expert_out = jnp.einsum(
        "rf,rd->fd", back_act, d_expert_rows, preferred_element_type=jnp.float32
    )
    d_returned = lax.all_to_all(
        d_expert_in.reshape(groups, CAP, model_width), "dp", split_axis=0, concat_axis=0, tiled=True
    )
    d_normed = d_normed + jnp.sum(collect_rows(d_returned, target, copies, rows_here), axis=1)
    d_normed = lax.psum(d_normed.astype(jnp.bfloat16), "tensor").astype(jnp.float32)
    d_resid_norm, g_norm_ffn = rms_back(resid, factor_f, norm_ffn, d_normed)
    d_resid = upstream + d_resid_norm
    d_resid_b = d_resid.astype(jnp.bfloat16)
    g_attn_out = jnp.einsum("tf,td->fd", attended, d_resid_b, preferred_element_type=jnp.float32)
    d_attended = jnp.einsum("td,fd->tf", d_resid_b, w_attn_out, preferred_element_type=jnp.float32)
    d_attended = d_attended.astype(jnp.bfloat16).reshape(rows_here, head_count, HD)
    recomputed = (
        jnp.einsum("qhd,khd->hqk", query, key_rows, preferred_element_type=jnp.float32)
        * score_scale
    )
    recomputed = jnp.where(allowed[None], recomputed, -1000000000.0)
    probs = jnp.exp(recomputed - log_total)
    probs_b = probs.astype(jnp.bfloat16)
    d_probs = jnp.einsum("qhd,khd->hqk", d_attended, value_rows, preferred_element_type=jnp.float32)
    d_value = jnp.einsum("hqk,qhd->khd", probs_b, d_attended, preferred_element_type=jnp.float32)
    inner = jnp.sum(d_probs * probs, axis=-1, keepdims=True)
    d_score = (probs * (d_probs - inner)).astype(jnp.bfloat16)
    d_query = (
        jnp.einsum("hqk,khd->qhd", d_score, key_rows, preferred_element_type=jnp.float32)
        * score_scale
    )
    d_key = (
        jnp.einsum("hqk,qhd->khd", d_score, query, preferred_element_type=jnp.float32) * score_scale
    )
    d_query = rotate_pairs(d_query, cosine, -sine).reshape(rows_here, head_count * HD)
    d_key = rotate_pairs(d_key, cosine, -sine).reshape(rows_here, head_count * HD)
    d_qkv = jnp.stack([d_query, d_key, d_value.reshape(rows_here, head_count * HD)]).astype(
        jnp.bfloat16
    )
    g_qkv = jnp.einsum("td,stf->sdf", normed_attn, d_qkv, preferred_element_type=jnp.float32)
    d_normed_attn = jnp.einsum("stf,sdf->td", d_qkv, w_qkv, preferred_element_type=jnp.float32)
    d_normed_attn = lax.psum(d_normed_attn.astype(jnp.bfloat16), "tensor").astype(jnp.float32)
    d_input_norm, g_norm_attn = rms_back(inputs, factor_a, norm_attn, d_normed_attn)
    grad_tokens = (d_resid + d_input_norm).astype(jnp.bfloat16)
    summed_all = (
        lax.psum_scatter(g_qkv, "dp", scatter_dimension=1, tiled=True),
        lax.psum_scatter(g_attn_out, "dp", scatter_dimension=1, tiled=True),
        lax.psum_scatter(g_norm_attn, "dp", scatter_dimension=0, tiled=True),
        lax.psum_scatter(g_shared_in, "dp", scatter_dimension=1, tiled=True),
        lax.psum_scatter(g_shared_out, "dp", scatter_dimension=1, tiled=True),
        lax.psum_scatter(g_norm_ffn, "dp", scatter_dimension=0, tiled=True),
    )
    return (
        output,
        grad_tokens,
        summed_all[0],
        summed_all[1],
        summed_all[2],
        summed_all[5],
        summed_all[3],
        summed_all[4],
        g_expert_in,
        g_expert_out,
    )


VMEM_BYTES = 64000 * 1024
FOLD = 96
NEAR = 8
WHOLE = 4
MESH = pl.DeviceIdType.MESH
VM = pl.BlockSpec(memory_space=pltpu.VMEM)
ANY = pl.BlockSpec(memory_space=pl.ANY)
f32 = jnp.float32
bf16 = jnp.bfloat16


def round_up(value, unit):
    return (value + unit - 1) // unit * unit


def dot(a, b):
    return jnp.dot(a, b, preferred_element_type=f32)


def dot_nt(a, b):
    return lax.dot_general(a, b, (((1,), (1,)), ((), ())), preferred_element_type=f32)


def dot_tn(a, b):
    return lax.dot_general(a, b, (((0,), (0,)), ((), ())), preferred_element_type=f32)


def sigmoid(values):
    return 0.5 * jnp.tanh(0.5 * values) + 0.5


def swap_halves(values):
    lane = lax.broadcasted_iota(jnp.int32, values.shape, 1)
    ahead = pltpu.roll(values, values.shape[1] - HD // 2, 1)
    behind = pltpu.roll(values, HD // 2, 1)
    return jnp.where(lax.rem(lane, HD) < HD // 2, ahead, behind)


def hello(groups):
    me, t = lax.axis_index("dp"), lax.axis_index("tensor")
    barrier = pltpu.get_barrier_semaphore()

    def greet(k, carry):
        pl.semaphore_signal(
            barrier, inc=1, device_id=(lax.rem(me + k, groups), t), device_id_type=MESH
        )
        return carry

    lax.fori_loop(1, groups, greet, 0)
    pl.semaphore_signal(barrier, inc=1, device_id=(me, 1 - t), device_id_type=MESH)
    pl.semaphore_wait(barrier, groups)


def segment_of(index, lens):
    segment = jnp.where(index < PROMPT, 0, 1)
    end = PROMPT
    for c in range(lens.shape[1]):
        end = end + lens[0, c]
        segment = segment + jnp.where(index >= end, 1, 0)
    return segment


def position_of(index, lens):
    segment = segment_of(index, lens)
    position, end = index, PROMPT
    for c in range(lens.shape[1]):
        position = jnp.where(segment == c + 1, PROMPT + index - end, position)
        end = end + lens[0, c]
    return position


def fill_bias(bias, lens, rows):
    step = FOLD

    def body(i, carry):
        at = pl.ds(pl.multiple_of(i * step, step), step)
        row = lax.broadcasted_iota(jnp.int32, (step, rows), 0) + i * step
        col = lax.broadcasted_iota(jnp.int32, (step, rows), 1)
        own = segment_of(lax.broadcasted_iota(jnp.int32, (step, 1), 0) + i * step, lens)
        other = segment_of(lax.broadcasted_iota(jnp.int32, (1, rows), 1), lens)
        ok = (col <= row) & ((other == 0) | (other == own))
        bias[at, :] = jnp.where(ok, 0.0, -1000000000.0)
        return carry

    lax.fori_loop(0, rows // step, body, 0)


def fill_angles(cos, sin, lens, rows):
    step = FOLD

    def body(i, carry):
        at = pl.ds(pl.multiple_of(i * step, step), step)
        lane = lax.broadcasted_iota(jnp.int32, (step, 128), 1)
        row = lax.broadcasted_iota(jnp.int32, (step, 128), 0) + i * step
        power = lax.rem(lane, HD // 2).astype(f32) * (-math.log(10000.0) / (HD // 2))
        angle = position_of(row, lens).astype(f32) * jnp.exp(power)
        cos[at, :] = jnp.cos(angle)
        sine = jnp.sin(angle)
        sin[at, :] = jnp.where(lax.rem(lane, HD) < HD // 2, -sine, sine)
        return carry

    lax.fori_loop(0, rows // step, body, 0)


def send(src, dst, ssem, rsem, to):
    return pltpu.make_async_remote_copy(
        src_ref=src, dst_ref=dst, send_sem=ssem, recv_sem=rsem, device_id=to, device_id_type=MESH
    )


def layer_kernel(
    G, na, nf, lens, rT, gT, h_tok, h_wqkv, h_wo, h_cot, si, so, ei, eo,
    h_out, h_gtok, h_gw1, h_gw2, gein, geout,
    tok, wqkv, wo, cot, cos, sin, qkv, lse, att_own, normed_a, resid, plan, gate, slot, bias, att, wo2,
    csend, drows, rows, near_send, rets, near_ret, ret, dxr, dnsh, dnsh_r, dnb, shp, partr, near_ro, ro, shpr, gna, gnar,
    a1, b1, d1, a2, b2, d2,
    s_x, r_x, s_c, r_c, s_cf, r_cf, s_r, r_r, s_f, r_f, s_dx, r_dx, s_ret, r_ret, s_p, r_p, s_po, r_po,
    s_k, r_k, s_y, r_y, s_z, r_z, lsem, osem,
):
    T, D = tok.shape
    HL = wqkv.shape[2]
    F = si.shape[2]
    S = plan.shape[0]
    C = S // G
    half, share, zs = D // 2, D // G, G // 4
    W2 = a2.shape[3]
    scale = HD ** (-0.5)
    me, t = lax.axis_index("dp"), lax.axis_index("tensor")
    core, y, z = lax.rem(me, 2), lax.rem(me // 2, 2), me // 4
    mine = pl.ds(pl.multiple_of(t * half, 128), half)
    theirs = pl.ds(pl.multiple_of((1 - t) * half, 128), half)
    partner = (me, 1 - t)
    sibling = (me + 1 - 2 * core, t)
    neighbour = (me + 2 - 4 * y, t)
    per, tile = 4, 256
    M, chunks, tiles = per * C, G // per, F // tile

    loads = [
        pltpu.make_async_copy(a, b, lsem.at[i])
        for i, (a, b) in enumerate(((h_cot, cot), (h_tok, tok), (h_wqkv, wqkv), (h_wo, wo)))
    ]
    for c in loads:
        c.start()
    hello(G)
    part_wo = pl.ds(pl.multiple_of(core * (HL // 2), 16), HL // 2)
    wo_copy = send(h_wo.at[part_wo], wo2.at[part_wo], s_x.at[0], r_x.at[0], partner)
    wo_copy.start()
    wo_pass = send(wo2.at[part_wo], wo2.at[part_wo], s_x.at[6], r_x.at[6], sibling)

    def row_at(k):
        return pl.ds(pl.multiple_of(k * C, C), C)

    def chunk_at(c):
        return pl.ds(c * M, M)

    near = NEAR
    whole = WHOLE

    def peer(k):
        to, weight = me, 1
        while weight < G:
            bit = lax.rem(k // weight, 2)
            to = to + weight * bit * (1 - 2 * lax.rem(me // weight, 2))
            weight = weight * 2
        return to

    def far_at(k):
        return pl.ds(pl.multiple_of((k - per) * C, C), C)

    def out_at(k):
        return pl.ds(pl.multiple_of((k - whole) * C, C), C)

    def far_chunk(c):
        return pl.ds((c - 1) * M, M)

    def out_chunk(c):
        return pl.ds((c - whole // per) * M, M)

    names = lax.broadcasted_iota(jnp.int32, (EXPERTS, T), 0)
    picks0, picks1 = rT[0:1, :] == names, rT[1:2, :] == names
    member = jnp.where(picks0 | picks1, 1.0, 0.0)
    upper = jnp.where(
        lax.broadcasted_iota(jnp.int32, (T, T), 0) < lax.broadcasted_iota(jnp.int32, (T, T), 1),
        1.0,
        0.0,
    ).astype(bf16)
    slot[...] = jnp.where(member > 0.0, dot(member.astype(bf16), upper), -1.0)
    gate[...] = jnp.where(picks0, gT[0:1, :], 0.0) + jnp.where(picks1, gT[1:2, :], 0.0)

    def cot_copy(k):
        return send(csend.at[row_at(k)], drows.at[row_at(k)], s_c.at[k], r_c.at[k], (peer(k), t))

    def cot_half(k):
        return send(
            csend.at[row_at(k), mine], drows.at[row_at(k), mine], s_c.at[k], r_c.at[k], (peer(k), t)
        )

    def cot_pass(k):
        return send(
            drows.at[row_at(k), mine], drows.at[row_at(k), mine], s_cf.at[k], r_cf.at[k], partner
        )

    def cot_hand_on(k):
        cot_half(k).wait_recv()
        cot_pass(k).start()

    def cot_step(i, carry):
        k = G - 1 - i
        e = peer(k)
        at = row_at(k)
        place = lax.broadcasted_iota(jnp.int32, (C, T), 0).astype(f32)
        hit = slot[pl.ds(e, 1), :] == place
        picked = jnp.where(hit, 1.0, 0.0).astype(bf16)
        plan[at, :] = picked
        weight = jnp.sum(jnp.where(hit, gate[pl.ds(e, 1), :], 0.0), axis=1, keepdims=True)
        grad = (dot(picked, cot[...]) * weight).astype(bf16)
        csend[at, :] = grad

        @pl.when(k >= near)
        def _():
            cot_half(k).start()

        @pl.when((k > 0) & (k < near))
        def _():
            cot_copy(k).start()

        @pl.when(k == 0)
        def _():
            drows[at, :] = grad

        return carry

    loads[0].wait()
    lax.fori_loop(0, G, cot_step, 0)

    fill_angles(cos, sin, lens, T)
    fill_bias(bias, lens, T)
    loads[1].wait()

    def norm_step(i, carry):
        at = pl.ds(pl.multiple_of(i * FOLD, FOLD), FOLD)
        x = tok[at, :].astype(f32)
        r = lax.rsqrt(jnp.mean(x * x, axis=1, keepdims=True) + epsilon)
        normed_a[at, :] = (x * r * na[...].reshape(1, D)).astype(bf16)
        return carry

    lax.fori_loop(0, T // FOLD, norm_step, 0)
    loads[2].wait()
    loads[3].wait()

    def project(s, turned):
        full = dot(normed_a[...], wqkv[s])
        for j in range(HL // 128):
            x = full[:, j * 128 : (j + 1) * 128]
            if turned:
                x = x * cos[...] + swap_halves(x) * sin[...]
            qkv[s, :, j * 128 : (j + 1) * 128] = x.astype(bf16)

    project(0, True)
    project(1, True)
    project(2, False)
    lane = lax.broadcasted_iota(jnp.int32, (T, 128), 1)

    def att_copy(j):
        at = pl.ds(pl.multiple_of(j * 128, 128), 128)
        return send(att_own.at[:, at], att.at[:, at], s_x.at[1 + j], r_x.at[1 + j], partner)

    lse[...] = jnp.zeros_like(lse)

    def attend(j, carry):
        at = pl.ds(pl.multiple_of(j * 128, 128), 128)
        q, k, v = qkv[0, :, at], qkv[1, :, at], qkv[2, :, at]
        outs = []
        for i in range(2):
            inside = (lane < HD) if i == 0 else (lane >= HD)
            s = dot_nt(jnp.where(inside, q, jnp.zeros_like(q)), k) * scale + bias[...]
            top = jnp.max(s, axis=1, keepdims=True)
            e = jnp.exp(s - top)
            total = jnp.sum(e, axis=1, keepdims=True)
            p = (e * (1.0 / total)).astype(bf16)
            lse[...] = jnp.where(lane == 2 * j + i, top + jnp.log(total), lse[...])
            outs.append(dot(p, v))
        att_own[:, at] = jnp.where(lane < HD, outs[0], outs[1]).astype(bf16)
        att_copy(j).start()
        return carry

    wo_copy.wait()
    wo_pass.start()
    lax.fori_loop(0, HL // 128, attend, 0)
    own_out = dot(att_own[...], wo[...])
    wo_pass.wait()
    for j in range(HL // 128):
        att_copy(j).wait()
    resid[...] = tok[...].astype(f32) + own_out + dot(att[...], wo2[...])

    def row_copy(k):
        return send(near_send.at[row_at(k)], rows.at[row_at(k)], s_r.at[k], r_r.at[k], (peer(k), t))

    def row_half(k):
        return send(rets.at[far_at(k)], rows.at[row_at(k), mine], s_r.at[k], r_r.at[k], (peer(k), t))

    def row_pass(k):
        return send(
            rows.at[row_at(k), mine], rows.at[row_at(k), mine], s_f.at[k], r_f.at[k], partner
        )

    def hand_on(k):
        row_half(k).wait_recv()
        row_pass(k).start()

    def dx_copy(c):
        return send(csend.at[chunk_at(c), theirs], dxr.at[far_chunk(c)], s_dx.at[c], r_dx.at[c], partner)

    def ret_copy(k):
        return send(csend.at[row_at(k)], near_ret.at[row_at(k)], s_ret.at[k], r_ret.at[k], (peer(k), t))

    def ret_half(k):
        return send(rets.at[far_at(k)], ret.at[far_at(k)], s_ret.at[k], r_ret.at[k], (peer(k), t))

    def return_chunk(c):
        dx_copy(c).wait_recv()
        total = (csend[chunk_at(c), mine].astype(f32) + dxr[far_chunk(c), :].astype(f32)).astype(bf16)
        for k in range(c * per, (c + 1) * per):
            if k >= near:
                row_half(k).wait_send()
        rets[far_chunk(c), :] = total
        for k in range(c * per, (c + 1) * per):
            ret_half(k).start()

    def part_copy(c):
        return send(csend.at[chunk_at(c), theirs], partr.at[out_chunk(c)], s_p.at[c], r_p.at[c], partner)

    def po_copy(k):
        return send(csend.at[row_at(k)], near_ro.at[row_at(k)], s_po.at[k], r_po.at[k], (peer(k), t))

    def po_half(k):
        return send(rets.at[far_at(k)], ro.at[out_at(k)], s_po.at[k], r_po.at[k], (peer(k), t))

    def return_part(c):
        part_copy(c).wait_recv()
        total = (csend[chunk_at(c), mine].astype(f32) + partr[out_chunk(c), :].astype(f32)).astype(bf16)
        for k in range(c * per, (c + 1) * per):
            ret_half(k).wait_send()
        rets[far_chunk(c), :] = total
        for k in range(c * per, (c + 1) * per):
            po_half(k).start()

    dnar, ob = rows.at[0:T], rows.at[T : 2 * T]
    out_copy = send(ob.at[:, mine], ob.at[:, mine], s_x.at[8], r_x.at[8], partner)
    gna_copy = send(gna, gnar, s_x.at[9], r_x.at[9], partner)
    dnb_copy = send(dnb.at[:, mine], dnb.at[:, mine], s_x.at[5], r_x.at[5], partner)
    dnsh_copy = send(dnsh.at[:, theirs], dnsh_r, s_x.at[4], r_x.at[4], partner)
    shp_copy = send(shp.at[:, theirs], shpr, s_x.at[7], r_x.at[7], partner)

    def columns(p):
        return slice(p * F, (p + 1) * F) if p < 3 else (slice(0, HL), slice(HL, W2))[p - 3]

    def fold_bufs(p):
        return (a1, b1, d1) if p < 3 else (a2, b2, d2)

    def fold_y(p):
        a, b, d = fold_bufs(p)
        return send(
            a.at[:, 1 - y, :, columns(p)], b.at[:, :, columns(p)], s_y.at[p], r_y.at[p], neighbour
        )

    def fold_z(p, k):
        a, b, d = fold_bufs(p)
        to = lax.rem(z + k, zs)
        return send(
            b.at[to, :, columns(p)], d.at[k - 1, :, columns(p)], s_z.at[p, k - 1], r_z.at[p, k - 1],
            (to * 4 + lax.rem(me, 4), t),
        )

    def fold_on(p):
        a, b, d = fold_bufs(p)
        fold_y(p).wait()

        def body(i, carry):
            b[i, :, columns(p)] = (
                b[i, :, columns(p)].astype(f32) + a[i, y, :, columns(p)].astype(f32)
            ).astype(bf16)
            return carry

        lax.fori_loop(0, zs, body, 0)
        for k in range(1, zs):
            fold_z(p, k).start()

    def fold_end(p, w):
        a, b, d = fold_bufs(p)
        total = b[z, :, columns(p)].astype(f32)
        for k in range(1, zs):
            fold_z(p, k).wait()
            total = total + d[k - 1, :, columns(p)].astype(f32)
        w[:, columns(p)] = total

    def experts(vsi, vso, vei, veo, act, dgu, normed, tall, wide):
        weights = [
            pltpu.make_async_copy(a, b, lsem.at[4 + i])
            for i, (a, b) in enumerate(((si, vsi), (so, vso), (ei, vei), (eo, veo)))
        ]
        for c in weights:
            c.start()

        def norm2_step(i, carry):
            at = pl.ds(pl.multiple_of(i * FOLD, FOLD), FOLD)
            x = resid[at, :]
            r = lax.rsqrt(jnp.mean(x * x, axis=1, keepdims=True) + epsilon)
            normed[at, :] = (x * r * nf[...].reshape(1, D)).astype(bf16)
            return carry

        lax.fori_loop(0, T // FOLD, norm2_step, 0)

        def near_step(k, carry):
            values = dot(plan[row_at(k), :], normed[...]).astype(bf16)

            @pl.when(k > 0)
            def _():
                near_send[row_at(k), :] = values
                row_copy(k).start()

            @pl.when(k == 0)
            def _():
                rows[row_at(k), :] = values

            return carry

        def far_step(i, carry):
            k = G - 1 - i
            rets[far_at(k), :] = dot(plan[row_at(k), :], normed[:, mine]).astype(bf16)
            row_half(k).start()
            return carry

        lax.fori_loop(0, G - near, far_step, 0)
        lax.fori_loop(0, near, near_step, 0)
        for k in range(G - 1, near - 1, -1):
            cot_hand_on(k)

        mid = slice(M, M + T)

        def shared_step(u, carry):
            at = pl.ds(pl.multiple_of(u * tile, tile), tile)
            pre = dot(normed[...], vsi[0, :, at])
            up = dot(normed[...], vsi[1, :, at])
            d_act = dot_nt(cot[...], vso[at, :])
            s = sigmoid(pre)
            gs = pre * s
            act[mid, at] = (gs * up).astype(bf16)
            dgu[0, mid, at] = (d_act * up * (s + gs * (1.0 - s))).astype(bf16)
            dgu[1, mid, at] = (d_act * gs).astype(bf16)
            return carry

        def tile_at(i):
            return pl.ds(pl.multiple_of(i * tile, tile), tile)

        def fold_core(i):
            return send(
                tall.at[lax.rem(i, 2), :, :, 1 - core], a1.at[:, :, :, tile_at(i)], s_k.at[i], r_k.at[i],
                sibling,
            )

        def core_end(i):
            fold_core(i).wait()

            def body(n, carry):
                u, v = n // 2, lax.rem(n, 2)
                a1[u, v, :, tile_at(i)] = (
                    a1[u, v, :, tile_at(i)].astype(f32) + tall[lax.rem(i, 2), u, v, core].astype(f32)
                ).astype(bf16)
                return carry

            lax.fori_loop(0, 2 * zs, body, 0)

        def shared_grads(p):
            def body(i, carry):
                at = tile_at(i - p * tiles)
                if p < 2:
                    grad = dot(vsi[0, :, 0:T], dgu[p, mid, at])
                else:
                    grad = dot(vsi[1, :, 0:T], act[mid, at])
                tall[lax.rem(i, 2)] = grad.astype(bf16).reshape(tall.shape[1:])
                fold_core(i).start()

                @pl.when(i > p * tiles)
                def _():
                    core_end(i - 1)

                return carry

            lax.fori_loop(p * tiles, (p + 1) * tiles, body, 0)
            core_end((p + 1) * tiles - 1)
            fold_y(p).start()

        def expert_chunk(c):
            for k in range(c * per, (c + 1) * per):
                if k >= near:
                    row_pass(k).wait_recv()
                    cot_pass(k).wait_recv()
                elif k > 0:
                    row_copy(k).wait_recv()
                    cot_copy(k).wait_recv()
            block = chunk_at(c)

            def unit_step(u, carry):
                at = pl.ds(pl.multiple_of(u * tile, tile), tile)
                pre = dot(rows[block, :], vei[0, :, at])
                up = dot(rows[block, :], vei[1, :, at])
                d_act = dot_nt(drows[block, :], veo[at, :])
                s = sigmoid(pre)
                gs = pre * s
                act[block, at] = (gs * up).astype(bf16)
                dgu[0, block, at] = (d_act * up * (s + gs * (1.0 - s))).astype(bf16)
                dgu[1, block, at] = (d_act * gs).astype(bf16)
                return carry

            lax.fori_loop(0, tiles, unit_step, 0)
            dx = dot_nt(dgu[0, block, :], vei[0]) + dot_nt(dgu[1, block, :], vei[1])
            for k in range(c * per, (c + 1) * per):
                if k >= near:
                    cot_half(k).wait_send()
                elif k > 0:
                    cot_copy(k).wait_send()
            csend[block, :] = dx.astype(bf16)
            if c > 0:
                dx_copy(c).start()
                return
            for k in range(c * per, (c + 1) * per):
                if k > 0:
                    ret_copy(k).start()
                else:
                    near_ret[0:C, :] = csend[0:C, :]

        weights[0].wait()
        weights[1].wait()
        lax.fori_loop(0, tiles, shared_step, 0)
        dnsh[...] = (dot_nt(dgu[0, mid, :], vsi[0]) + dot_nt(dgu[1, mid, :], vsi[1])).astype(bf16)
        weights[2].wait()
        weights[3].wait()
        vsi[0, :, 0:T] = normed[...].T
        vsi[1, :, 0:T] = cot[...].T
        shp[...] = dot(act[mid, :], vso[...]).astype(bf16)
        expert_chunk(0)
        for k in range(G - 1, G - 5, -1):
            hand_on(k)
        shared_grads(0)
        expert_chunk(3)
        for k in range(G - 5, G - 7, -1):
            hand_on(k)
        shared_grads(1)
        for k in range(G - 7, near - 1, -1):
            hand_on(k)
        shared_grads(2)
        return_chunk(3)

        expert_chunk(2)
        expert_chunk(1)
        for k in range(1, per):
            ret_copy(k).wait_recv()
        dnsh[...] = (dnsh[...].astype(f32) + dot_tn(plan[0:M, :], near_ret[...])).astype(bf16)
        dnsh_copy.start()
        return_chunk(2)

        def part_chunk(c):
            if c > 0:
                dx_copy(c).wait_send()
            else:
                for k in range(1, per):
                    ret_copy(k).wait_send()
            csend[chunk_at(c), :] = dot(act[chunk_at(c), :], veo[...]).astype(bf16)

        part_chunk(0)
        near_ro[0:C, :] = csend[0:C, :]
        part_chunk(3)
        return_chunk(1)
        part_copy(3).start()
        part_chunk(2)
        part_chunk(1)
        for k in range(1, whole):
            po_copy(k).start()
        sides = [slice(0, S // 2), slice(S // 2, S)]
        for n in range(2):
            vsi[n, :, 0 : S // 2] = rows[sides[n], :].T

        def gein_copy(i):
            return pltpu.make_async_copy(
                tall.at[lax.rem(i, 2)], gein.at[i // tiles, :, :, :, :, tile_at(lax.rem(i, tiles))],
                osem.at[lax.rem(i, 2)],
            )

        def gein_step(i, carry):
            @pl.when(i > 1)
            def _():
                gein_copy(i - 2).wait()

            at = tile_at(lax.rem(i, tiles))
            grad = dot(vsi[0, :, 0 : S // 2], dgu[i // tiles, sides[0], at])
            grad = grad + dot(vsi[1, :, 0 : S // 2], dgu[i // tiles, sides[1], at])
            tall[lax.rem(i, 2)] = grad.astype(bf16).reshape(tall.shape[1:])
            gein_copy(i).start()
            return carry

        first = 2
        lax.fori_loop(0, first, gein_step, 0)
        for k in range(near, G):
            row_pass(k).wait_send()

        dnsh_copy.wait()
        total = dnsh[:, mine].astype(f32) + dnsh_r[...].astype(f32)
        for k in range(per, G):
            ret_half(k).wait_recv()
        total = total + dot_tn(plan[M:S, :], ret[...])
        dnb[:, mine] = total.astype(bf16)
        dnb_copy.start()
        part_copy(2).start()
        if whole == per:
            part_copy(1).start()
        for p in range(3):
            fold_on(p)
        lax.fori_loop(first, 2 * tiles, gein_step, 0)
        return_part(3)

        def geout_copy(i):
            return pltpu.make_async_copy(
                wide.at[lax.rem(i, 2)], geout.at[tile_at(i), :], osem.at[2 + lax.rem(i, 2)]
            )

        def geout_step(i, carry):
            @pl.when(i > 1)
            def _():
                geout_copy(i - 2).wait()

            wide[lax.rem(i, 2)] = dot_tn(act[:, tile_at(i)], drows[...]).astype(bf16)
            geout_copy(i).start()
            return carry

        lax.fori_loop(0, tiles, geout_step, 0)
        gein_copy(2 * tiles - 2).wait()
        gein_copy(2 * tiles - 1).wait()
        geout_copy(tiles - 2).wait()
        geout_copy(tiles - 1).wait()

    pl.run_scoped(
        experts,
        pltpu.VMEM((2, D, F), bf16),
        pltpu.VMEM((F, D), bf16),
        pltpu.VMEM((2, D, F), bf16),
        pltpu.VMEM((F, D), bf16),
        pltpu.VMEM((S, F), bf16),
        pltpu.VMEM((2, S, F), bf16),
        pltpu.VMEM((T, D), bf16),
        pltpu.VMEM((2, zs, 2, 2, share, tile), bf16),
        pltpu.VMEM((2, tile, D), bf16),
    )

    def attention_back(dres, dresb, da, dqkv, turned, turned2, pay, gated, dna, gtok, w1, w2):
        dna_copy = send(dna, dnar, s_x.at[10], r_x.at[10], partner)
        turned[...] = normed_a[...].T
        dnb_copy.wait()

        def gated_rows(c):
            for k in range(c * per, (c + 1) * per):
                gated[(k - c * per) * C : (k - c * per + 1) * C, :] = (
                    plan[row_at(k), :].astype(f32) * gate[pl.ds(peer(k), 1), :]
                ).astype(bf16)
            return gated[...]

        def dres_step(i, carry):
            at = pl.ds(pl.multiple_of(i * FOLD, FOLD), FOLD)
            y_ = dnb[at, :].astype(f32)
            x = resid[at, :]
            r = lax.rsqrt(jnp.mean(x * x, axis=1, keepdims=True) + epsilon)
            a = y_ * nf[...].reshape(1, D)
            inner = jnp.mean(a * x, axis=1, keepdims=True)
            xr = x * r
            value = cot[at, :].astype(f32) + r * a - xr * (r * r * inner)
            dres[at, :] = value
            dresb[at, :] = value.astype(bf16)
            return carry + jnp.sum(y_ * xr, axis=0, keepdims=True)

        gnf = lax.fori_loop(0, T // FOLD, dres_step, jnp.zeros((1, D), f32))
        da[...] = dot_nt(dresb[...], wo[...]).astype(bf16)
        turned2[...] = dresb[...].T
        pay[:, :, :, :, 0:HL] = dot(turned2[...], att_own[...]).astype(bf16).reshape(zs, 2, 2, share, HL)

        def pay_core(p):
            return send(
                pay.at[:, :, 1 - core, :, columns(p)], a2.at[:, :, :, columns(p)], s_x.at[8 + p], r_x.at[8 + p],
                sibling,
            )

        def pay_on(p):
            pay_core(p).wait()

            def body(n, carry):
                u, v = n // 2, lax.rem(n, 2)
                a2[u, v, :, columns(p)] = (
                    a2[u, v, :, columns(p)].astype(f32) + pay[u, v, core, :, columns(p)].astype(f32)
                ).astype(bf16)
                return carry

            lax.fori_loop(0, 2 * zs, body, 0)
            fold_y(p).start()

        pay_core(3).start()

        def attend_back(j, carry):
            at = pl.ds(pl.multiple_of(j * 128, 128), 128)
            q, k, v, g = qkv[0, :, at], qkv[1, :, at], qkv[2, :, at], da[:, at]
            none = jnp.zeros_like(q)
            dq = dk = dv = jnp.zeros((T, 128), f32)
            for i in range(2):
                inside = (lane < HD) if i == 0 else (lane >= HD)
                qi, ki, gi = (jnp.where(inside, x, none) for x in (q, k, g))
                total = jnp.sum(jnp.where(lane == 2 * j + i, lse[...], 0.0), axis=1, keepdims=True)
                p = jnp.exp(dot_nt(qi, k) * scale + bias[...] - total)
                dp = dot_nt(gi, v)
                inner = jnp.sum(dp * p, axis=1, keepdims=True)
                ds = (p * (dp - inner)).astype(bf16)
                dv = dv + dot_tn(p.astype(bf16), gi)
                dq = dq + dot(ds, ki)
                dk = dk + dot_tn(ds, qi)
            dq, dk = dq * scale, dk * scale
            dqkv[0, :, at] = (dq * cos[...] - swap_halves(dq) * sin[...]).astype(bf16)
            dqkv[1, :, at] = (dk * cos[...] - swap_halves(dk) * sin[...]).astype(bf16)
            dqkv[2, :, at] = dv.astype(bf16)
            return carry

        lax.fori_loop(0, HL // 128, attend_back, 0)
        pay_on(3)

        dna[...] = (
            dot_nt(dqkv[0], wqkv[0]) + dot_nt(dqkv[1], wqkv[1]) + dot_nt(dqkv[2], wqkv[2])
        ).astype(bf16)

        def gain_step(i, carry):
            at = pl.ds(pl.multiple_of(i * FOLD, FOLD), FOLD)
            x = tok[at, :].astype(f32)
            r = lax.rsqrt(jnp.mean(x * x, axis=1, keepdims=True) + epsilon)
            return carry + jnp.sum(dna[at, :].astype(f32) * x * r, axis=0, keepdims=True)

        gna[...] = jnp.broadcast_to(
            lax.fori_loop(0, T // FOLD, gain_step, jnp.zeros((1, D), f32)), gna.shape
        )
        gna_copy.start()
        dna_copy.start()
        return_part(2)
        if whole == per:
            return_part(1)
        mixed = shp[...].astype(f32)
        for c in range(whole // per):
            for k in range(max(1, c * per), (c + 1) * per):
                po_copy(k).wait_recv()
            mixed = mixed + dot_tn(gated_rows(c), near_ro[chunk_at(c), :])
        shp[...] = mixed.astype(bf16)
        shp_copy.start()
        for s in range(3):
            pay[:, :, :, :, (s + 1) * HL : (s + 2) * HL] = (
                dot(turned[...], dqkv[s]).astype(bf16).reshape(zs, 2, 2, share, HL)
            )
        gna_copy.wait()
        row = lax.broadcasted_iota(jnp.int32, (128, D), 0)
        gains = jnp.where(row == 0, gnf, jnp.where(row == 1, gna[0:1, :] + gnar[0:1, :], 0.0))
        pay[:, :, :, :, 4 * HL :] = gains.T.astype(bf16).reshape(zs, 2, 2, share, 128)
        pay_core(4).start()
        fold_on(3)
        pay_on(4)
        for p in range(3):
            fold_end(p, w1)
        fold_on(4)

        shp_copy.wait()
        mixed = shp[:, mine].astype(f32) + shpr[...].astype(f32)
        for c in range(whole // per, chunks):
            for k in range(c * per, (c + 1) * per):
                po_half(k).wait_recv()
            mixed = mixed + dot_tn(gated_rows(c), ro[out_chunk(c), :])
        ob[:, mine] = (resid[:, mine] + mixed).astype(bf16)
        out_copy.start()
        dna_copy.wait()

        def last_step(i, carry):
            at = pl.ds(pl.multiple_of(i * FOLD, FOLD), FOLD)
            x = tok[at, :].astype(f32)
            r = lax.rsqrt(jnp.mean(x * x, axis=1, keepdims=True) + epsilon)
            a = (dna[at, :].astype(f32) + dnar[at, :].astype(f32)) * na[...].reshape(1, D)
            inner = jnp.mean(a * x, axis=1, keepdims=True)
            gtok[at, :] = (dres[at, :] + r * a - x * (r * r * r * inner)).astype(bf16)
            return carry

        lax.fori_loop(0, T // FOLD, last_step, 0)
        fold_end(3, w2)
        fold_end(4, w2)
        ends = [
            pltpu.make_async_copy(a, b, osem.at[i])
            for i, (a, b) in enumerate(((gtok, h_gtok), (w1, h_gw1), (w2, h_gw2), (ob, h_out)))
        ]
        for c in ends[:3]:
            c.start()
        out_copy.wait()
        ends[3].start()
        for c in ends:
            c.wait()

    pl.run_scoped(
        attention_back,
        pltpu.VMEM((T, D), f32),
        pltpu.VMEM((T, D), bf16),
        pltpu.VMEM((T, HL), bf16),
        pltpu.VMEM((3, T, HL), bf16),
        pltpu.VMEM((D, T), bf16),
        pltpu.VMEM((D, T), bf16),
        pltpu.VMEM((zs, 2, 2, share, W2), bf16),
        pltpu.VMEM((M, T), bf16),
        pltpu.VMEM((T, D), bf16),
        pltpu.VMEM((T, D), bf16),
        pltpu.VMEM((share, 3 * F), f32),
        pltpu.VMEM((share, W2), f32),
    )
    for k in range(near, G):
        cot_pass(k).wait_send()
    for k in range(whole, G):
        po_half(k).wait_send()
    for k in range(1, near):
        row_copy(k).wait_send()
    for k in range(1, whole):
        po_copy(k).wait_send()
    for k in range(per, whole):
        ret_half(k).wait_send()
    for c in range(whole // per, chunks):
        part_copy(c).wait_send()


def finish_kernel(
    HL, F, h_out, h_gtok, h_gw1, h_gw2, h_gein, h_geout,
    out, gtok, gqkv, gao, gna, gnf, gsi, gso, gein, geout,
):
    out[...] = h_out[...]
    gtok[...] = h_gtok[...]
    gein[...] = h_gein[...].astype(f32)
    geout[...] = h_geout[...].astype(f32)

    @pl.when(pl.program_id(0) == 0)
    def _():
        for s in range(3):
            gqkv[s] = h_gw2[:, (s + 1) * HL : (s + 2) * HL]
        gao[...] = h_gw2[:, 0:HL]
        gains = h_gw2[:, 4 * HL :].T
        gnf[...] = gains[0:1, :]
        gna[...] = gains[1:2, :]
        for s in range(2):
            gsi[s] = h_gw1[:, s * F : (s + 1) * F]
        gso[...] = h_gw1[:, 2 * F :]


def fused(
    tokens, cont_lengths, routes, route_gates, w_qkv, w_attn_out, norm_attn, norm_ffn,
    shared_in, shared_out, expert_in, expert_out, cotangent,
):
    T, D = tokens.shape
    G = lax.axis_size("dp")
    HL, F = w_qkv.shape[2], shared_in.shape[2]
    C = round_up(CAP, 16)
    S = G * C
    half, share, zs = D // 2, D // G, G // 4
    W1, W2 = 3 * F, 4 * HL + 128
    shape = jax.ShapeDtypeStruct
    dma = pltpu.SemaphoreType.DMA
    SM = pl.BlockSpec(memory_space=pltpu.SMEM)
    out, gtok, gw1, gw2, gein, geout = pl.pallas_call(
        functools.partial(layer_kernel, G),
        out_shape=(
            shape((T, D), bf16), shape((T, D), bf16), shape((share, W1), f32), shape((share, W2), f32),
            shape((2, zs, 2, 2, share, F), bf16), shape((F, D), bf16),
        ),
        in_specs=[VM] * 2 + [SM] + [VM] * 2 + [ANY] * 8,
        out_specs=(ANY,) * 6,
        scratch_shapes=[
            pltpu.VMEM((T, D), bf16),
            pltpu.VMEM((3, D, HL), bf16),
            pltpu.VMEM((HL, D), bf16),
            pltpu.VMEM((T, D), bf16),
            pltpu.VMEM((T, 128), f32),
            pltpu.VMEM((T, 128), f32),
            pltpu.VMEM((3, T, HL), bf16),
            pltpu.VMEM((T, 128), f32),
            pltpu.VMEM((T, HL), bf16),
            pltpu.VMEM((T, D), bf16),
            pltpu.VMEM((T, D), f32),
            pltpu.VMEM((S, T), bf16),
            pltpu.VMEM((EXPERTS, T), f32),
            pltpu.VMEM((EXPERTS, T), f32),
            pltpu.VMEM((T, T), f32),
            pltpu.VMEM((T, HL), bf16),
            pltpu.VMEM((HL, D), bf16),
            pltpu.VMEM((S, D), bf16),
            pltpu.VMEM((S, D), bf16),
            pltpu.VMEM((S, D), bf16),
            pltpu.VMEM((NEAR * C, D), bf16),
            pltpu.VMEM((S - 4 * C, half), bf16),
            pltpu.VMEM((4 * C, D), bf16),
            pltpu.VMEM((S - 4 * C, half), bf16),
            pltpu.VMEM((S - 4 * C, half), bf16),
            pltpu.VMEM((T, D), bf16),
            pltpu.VMEM((T, half), bf16),
            pltpu.VMEM((T, D), bf16),
            pltpu.VMEM((T, D), bf16),
            pltpu.VMEM((S - WHOLE * C, half), bf16),
            pltpu.VMEM((WHOLE * C, D), bf16),
            pltpu.VMEM((S - WHOLE * C, half), bf16),
            pltpu.VMEM((T, half), bf16),
            pltpu.VMEM((8, D), f32),
            pltpu.VMEM((8, D), f32),
            *[
                pltpu.VMEM((*dims, share, width), bf16)
                for width in (W1, W2)
                for dims in ((zs, 2), (zs,), (zs - 1,))
            ],
            dma((13,)), dma((13,)), *[dma((G,))] * 8, dma((4,)), dma((4,)), dma((G,)), dma((G,)),
            dma((4,)), dma((4,)), dma((G,)), dma((G,)), dma((12,)), dma((12,)), dma((5,)), dma((5,)),
            dma((5, zs - 1)), dma((5, zs - 1)), dma((8,)), dma((4,)),
        ],
        compiler_params=pltpu.CompilerParams(
            collective_id=0, has_side_effects=True, vmem_limit_bytes=VMEM_BYTES
        ),
        name="layer",
    )(
        norm_attn, norm_ffn, cont_lengths, routes.T, route_gates.T, tokens, w_qkv, w_attn_out, cotangent,
        shared_in, shared_out, expert_in, expert_out,
    )
    steps = 2

    def rows_of(*dims):
        return pl.BlockSpec(dims, lambda i: (0,) * (len(dims) - 2) + (i, 0))

    def whole(*dims):
        return pl.BlockSpec(dims, lambda i: (0,) * len(dims))

    results = ((3, share, HL), (share, HL), (1, share), (1, share), (2, share, F), (share, F))
    out, gtok, gqkv, gao, gna, gnf, gsi, gso, gein, geout = pl.pallas_call(
        functools.partial(finish_kernel, HL, F),
        grid=(steps,),
        out_shape=(
            shape((T, D), bf16), shape((T, D), bf16), *[shape(r, f32) for r in results],
            shape((2, D, F), f32), shape((F, D), f32),
        ),
        in_specs=[
            rows_of(T // steps, D), rows_of(T // steps, D), whole(share, W1), whole(share, W2),
            rows_of(2, D // steps, F), rows_of(F // steps, D),
        ],
        out_specs=(
            rows_of(T // steps, D), rows_of(T // steps, D), *[whole(*r) for r in results],
            rows_of(2, D // steps, F), rows_of(F // steps, D),
        ),
        compiler_params=pltpu.CompilerParams(vmem_limit_bytes=VMEM_BYTES),
        name="finish",
    )(out, gtok, gw1, gw2, gein.reshape(2, D, F), geout)
    return (out, gtok, gqkv, gao.T, gna[0], gnf[0], gsi, gso.T, gein, geout)


def solution(mesh):
    placed = (
        P("dp", None),
        P("dp", None),
        P("dp", None),
        P("dp", None),
        P(None, None, "tensor"),
        P("tensor", None),
        P(),
        P(),
        P(None, None, "tensor"),
        P("tensor", None),
        P(None, None, ("dp", "tensor")),
        P(("dp", "tensor"), None),
        P("dp", None),
    )
    return jax.shard_map(
        fused if mesh.shape["dp"] == EXPERTS else local,
        mesh=mesh,
        in_specs=placed,
        out_specs=(
            P("dp", None),
            P("dp", None),
            P(None, "dp", "tensor"),
            P("tensor", "dp"),
            P("dp"),
            P("dp"),
            P(None, "dp", "tensor"),
            P("tensor", "dp"),
            P(None, None, ("dp", "tensor")),
            P(("dp", "tensor"), None),
        ),
        check_vma=False,
    )
```

```python
import functools
import math

import jax
import jax.numpy as jnp
from jax import lax
from jax.experimental import pallas as pl
from jax.experimental.pallas import tpu as pltpu
from jax.sharding import PartitionSpec as P

HD = 64
EXPERTS = 16
TOP = 2
PROMPT = 64
CAP = 92


epsilon = 1e-06


def rms_parts(values, gain):
    factor = lax.rsqrt(jnp.mean(values * values, axis=-1, keepdims=True) + epsilon)
    return (values * factor * gain, factor)


def rms_back(values, factor, gain, incoming):
    weighted = incoming * gain
    inner = jnp.mean(weighted * values, axis=-1, keepdims=True)
    return (
        factor * weighted - values * factor * factor * factor * inner,
        jnp.sum(incoming * values * factor, axis=0),
    )


def silu_act(values):
    return values * jax.nn.sigmoid(values)


def swiglu_back(gate_up, d_act):
    sigma = jax.nn.sigmoid(gate_up[0])
    d_gate = d_act * gate_up[1] * sigma * (1.0 + gate_up[0] * (1.0 - sigma))
    d_upper = d_act * gate_up[0] * sigma
    return jnp.stack([d_gate, d_upper]).astype(jnp.bfloat16)


def group_layout(lengths, rows_here):
    row_index = jnp.arange(rows_here, dtype=jnp.int32)
    cont_ends = PROMPT + jnp.cumsum(lengths, dtype=jnp.int32)
    begins = cont_ends - lengths
    later = jnp.sum(
        (row_index[:, None] >= cont_ends[None, :]).astype(jnp.int32), axis=1, dtype=jnp.int32
    )
    segment = jnp.where(row_index < PROMPT, 0, 1 + later)
    member = (
        segment[:, None] == jnp.arange(1, lengths.shape[0] + 1, dtype=jnp.int32)[None, :]
    ).astype(jnp.int32)
    offset = jnp.sum(member * begins[None, :], axis=1, dtype=jnp.int32)
    position = jnp.where(segment == 0, row_index, PROMPT + row_index - offset)
    allowed = (row_index[None, :] <= row_index[:, None]) & (
        (segment[None, :] == 0) | (segment[None, :] == segment[:, None])
    )
    return (position, allowed)


def rope_tables(position):
    half_size = HD // 2
    inv_freq = 10000.0 ** (-jnp.arange(half_size, dtype=jnp.float32) / half_size)
    angles = position.astype(jnp.float32)[:, None] * inv_freq[None, :]
    return (jnp.cos(angles)[:, None, :], jnp.sin(angles)[:, None, :])


def rotate_pairs(values, cosine, sine):
    half_size = values.shape[-1] // 2
    front_half = values[..., :half_size]
    back_half = values[..., half_size:]
    return jnp.concatenate(
        [front_half * cosine - back_half * sine, front_half * sine + back_half * cosine], axis=-1
    )


def dispatch_plan(routes):
    flat_routes = routes.reshape(-1)
    one_hot = (flat_routes[:, None] == jnp.arange(EXPERTS, dtype=jnp.int32)[None, :]).astype(
        jnp.int32
    )
    earlier = jnp.cumsum(one_hot, axis=0, dtype=jnp.int32) - one_hot
    place_in = jnp.sum(earlier * one_hot, axis=1, dtype=jnp.int32)
    target = flat_routes * CAP + place_in
    pair_count = flat_routes.shape[0]
    slot_table = (
        jnp.full((EXPERTS * CAP,), pair_count, jnp.int32)
        .at[target]
        .set(jnp.arange(pair_count, dtype=jnp.int32))
    )
    return (target, slot_table)


def spread_rows(padded, indices, copies):
    model_width = padded.shape[1]
    picked = jnp.take(padded, indices, axis=0).reshape(EXPERTS, 1, CAP, model_width)
    return jnp.broadcast_to(picked, (EXPERTS, copies, CAP, model_width)).reshape(
        EXPERTS * copies, CAP, model_width
    )


def collect_rows(returned, target, copies, rows_here):
    model_width = returned.shape[2]
    summed = jnp.sum(returned.reshape(EXPERTS, copies, CAP, model_width), axis=1, dtype=jnp.float32)
    summed = summed.reshape(EXPERTS * CAP, model_width)
    return jnp.take(summed, target, axis=0).reshape(rows_here, TOP, model_width)


def local(
    tokens,
    cont_lengths,
    routes,
    route_gates,
    w_qkv,
    w_attn_out,
    norm_attn,
    norm_ffn,
    shared_in,
    shared_out,
    expert_in,
    expert_out,
    cotangent,
):
    rows_here = tokens.shape[0]
    model_width = tokens.shape[1]
    groups = lax.axis_size("dp")
    copies = groups // EXPERTS
    head_count = w_qkv.shape[2] // HD
    score_scale = HD ** (-0.5)
    inputs = tokens.astype(jnp.float32)
    position, allowed = group_layout(cont_lengths[0], rows_here)
    cosine, sine = rope_tables(position)
    normed_a, factor_a = rms_parts(inputs, norm_attn)
    normed_attn = normed_a.astype(jnp.bfloat16)
    projected = jnp.einsum("td,sdf->stf", normed_attn, w_qkv, preferred_element_type=jnp.float32)
    query = rotate_pairs(projected[0].reshape(rows_here, head_count, HD), cosine, sine).astype(
        jnp.bfloat16
    )
    key_rows = rotate_pairs(projected[1].reshape(rows_here, head_count, HD), cosine, sine).astype(
        jnp.bfloat16
    )
    value_rows = projected[2].reshape(rows_here, head_count, HD).astype(jnp.bfloat16)
    score = (
        jnp.einsum("qhd,khd->hqk", query, key_rows, preferred_element_type=jnp.float32)
        * score_scale
    )
    score = jnp.where(allowed[None], score, -1000000000.0)
    row_max = jnp.max(score, axis=-1, keepdims=True)
    exponent = jnp.exp(score - row_max)
    row_total = jnp.sum(exponent, axis=-1, keepdims=True)
    log_total = row_max + jnp.log(row_total)
    weights_b = (exponent / row_total).astype(jnp.bfloat16)
    attended = jnp.einsum("hqk,khd->qhd", weights_b, value_rows, preferred_element_type=jnp.float32)
    attended = attended.reshape(rows_here, head_count * HD).astype(jnp.bfloat16)
    attn_part = jnp.dot(attended, w_attn_out, preferred_element_type=jnp.float32)
    resid = inputs + lax.psum(attn_part.astype(jnp.bfloat16), "tensor").astype(jnp.float32)
    normed_f, factor_f = rms_parts(resid, norm_ffn)
    normed_ffn = normed_f.astype(jnp.bfloat16)
    gate_up = jnp.einsum("td,sdf->stf", normed_ffn, shared_in, preferred_element_type=jnp.float32)
    shared_act = (silu_act(gate_up[0]) * gate_up[1]).astype(jnp.bfloat16)
    shared_part = jnp.dot(shared_act, shared_out, preferred_element_type=jnp.float32)
    target, slot_table = dispatch_plan(routes)
    padded_rows = jnp.concatenate([normed_ffn, jnp.zeros((1, model_width), jnp.bfloat16)], axis=0)
    send_rows = spread_rows(padded_rows, slot_table // TOP, copies)
    arrived = lax.all_to_all(send_rows, "dp", split_axis=0, concat_axis=0, tiled=True)
    expert_input = arrived.reshape(groups * CAP, model_width)
    expert_gu = jnp.einsum(
        "rd,sdf->srf", expert_input, expert_in, preferred_element_type=jnp.float32
    )
    expert_act = (silu_act(expert_gu[0]) * expert_gu[1]).astype(jnp.bfloat16)
    expert_part = jnp.dot(expert_act, expert_out, preferred_element_type=jnp.float32).astype(
        jnp.bfloat16
    )
    returned = lax.all_to_all(
        expert_part.reshape(groups, CAP, model_width), "dp", split_axis=0, concat_axis=0, tiled=True
    )
    picked = collect_rows(returned, target, copies, rows_here)
    mixed = jnp.sum(route_gates[:, :, None] * picked, axis=1)
    ffn_total = lax.psum((shared_part + mixed).astype(jnp.bfloat16), "tensor").astype(jnp.float32)
    output = (resid + ffn_total).astype(jnp.bfloat16)
    upstream = cotangent.astype(jnp.float32)
    d_shared_act = jnp.einsum(
        "td,fd->tf", cotangent, shared_out, preferred_element_type=jnp.float32
    )
    d_shared_gu = swiglu_back(gate_up, d_shared_act)
    d_normed = jnp.einsum("stf,sdf->td", d_shared_gu, shared_in, preferred_element_type=jnp.float32)
    g_shared_in = jnp.einsum(
        "td,stf->sdf", normed_ffn, d_shared_gu, preferred_element_type=jnp.float32
    )
    g_shared_out = jnp.einsum(
        "tf,td->fd", shared_act, cotangent, preferred_element_type=jnp.float32
    )
    pair_grad = (
        (route_gates[:, :, None] * upstream[:, None, :])
        .reshape(rows_here * TOP, model_width)
        .astype(jnp.bfloat16)
    )
    padded_grad = jnp.concatenate([pair_grad, jnp.zeros((1, model_width), jnp.bfloat16)], axis=0)
    send_grad = spread_rows(padded_grad, slot_table, copies)
    again_rows = spread_rows(padded_rows, slot_table // TOP, copies)
    grad_arrived, rows_arrived = (
        lax.all_to_all(send_grad, "dp", split_axis=0, concat_axis=0, tiled=True),
        lax.all_to_all(again_rows, "dp", split_axis=0, concat_axis=0, tiled=True),
    )
    rows_back = rows_arrived.reshape(groups * CAP, model_width)
    d_expert_rows = grad_arrived.reshape(groups * CAP, model_width)
    back_gu = jnp.einsum("rd,sdf->srf", rows_back, expert_in, preferred_element_type=jnp.float32)
    back_act = (silu_act(back_gu[0]) * back_gu[1]).astype(jnp.bfloat16)
    d_expert_act = jnp.einsum(
        "rd,fd->rf", d_expert_rows, expert_out, preferred_element_type=jnp.float32
    )
    d_expert_gu = swiglu_back(back_gu, d_expert_act)
    d_expert_in = jnp.einsum(
        "srf,sdf->rd", d_expert_gu, expert_in, preferred_element_type=jnp.float32
    ).astype(jnp.bfloat16)
    g_expert_in = jnp.einsum(
        "rd,srf->sdf", rows_back, d_expert_gu, preferred_element_type=jnp.float32
    )
    g_expert_out = jnp.einsum(
        "rf,rd->fd", back_act, d_expert_rows, preferred_element_type=jnp.float32
    )
    d_returned = lax.all_to_all(
        d_expert_in.reshape(groups, CAP, model_width), "dp", split_axis=0, concat_axis=0, tiled=True
    )
    d_normed = d_normed + jnp.sum(collect_rows(d_returned, target, copies, rows_here), axis=1)
    d_normed = lax.psum(d_normed.astype(jnp.bfloat16), "tensor").astype(jnp.float32)
    d_resid_norm, g_norm_ffn = rms_back(resid, factor_f, norm_ffn, d_normed)
    d_resid = upstream + d_resid_norm
    d_resid_b = d_resid.astype(jnp.bfloat16)
    g_attn_out = jnp.einsum("tf,td->fd", attended, d_resid_b, preferred_element_type=jnp.float32)
    d_attended = jnp.einsum("td,fd->tf", d_resid_b, w_attn_out, preferred_element_type=jnp.float32)
    d_attended = d_attended.astype(jnp.bfloat16).reshape(rows_here, head_count, HD)
    recomputed = (
        jnp.einsum("qhd,khd->hqk", query, key_rows, preferred_element_type=jnp.float32)
        * score_scale
    )
    recomputed = jnp.where(allowed[None], recomputed, -1000000000.0)
    probs = jnp.exp(recomputed - log_total)
    probs_b = probs.astype(jnp.bfloat16)
    d_probs = jnp.einsum("qhd,khd->hqk", d_attended, value_rows, preferred_element_type=jnp.float32)
    d_value = jnp.einsum("hqk,qhd->khd", probs_b, d_attended, preferred_element_type=jnp.float32)
    inner = jnp.sum(d_probs * probs, axis=-1, keepdims=True)
    d_score = (probs * (d_probs - inner)).astype(jnp.bfloat16)
    d_query = (
        jnp.einsum("hqk,khd->qhd", d_score, key_rows, preferred_element_type=jnp.float32)
        * score_scale
    )
    d_key = (
        jnp.einsum("hqk,qhd->khd", d_score, query, preferred_element_type=jnp.float32) * score_scale
    )
    d_query = rotate_pairs(d_query, cosine, -sine).reshape(rows_here, head_count * HD)
    d_key = rotate_pairs(d_key, cosine, -sine).reshape(rows_here, head_count * HD)
    d_qkv = jnp.stack([d_query, d_key, d_value.reshape(rows_here, head_count * HD)]).astype(
        jnp.bfloat16
    )
    g_qkv = jnp.einsum("td,stf->sdf", normed_attn, d_qkv, preferred_element_type=jnp.float32)
    d_normed_attn = jnp.einsum("stf,sdf->td", d_qkv, w_qkv, preferred_element_type=jnp.float32)
    d_normed_attn = lax.psum(d_normed_attn.astype(jnp.bfloat16), "tensor").astype(jnp.float32)
    d_input_norm, g_norm_attn = rms_back(inputs, factor_a, norm_attn, d_normed_attn)
    grad_tokens = (d_resid + d_input_norm).astype(jnp.bfloat16)
    summed_all = (
        lax.psum_scatter(g_qkv, "dp", scatter_dimension=1, tiled=True),
        lax.psum_scatter(g_attn_out, "dp", scatter_dimension=1, tiled=True),
        lax.psum_scatter(g_norm_attn, "dp", scatter_dimension=0, tiled=True),
        lax.psum_scatter(g_shared_in, "dp", scatter_dimension=1, tiled=True),
        lax.psum_scatter(g_shared_out, "dp", scatter_dimension=1, tiled=True),
        lax.psum_scatter(g_norm_ffn, "dp", scatter_dimension=0, tiled=True),
    )
    return (
        output,
        grad_tokens,
        summed_all[0],
        summed_all[1],
        summed_all[2],
        summed_all[5],
        summed_all[3],
        summed_all[4],
        g_expert_in,
        g_expert_out,
    )


VMEM_BYTES = 64000 * 1024
FOLD = 96
NEAR = 8
WHOLE = 4
MESH = pl.DeviceIdType.MESH
VM = pl.BlockSpec(memory_space=pltpu.VMEM)
ANY = pl.BlockSpec(memory_space=pl.ANY)
f32 = jnp.float32
bf16 = jnp.bfloat16


def round_up(value, unit):
    return (value + unit - 1) // unit * unit


def dot(a, b):
    return jnp.dot(a, b, preferred_element_type=f32)


def dot_nt(a, b):
    return lax.dot_general(a, b, (((1,), (1,)), ((), ())), preferred_element_type=f32)


def dot_tn(a, b):
    return lax.dot_general(a, b, (((0,), (0,)), ((), ())), preferred_element_type=f32)


def sigmoid(values):
    return 0.5 * jnp.tanh(0.5 * values) + 0.5


def swap_halves(values):
    lane = lax.broadcasted_iota(jnp.int32, values.shape, 1)
    ahead = pltpu.roll(values, values.shape[1] - HD // 2, 1)
    behind = pltpu.roll(values, HD // 2, 1)
    return jnp.where(lax.rem(lane, HD) < HD // 2, ahead, behind)


def hello(groups):
    me, t = lax.axis_index("dp"), lax.axis_index("tensor")
    barrier = pltpu.get_barrier_semaphore()

    def greet(k, carry):
        pl.semaphore_signal(
            barrier, inc=1, device_id=(lax.rem(me + k, groups), t), device_id_type=MESH
        )
        return carry

    lax.fori_loop(1, groups, greet, 0)
    pl.semaphore_signal(barrier, inc=1, device_id=(me, 1 - t), device_id_type=MESH)
    pl.semaphore_wait(barrier, groups)


def segment_of(index, lens):
    segment = jnp.where(index < PROMPT, 0, 1)
    end = PROMPT
    for c in range(lens.shape[1]):
        end = end + lens[0, c]
        segment = segment + jnp.where(index >= end, 1, 0)
    return segment


def position_of(index, lens):
    segment = segment_of(index, lens)
    position, end = index, PROMPT
    for c in range(lens.shape[1]):
        position = jnp.where(segment == c + 1, PROMPT + index - end, position)
        end = end + lens[0, c]
    return position


def fill_bias(bias, lens, rows):
    step = FOLD

    def body(i, carry):
        at = pl.ds(pl.multiple_of(i * step, step), step)
        row = lax.broadcasted_iota(jnp.int32, (step, rows), 0) + i * step
        col = lax.broadcasted_iota(jnp.int32, (step, rows), 1)
        own = segment_of(lax.broadcasted_iota(jnp.int32, (step, 1), 0) + i * step, lens)
        other = segment_of(lax.broadcasted_iota(jnp.int32, (1, rows), 1), lens)
        ok = (col <= row) & ((other == 0) | (other == own))
        bias[at, :] = jnp.where(ok, 0.0, -1000000000.0)
        return carry

    lax.fori_loop(0, rows // step, body, 0)


def fill_angles(cos, sin, lens, rows):
    step = FOLD

    def body(i, carry):
        at = pl.ds(pl.multiple_of(i * step, step), step)
        lane = lax.broadcasted_iota(jnp.int32, (step, 128), 1)
        row = lax.broadcasted_iota(jnp.int32, (step, 128), 0) + i * step
        power = lax.rem(lane, HD // 2).astype(f32) * (-math.log(10000.0) / (HD // 2))
        angle = position_of(row, lens).astype(f32) * jnp.exp(power)
        cos[at, :] = jnp.cos(angle)
        sine = jnp.sin(angle)
        sin[at, :] = jnp.where(lax.rem(lane, HD) < HD // 2, -sine, sine)
        return carry

    lax.fori_loop(0, rows // step, body, 0)


def send(src, dst, ssem, rsem, to):
    return pltpu.make_async_remote_copy(
        src_ref=src, dst_ref=dst, send_sem=ssem, recv_sem=rsem, device_id=to, device_id_type=MESH
    )


def layer_kernel(
    G, na, nf, lens, rT, gT, h_tok, h_wqkv, h_wo, h_cot, si, so, ei, eo,
    h_out, h_gtok, h_gw1, h_gw2, gein, geout,
    tok, wqkv, wo, cot, cos, sin, qkv, lse, att_own, normed_a, resid, plan, gate, slot, bias, att, wo2,
    csend, drows, rows, near_send, rets, near_ret, ret, dxr, dnsh, dnsh_r, dnb, shp, partr, near_ro, ro, shpr, gna, gnar,
    a1, b1, d1, a2, b2, d2,
    s_x, r_x, s_c, r_c, s_cf, r_cf, s_r, r_r, s_f, r_f, s_dx, r_dx, s_ret, r_ret, s_p, r_p, s_po, r_po,
    s_k, r_k, s_y, r_y, s_z, r_z, lsem, osem,
):
    T, D = tok.shape
    HL = wqkv.shape[2]
    F = si.shape[2]
    S = plan.shape[0]
    C = S // G
    half, share, zs = D // 2, D // G, G // 4
    W2 = a2.shape[3]
    scale = HD ** (-0.5)
    me, t = lax.axis_index("dp"), lax.axis_index("tensor")
    core, y, z = lax.rem(me, 2), lax.rem(me // 2, 2), me // 4
    mine = pl.ds(pl.multiple_of(t * half, 128), half)
    theirs = pl.ds(pl.multiple_of((1 - t) * half, 128), half)
    partner = (me, 1 - t)
    sibling = (me + 1 - 2 * core, t)
    neighbour = (me + 2 - 4 * y, t)
    per, tile = 4, 256
    M, chunks, tiles = per * C, G // per, F // tile

    loads = [
        pltpu.make_async_copy(a, b, lsem.at[i])
        for i, (a, b) in enumerate(((h_cot, cot), (h_tok, tok), (h_wqkv, wqkv), (h_wo, wo)))
    ]
    for c in loads:
        c.start()
    hello(G)
    part_wo = pl.ds(pl.multiple_of(core * (HL // 2), 16), HL // 2)
    wo_copy = send(h_wo.at[part_wo], wo2.at[part_wo], s_x.at[0], r_x.at[0], partner)
    wo_copy.start()
    wo_pass = send(wo2.at[part_wo], wo2.at[part_wo], s_x.at[6], r_x.at[6], sibling)

    def row_at(k):
        return pl.ds(pl.multiple_of(k * C, C), C)

    def chunk_at(c):
        return pl.ds(c * M, M)

    near = NEAR
    whole = WHOLE

    def peer(k):
        to, weight = me, 1
        while weight < G:
            bit = lax.rem(k // weight, 2)
            to = to + weight * bit * (1 - 2 * lax.rem(me // weight, 2))
            weight = weight * 2
        return to

    def far_at(k):
        return pl.ds(pl.multiple_of((k - per) * C, C), C)

    def out_at(k):
        return pl.ds(pl.multiple_of((k - whole) * C, C), C)

    def far_chunk(c):
        return pl.ds((c - 1) * M, M)

    def out_chunk(c):
        return pl.ds((c - whole // per) * M, M)

    names = lax.broadcasted_iota(jnp.int32, (EXPERTS, T), 0)
    picks0, picks1 = rT[0:1, :] == names, rT[1:2, :] == names
    member = jnp.where(picks0 | picks1, 1.0, 0.0)
    upper = jnp.where(
        lax.broadcasted_iota(jnp.int32, (T, T), 0) < lax.broadcasted_iota(jnp.int32, (T, T), 1),
        1.0,
        0.0,
    ).astype(bf16)
    slot[...] = jnp.where(member > 0.0, dot(member.astype(bf16), upper), -1.0)
    gate[...] = jnp.where(picks0, gT[0:1, :], 0.0) + jnp.where(picks1, gT[1:2, :], 0.0)

    def cot_copy(k):
        return send(csend.at[row_at(k)], drows.at[row_at(k)], s_c.at[k], r_c.at[k], (peer(k), t))

    def cot_half(k):
        return send(
            csend.at[row_at(k), mine], drows.at[row_at(k), mine], s_c.at[k], r_c.at[k], (peer(k), t)
        )

    def cot_pass(k):
        return send(
            drows.at[row_at(k), mine], drows.at[row_at(k), mine], s_cf.at[k], r_cf.at[k], partner
        )

    def cot_hand_on(k):
        cot_half(k).wait_recv()
        cot_pass(k).start()

    def cot_step(i, carry):
        k = G - 1 - i
        e = peer(k)
        at = row_at(k)
        place = lax.broadcasted_iota(jnp.int32, (C, T), 0).astype(f32)
        hit = slot[pl.ds(e, 1), :] == place
        picked = jnp.where(hit, 1.0, 0.0).astype(bf16)
        plan[at, :] = picked
        weight = jnp.sum(jnp.where(hit, gate[pl.ds(e, 1), :], 0.0), axis=1, keepdims=True)
        grad = (dot(picked, cot[...]) * weight).astype(bf16)
        csend[at, :] = grad

        @pl.when(k >= near)
        def _():
            cot_half(k).start()

        @pl.when((k > 0) & (k < near))
        def _():
            cot_copy(k).start()

        @pl.when(k == 0)
        def _():
            drows[at, :] = grad

        return carry

    loads[0].wait()
    lax.fori_loop(0, G, cot_step, 0)

    fill_angles(cos, sin, lens, T)
    fill_bias(bias, lens, T)
    loads[1].wait()

    def norm_step(i, carry):
        at = pl.ds(pl.multiple_of(i * FOLD, FOLD), FOLD)
        x = tok[at, :].astype(f32)
        r = lax.rsqrt(jnp.mean(x * x, axis=1, keepdims=True) + epsilon)
        normed_a[at, :] = (x * r * na[...].reshape(1, D)).astype(bf16)
        return carry

    lax.fori_loop(0, T // FOLD, norm_step, 0)
    loads[2].wait()
    loads[3].wait()

    def project(s, turned):
        full = dot(normed_a[...], wqkv[s])
        for j in range(HL // 128):
            x = full[:, j * 128 : (j + 1) * 128]
            if turned:
                x = x * cos[...] + swap_halves(x) * sin[...]
            qkv[s, :, j * 128 : (j + 1) * 128] = x.astype(bf16)

    project(0, True)
    project(1, True)
    project(2, False)
    lane = lax.broadcasted_iota(jnp.int32, (T, 128), 1)

    def att_copy(j):
        at = pl.ds(pl.multiple_of(j * 128, 128), 128)
        return send(att_own.at[:, at], att.at[:, at], s_x.at[1 + j], r_x.at[1 + j], partner)

    lse[...] = jnp.zeros_like(lse)

    def attend(j, carry):
        at = pl.ds(pl.multiple_of(j * 128, 128), 128)
        q, k, v = qkv[0, :, at], qkv[1, :, at], qkv[2, :, at]
        outs = []
        for i in range(2):
            inside = (lane < HD) if i == 0 else (lane >= HD)
            s = dot_nt(jnp.where(inside, q, jnp.zeros_like(q)), k) * scale + bias[...]
            top = jnp.max(s, axis=1, keepdims=True)
            e = jnp.exp(s - top)
            total = jnp.sum(e, axis=1, keepdims=True)
            p = (e * (1.0 / total)).astype(bf16)
            lse[...] = jnp.where(lane == 2 * j + i, top + jnp.log(total), lse[...])
            outs.append(dot(p, v))
        att_own[:, at] = jnp.where(lane < HD, outs[0], outs[1]).astype(bf16)
        att_copy(j).start()
        return carry

    wo_copy.wait()
    wo_pass.start()
    lax.fori_loop(0, HL // 128, attend, 0)
    own_out = dot(att_own[...], wo[...])
    wo_pass.wait()
    for j in range(HL // 128):
        att_copy(j).wait()
    resid[...] = tok[...].astype(f32) + own_out + dot(att[...], wo2[...])

    def row_copy(k):
        return send(near_send.at[row_at(k)], rows.at[row_at(k)], s_r.at[k], r_r.at[k], (peer(k), t))

    def row_half(k):
        return send(rets.at[far_at(k)], rows.at[row_at(k), mine], s_r.at[k], r_r.at[k], (peer(k), t))

    def row_pass(k):
        return send(
            rows.at[row_at(k), mine], rows.at[row_at(k), mine], s_f.at[k], r_f.at[k], partner
        )

    def hand_on(k):
        row_half(k).wait_recv()
        row_pass(k).start()

    def dx_copy(c):
        return send(csend.at[chunk_at(c), theirs], dxr.at[far_chunk(c)], s_dx.at[c], r_dx.at[c], partner)

    def ret_copy(k):
        return send(csend.at[row_at(k)], near_ret.at[row_at(k)], s_ret.at[k], r_ret.at[k], (peer(k), t))

    def ret_half(k):
        return send(rets.at[far_at(k)], ret.at[far_at(k)], s_ret.at[k], r_ret.at[k], (peer(k), t))

    def return_chunk(c):
        dx_copy(c).wait_recv()
        total = (csend[chunk_at(c), mine].astype(f32) + dxr[far_chunk(c), :].astype(f32)).astype(bf16)
        for k in range(c * per, (c + 1) * per):
            if k >= near:
                row_half(k).wait_send()
        rets[far_chunk(c), :] = total
        for k in range(c * per, (c + 1) * per):
            ret_half(k).start()

    def part_copy(c):
        return send(csend.at[chunk_at(c), theirs], partr.at[out_chunk(c)], s_p.at[c], r_p.at[c], partner)

    def po_copy(k):
        return send(csend.at[row_at(k)], near_ro.at[row_at(k)], s_po.at[k], r_po.at[k], (peer(k), t))

    def po_half(k):
        return send(rets.at[far_at(k)], ro.at[out_at(k)], s_po.at[k], r_po.at[k], (peer(k), t))

    def return_part(c):
        part_copy(c).wait_recv()
        total = (csend[chunk_at(c), mine].astype(f32) + partr[out_chunk(c), :].astype(f32)).astype(bf16)
        for k in range(c * per, (c + 1) * per):
            ret_half(k).wait_send()
        rets[far_chunk(c), :] = total
        for k in range(c * per, (c + 1) * per):
            po_half(k).start()

    dnar, ob = rows.at[0:T], rows.at[T : 2 * T]
    out_copy = send(ob.at[:, mine], ob.at[:, mine], s_x.at[8], r_x.at[8], partner)
    gna_copy = send(gna, gnar, s_x.at[9], r_x.at[9], partner)
    dnb_copy = send(dnb.at[:, mine], dnb.at[:, mine], s_x.at[5], r_x.at[5], partner)
    dnsh_copy = send(dnsh.at[:, theirs], dnsh_r, s_x.at[4], r_x.at[4], partner)
    shp_copy = send(shp.at[:, theirs], shpr, s_x.at[7], r_x.at[7], partner)

    def columns(p):
        return slice(p * F, (p + 1) * F) if p < 3 else (slice(0, HL), slice(HL, W2))[p - 3]

    def fold_bufs(p):
        return (a1, b1, d1) if p < 3 else (a2, b2, d2)

    def fold_y(p):
        a, b, d = fold_bufs(p)
        return send(
            a.at[:, 1 - y, :, columns(p)], b.at[:, :, columns(p)], s_y.at[p], r_y.at[p], neighbour
        )

    def fold_z(p, k):
        a, b, d = fold_bufs(p)
        to = lax.rem(z + k, zs)
        return send(
            b.at[to, :, columns(p)], d.at[k - 1, :, columns(p)], s_z.at[p, k - 1], r_z.at[p, k - 1],
            (to * 4 + lax.rem(me, 4), t),
        )

    def fold_on(p):
        a, b, d = fold_bufs(p)
        fold_y(p).wait()

        def body(i, carry):
            b[i, :, columns(p)] = (
                b[i, :, columns(p)].astype(f32) + a[i, y, :, columns(p)].astype(f32)
            ).astype(bf16)
            return carry

        lax.fori_loop(0, zs, body, 0)
        for k in range(1, zs):
            fold_z(p, k).start()

    def fold_end(p, w):
        a, b, d = fold_bufs(p)
        total = b[z, :, columns(p)].astype(f32)
        for k in range(1, zs):
            fold_z(p, k).wait()
            total = total + d[k - 1, :, columns(p)].astype(f32)
        w[:, columns(p)] = total

    def experts(vsi, vso, vei, veo, act, dgu, normed, tall, wide):
        weights = [
            pltpu.make_async_copy(a, b, lsem.at[4 + i])
            for i, (a, b) in enumerate(((si, vsi), (so, vso), (ei, vei), (eo, veo)))
        ]
        for c in weights:
            c.start()

        def norm2_step(i, carry):
            at = pl.ds(pl.multiple_of(i * FOLD, FOLD), FOLD)
            x = resid[at, :]
            r = lax.rsqrt(jnp.mean(x * x, axis=1, keepdims=True) + epsilon)
            normed[at, :] = (x * r * nf[...].reshape(1, D)).astype(bf16)
            return carry

        lax.fori_loop(0, T // FOLD, norm2_step, 0)

        def near_step(k, carry):
            values = dot(plan[row_at(k), :], normed[...]).astype(bf16)

            @pl.when(k > 0)
            def _():
                near_send[row_at(k), :] = values
                row_copy(k).start()

            @pl.when(k == 0)
            def _():
                rows[row_at(k), :] = values

            return carry

        def far_step(i, carry):
            k = G - 1 - i
            rets[far_at(k), :] = dot(plan[row_at(k), :], normed[:, mine]).astype(bf16)
            row_half(k).start()
            return carry

        lax.fori_loop(0, G - near, far_step, 0)
        lax.fori_loop(0, near, near_step, 0)
        for k in range(G - 1, G - 5, -1):
            cot_hand_on(k)

        mid = slice(M, M + T)

        def shared_step(u, carry):
            at = pl.ds(pl.multiple_of(u * tile, tile), tile)
            pre = dot(normed[...], vsi[0, :, at])
            up = dot(normed[...], vsi[1, :, at])
            d_act = dot_nt(cot[...], vso[at, :])
            s = sigmoid(pre)
            gs = pre * s
            act[mid, at] = (gs * up).astype(bf16)
            dgu[0, mid, at] = (d_act * up * (s + gs * (1.0 - s))).astype(bf16)
            dgu[1, mid, at] = (d_act * gs).astype(bf16)
            return carry

        def tile_at(i):
            return pl.ds(pl.multiple_of(i * tile, tile), tile)

        def fold_core(i):
            return send(
                tall.at[lax.rem(i, 2), :, :, 1 - core], a1.at[:, :, :, tile_at(i)], s_k.at[i], r_k.at[i],
                sibling,
            )

        def core_end(i):
            fold_core(i).wait()

            def body(n, carry):
                u, v = n // 2, lax.rem(n, 2)
                a1[u, v, :, tile_at(i)] = (
                    a1[u, v, :, tile_at(i)].astype(f32) + tall[lax.rem(i, 2), u, v, core].astype(f32)
                ).astype(bf16)
                return carry

            lax.fori_loop(0, 2 * zs, body, 0)

        def shared_grads(p):
            def body(i, carry):
                at = tile_at(i - p * tiles)
                if p < 2:
                    grad = dot(vsi[0, :, 0:T], dgu[p, mid, at])
                else:
                    grad = dot(vsi[1, :, 0:T], act[mid, at])
                tall[lax.rem(i, 2)] = grad.astype(bf16).reshape(tall.shape[1:])
                fold_core(i).start()

                @pl.when(i > p * tiles)
                def _():
                    core_end(i - 1)

                return carry

            lax.fori_loop(p * tiles, (p + 1) * tiles, body, 0)
            core_end((p + 1) * tiles - 1)
            fold_y(p).start()

        def expert_chunk(c):
            for k in range(c * per, (c + 1) * per):
                if k >= near:
                    row_pass(k).wait_recv()
                    cot_pass(k).wait_recv()
                elif k > 0:
                    row_copy(k).wait_recv()
                    cot_copy(k).wait_recv()
            block = chunk_at(c)

            def unit_step(u, carry):
                at = pl.ds(pl.multiple_of(u * tile, tile), tile)
                pre = dot(rows[block, :], vei[0, :, at])
                up = dot(rows[block, :], vei[1, :, at])
                d_act = dot_nt(drows[block, :], veo[at, :])
                s = sigmoid(pre)
                gs = pre * s
                act[block, at] = (gs * up).astype(bf16)
                dgu[0, block, at] = (d_act * up * (s + gs * (1.0 - s))).astype(bf16)
                dgu[1, block, at] = (d_act * gs).astype(bf16)
                return carry

            lax.fori_loop(0, tiles, unit_step, 0)
            dx = dot_nt(dgu[0, block, :], vei[0]) + dot_nt(dgu[1, block, :], vei[1])
            for k in range(c * per, (c + 1) * per):
                if k >= near:
                    cot_half(k).wait_send()
                elif k > 0:
                    cot_copy(k).wait_send()
            csend[block, :] = dx.astype(bf16)
            if c > 0:
                dx_copy(c).start()
                return
            for k in range(c * per, (c + 1) * per):
                if k > 0:
                    ret_copy(k).start()
                else:
                    near_ret[0:C, :] = csend[0:C, :]

        weights[0].wait()
        weights[1].wait()
        lax.fori_loop(0, tiles, shared_step, 0)
        for k in range(G - 5, near - 1, -1):
            cot_hand_on(k)
        dnsh[...] = (dot_nt(dgu[0, mid, :], vsi[0]) + dot_nt(dgu[1, mid, :], vsi[1])).astype(bf16)
        weights[2].wait()
        weights[3].wait()
        vsi[0, :, 0:T] = normed[...].T
        vsi[1, :, 0:T] = cot[...].T
        shp[...] = dot(act[mid, :], vso[...]).astype(bf16)
        expert_chunk(0)
        for k in range(G - 1, G - 5, -1):
            hand_on(k)
        shared_grads(0)
        expert_chunk(3)
        for k in range(G - 5, G - 7, -1):
            hand_on(k)
        shared_grads(1)
        for k in range(G - 7, near - 1, -1):
            hand_on(k)
        shared_grads(2)
        return_chunk(3)

        expert_chunk(2)
        expert_chunk(1)
        for k in range(1, per):
            ret_copy(k).wait_recv()
        dnsh[...] = (dnsh[...].astype(f32) + dot_tn(plan[0:M, :], near_ret[...])).astype(bf16)
        dnsh_copy.start()
        return_chunk(2)

        def part_chunk(c):
            if c > 0:
                dx_copy(c).wait_send()
            else:
                for k in range(1, per):
                    ret_copy(k).wait_send()
            csend[chunk_at(c), :] = dot(act[chunk_at(c), :], veo[...]).astype(bf16)

        part_chunk(0)
        near_ro[0:C, :] = csend[0:C, :]
        part_chunk(3)
        return_chunk(1)
        part_copy(3).start()
        part_chunk(2)
        part_chunk(1)
        for k in range(1, whole):
            po_copy(k).start()
        sides = [slice(0, S // 2), slice(S // 2, S)]
        for n in range(2):
            vsi[n, :, 0 : S // 2] = rows[sides[n], :].T

        def gein_copy(i):
            return pltpu.make_async_copy(
                tall.at[lax.rem(i, 2)], gein.at[i // tiles, :, :, :, :, tile_at(lax.rem(i, tiles))],
                osem.at[lax.rem(i, 2)],
            )

        def gein_step(i, carry):
            @pl.when(i > 1)
            def _():
                gein_copy(i - 2).wait()

            at = tile_at(lax.rem(i, tiles))
            grad = dot(vsi[0, :, 0 : S // 2], dgu[i // tiles, sides[0], at])
            grad = grad + dot(vsi[1, :, 0 : S // 2], dgu[i // tiles, sides[1], at])
            tall[lax.rem(i, 2)] = grad.astype(bf16).reshape(tall.shape[1:])
            gein_copy(i).start()
            return carry

        first = 2
        lax.fori_loop(0, first, gein_step, 0)
        for k in range(near, G):
            row_pass(k).wait_send()

        dnsh_copy.wait()
        total = dnsh[:, mine].astype(f32) + dnsh_r[...].astype(f32)
        for k in range(per, G):
            ret_half(k).wait_recv()
        total = total + dot_tn(plan[M:S, :], ret[...])
        dnb[:, mine] = total.astype(bf16)
        dnb_copy.start()
        part_copy(2).start()
        if whole == per:
            part_copy(1).start()
        for p in range(3):
            fold_on(p)
        lax.fori_loop(first, 2 * tiles, gein_step, 0)
        return_part(3)

        def geout_copy(i):
            return pltpu.make_async_copy(
                wide.at[lax.rem(i, 2)], geout.at[tile_at(i), :], osem.at[2 + lax.rem(i, 2)]
            )

        def geout_step(i, carry):
            @pl.when(i > 1)
            def _():
                geout_copy(i - 2).wait()

            wide[lax.rem(i, 2)] = dot_tn(act[:, tile_at(i)], drows[...]).astype(bf16)
            geout_copy(i).start()
            return carry

        lax.fori_loop(0, tiles, geout_step, 0)
        gein_copy(2 * tiles - 2).wait()
        gein_copy(2 * tiles - 1).wait()
        geout_copy(tiles - 2).wait()
        geout_copy(tiles - 1).wait()

    pl.run_scoped(
        experts,
        pltpu.VMEM((2, D, F), bf16),
        pltpu.VMEM((F, D), bf16),
        pltpu.VMEM((2, D, F), bf16),
        pltpu.VMEM((F, D), bf16),
        pltpu.VMEM((S, F), bf16),
        pltpu.VMEM((2, S, F), bf16),
        pltpu.VMEM((T, D), bf16),
        pltpu.VMEM((2, zs, 2, 2, share, tile), bf16),
        pltpu.VMEM((2, tile, D), bf16),
    )

    def attention_back(dres, dresb, da, dqkv, turned, turned2, pay, gated, dna, gtok, w1, w2):
        dna_copy = send(dna, dnar, s_x.at[10], r_x.at[10], partner)
        turned[...] = normed_a[...].T
        dnb_copy.wait()

        def gated_rows(c):
            for k in range(c * per, (c + 1) * per):
                gated[(k - c * per) * C : (k - c * per + 1) * C, :] = (
                    plan[row_at(k), :].astype(f32) * gate[pl.ds(peer(k), 1), :]
                ).astype(bf16)
            return gated[...]

        def dres_step(i, carry):
            at = pl.ds(pl.multiple_of(i * FOLD, FOLD), FOLD)
            y_ = dnb[at, :].astype(f32)
            x = resid[at, :]
            r = lax.rsqrt(jnp.mean(x * x, axis=1, keepdims=True) + epsilon)
            a = y_ * nf[...].reshape(1, D)
            inner = jnp.mean(a * x, axis=1, keepdims=True)
            xr = x * r
            value = cot[at, :].astype(f32) + r * a - xr * (r * r * inner)
            dres[at, :] = value
            dresb[at, :] = value.astype(bf16)
            return carry + jnp.sum(y_ * xr, axis=0, keepdims=True)

        gnf = lax.fori_loop(0, T // FOLD, dres_step, jnp.zeros((1, D), f32))
        da[...] = dot_nt(dresb[...], wo[...]).astype(bf16)
        turned2[...] = dresb[...].T
        pay[:, :, :, :, 0:HL] = dot(turned2[...], att_own[...]).astype(bf16).reshape(zs, 2, 2, share, HL)

        def pay_core(p):
            return send(
                pay.at[:, :, 1 - core, :, columns(p)], a2.at[:, :, :, columns(p)], s_x.at[8 + p], r_x.at[8 + p],
                sibling,
            )

        def pay_on(p):
            pay_core(p).wait()

            def body(n, carry):
                u, v = n // 2, lax.rem(n, 2)
                a2[u, v, :, columns(p)] = (
                    a2[u, v, :, columns(p)].astype(f32) + pay[u, v, core, :, columns(p)].astype(f32)
                ).astype(bf16)
                return carry

            lax.fori_loop(0, 2 * zs, body, 0)
            fold_y(p).start()

        pay_core(3).start()

        def attend_back(j, carry):
            at = pl.ds(pl.multiple_of(j * 128, 128), 128)
            q, k, v, g = qkv[0, :, at], qkv[1, :, at], qkv[2, :, at], da[:, at]
            none = jnp.zeros_like(q)
            dq = dk = dv = jnp.zeros((T, 128), f32)
            for i in range(2):
                inside = (lane < HD) if i == 0 else (lane >= HD)
                qi, ki, gi = (jnp.where(inside, x, none) for x in (q, k, g))
                total = jnp.sum(jnp.where(lane == 2 * j + i, lse[...], 0.0), axis=1, keepdims=True)
                p = jnp.exp(dot_nt(qi, k) * scale + bias[...] - total)
                dp = dot_nt(gi, v)
                inner = jnp.sum(dp * p, axis=1, keepdims=True)
                ds = (p * (dp - inner)).astype(bf16)
                dv = dv + dot_tn(p.astype(bf16), gi)
                dq = dq + dot(ds, ki)
                dk = dk + dot_tn(ds, qi)
            dq, dk = dq * scale, dk * scale
            dqkv[0, :, at] = (dq * cos[...] - swap_halves(dq) * sin[...]).astype(bf16)
            dqkv[1, :, at] = (dk * cos[...] - swap_halves(dk) * sin[...]).astype(bf16)
            dqkv[2, :, at] = dv.astype(bf16)
            return carry

        lax.fori_loop(0, HL // 128, attend_back, 0)
        pay_on(3)

        dna[...] = (
            dot_nt(dqkv[0], wqkv[0]) + dot_nt(dqkv[1], wqkv[1]) + dot_nt(dqkv[2], wqkv[2])
        ).astype(bf16)

        def gain_step(i, carry):
            at = pl.ds(pl.multiple_of(i * FOLD, FOLD), FOLD)
            x = tok[at, :].astype(f32)
            r = lax.rsqrt(jnp.mean(x * x, axis=1, keepdims=True) + epsilon)
            return carry + jnp.sum(dna[at, :].astype(f32) * x * r, axis=0, keepdims=True)

        gna[...] = jnp.broadcast_to(
            lax.fori_loop(0, T // FOLD, gain_step, jnp.zeros((1, D), f32)), gna.shape
        )
        gna_copy.start()
        dna_copy.start()
        return_part(2)
        if whole == per:
            return_part(1)
        mixed = shp[...].astype(f32)
        for c in range(whole // per):
            for k in range(max(1, c * per), (c + 1) * per):
                po_copy(k).wait_recv()
            mixed = mixed + dot_tn(gated_rows(c), near_ro[chunk_at(c), :])
        shp[...] = mixed.astype(bf16)
        shp_copy.start()
        for s in range(3):
            pay[:, :, :, :, (s + 1) * HL : (s + 2) * HL] = (
                dot(turned[...], dqkv[s]).astype(bf16).reshape(zs, 2, 2, share, HL)
            )
        gna_copy.wait()
        row = lax.broadcasted_iota(jnp.int32, (128, D), 0)
        gains = jnp.where(row == 0, gnf, jnp.where(row == 1, gna[0:1, :] + gnar[0:1, :], 0.0))
        pay[:, :, :, :, 4 * HL :] = gains.T.astype(bf16).reshape(zs, 2, 2, share, 128)
        pay_core(4).start()
        fold_on(3)
        pay_on(4)
        for p in range(3):
            fold_end(p, w1)
        fold_on(4)

        shp_copy.wait()
        mixed = shp[:, mine].astype(f32) + shpr[...].astype(f32)
        for c in range(whole // per, chunks):
            for k in range(c * per, (c + 1) * per):
                po_half(k).wait_recv()
            mixed = mixed + dot_tn(gated_rows(c), ro[out_chunk(c), :])
        ob[:, mine] = (resid[:, mine] + mixed).astype(bf16)
        out_copy.start()
        dna_copy.wait()

        def last_step(i, carry):
            at = pl.ds(pl.multiple_of(i * FOLD, FOLD), FOLD)
            x = tok[at, :].astype(f32)
            r = lax.rsqrt(jnp.mean(x * x, axis=1, keepdims=True) + epsilon)
            a = (dna[at, :].astype(f32) + dnar[at, :].astype(f32)) * na[...].reshape(1, D)
            inner = jnp.mean(a * x, axis=1, keepdims=True)
            gtok[at, :] = (dres[at, :] + r * a - x * (r * r * r * inner)).astype(bf16)
            return carry

        lax.fori_loop(0, T // FOLD, last_step, 0)
        fold_end(3, w2)
        fold_end(4, w2)
        ends = [
            pltpu.make_async_copy(a, b, osem.at[i])
            for i, (a, b) in enumerate(((gtok, h_gtok), (w1, h_gw1), (w2, h_gw2), (ob, h_out)))
        ]
        for c in ends[:3]:
            c.start()
        out_copy.wait()
        ends[3].start()
        for c in ends:
            c.wait()

    pl.run_scoped(
        attention_back,
        pltpu.VMEM((T, D), f32),
        pltpu.VMEM((T, D), bf16),
        pltpu.VMEM((T, HL), bf16),
        pltpu.VMEM((3, T, HL), bf16),
        pltpu.VMEM((D, T), bf16),
        pltpu.VMEM((D, T), bf16),
        pltpu.VMEM((zs, 2, 2, share, W2), bf16),
        pltpu.VMEM((M, T), bf16),
        pltpu.VMEM((T, D), bf16),
        pltpu.VMEM((T, D), bf16),
        pltpu.VMEM((share, 3 * F), f32),
        pltpu.VMEM((share, W2), f32),
    )
    for k in range(near, G):
        cot_pass(k).wait_send()
    for k in range(whole, G):
        po_half(k).wait_send()
    for k in range(1, near):
        row_copy(k).wait_send()
    for k in range(1, whole):
        po_copy(k).wait_send()
    for k in range(per, whole):
        ret_half(k).wait_send()
    for c in range(whole // per, chunks):
        part_copy(c).wait_send()


def finish_kernel(
    HL, F, h_out, h_gtok, h_gw1, h_gw2, h_gein, h_geout,
    out, gtok, gqkv, gao, gna, gnf, gsi, gso, gein, geout,
):
    out[...] = h_out[...]
    gtok[...] = h_gtok[...]
    gein[...] = h_gein[...].astype(f32)
    geout[...] = h_geout[...].astype(f32)

    @pl.when(pl.program_id(0) == 0)
    def _():
        for s in range(3):
            gqkv[s] = h_gw2[:, (s + 1) * HL : (s + 2) * HL]
        gao[...] = h_gw2[:, 0:HL]
        gains = h_gw2[:, 4 * HL :].T
        gnf[...] = gains[0:1, :]
        gna[...] = gains[1:2, :]
        for s in range(2):
            gsi[s] = h_gw1[:, s * F : (s + 1) * F]
        gso[...] = h_gw1[:, 2 * F :]


def fused(
    tokens, cont_lengths, routes, route_gates, w_qkv, w_attn_out, norm_attn, norm_ffn,
    shared_in, shared_out, expert_in, expert_out, cotangent,
):
    T, D = tokens.shape
    G = lax.axis_size("dp")
    HL, F = w_qkv.shape[2], shared_in.shape[2]
    C = round_up(CAP, 16)
    S = G * C
    half, share, zs = D // 2, D // G, G // 4
    W1, W2 = 3 * F, 4 * HL + 128
    shape = jax.ShapeDtypeStruct
    dma = pltpu.SemaphoreType.DMA
    SM = pl.BlockSpec(memory_space=pltpu.SMEM)
    out, gtok, gw1, gw2, gein, geout = pl.pallas_call(
        functools.partial(layer_kernel, G),
        out_shape=(
            shape((T, D), bf16), shape((T, D), bf16), shape((share, W1), f32), shape((share, W2), f32),
            shape((2, zs, 2, 2, share, F), bf16), shape((F, D), bf16),
        ),
        in_specs=[VM] * 2 + [SM] + [VM] * 2 + [ANY] * 8,
        out_specs=(ANY,) * 6,
        scratch_shapes=[
            pltpu.VMEM((T, D), bf16),
            pltpu.VMEM((3, D, HL), bf16),
            pltpu.VMEM((HL, D), bf16),
            pltpu.VMEM((T, D), bf16),
            pltpu.VMEM((T, 128), f32),
            pltpu.VMEM((T, 128), f32),
            pltpu.VMEM((3, T, HL), bf16),
            pltpu.VMEM((T, 128), f32),
            pltpu.VMEM((T, HL), bf16),
            pltpu.VMEM((T, D), bf16),
            pltpu.VMEM((T, D), f32),
            pltpu.VMEM((S, T), bf16),
            pltpu.VMEM((EXPERTS, T), f32),
            pltpu.VMEM((EXPERTS, T), f32),
            pltpu.VMEM((T, T), f32),
            pltpu.VMEM((T, HL), bf16),
            pltpu.VMEM((HL, D), bf16),
            pltpu.VMEM((S, D), bf16),
            pltpu.VMEM((S, D), bf16),
            pltpu.VMEM((S, D), bf16),
            pltpu.VMEM((NEAR * C, D), bf16),
            pltpu.VMEM((S - 4 * C, half), bf16),
            pltpu.VMEM((4 * C, D), bf16),
            pltpu.VMEM((S - 4 * C, half), bf16),
            pltpu.VMEM((S - 4 * C, half), bf16),
            pltpu.VMEM((T, D), bf16),
            pltpu.VMEM((T, half), bf16),
            pltpu.VMEM((T, D), bf16),
            pltpu.VMEM((T, D), bf16),
            pltpu.VMEM((S - WHOLE * C, half), bf16),
            pltpu.VMEM((WHOLE * C, D), bf16),
            pltpu.VMEM((S - WHOLE * C, half), bf16),
            pltpu.VMEM((T, half), bf16),
            pltpu.VMEM((8, D), f32),
            pltpu.VMEM((8, D), f32),
            *[
                pltpu.VMEM((*dims, share, width), bf16)
                for width in (W1, W2)
                for dims in ((zs, 2), (zs,), (zs - 1,))
            ],
            dma((13,)), dma((13,)), *[dma((G,))] * 8, dma((4,)), dma((4,)), dma((G,)), dma((G,)),
            dma((4,)), dma((4,)), dma((G,)), dma((G,)), dma((12,)), dma((12,)), dma((5,)), dma((5,)),
            dma((5, zs - 1)), dma((5, zs - 1)), dma((8,)), dma((4,)),
        ],
        compiler_params=pltpu.CompilerParams(
            collective_id=0, has_side_effects=True, vmem_limit_bytes=VMEM_BYTES
        ),
        name="layer",
    )(
        norm_attn, norm_ffn, cont_lengths, routes.T, route_gates.T, tokens, w_qkv, w_attn_out, cotangent,
        shared_in, shared_out, expert_in, expert_out,
    )
    steps = 2

    def rows_of(*dims):
        return pl.BlockSpec(dims, lambda i: (0,) * (len(dims) - 2) + (i, 0))

    def whole(*dims):
        return pl.BlockSpec(dims, lambda i: (0,) * len(dims))

    results = ((3, share, HL), (share, HL), (1, share), (1, share), (2, share, F), (share, F))
    out, gtok, gqkv, gao, gna, gnf, gsi, gso, gein, geout = pl.pallas_call(
        functools.partial(finish_kernel, HL, F),
        grid=(steps,),
        out_shape=(
            shape((T, D), bf16), shape((T, D), bf16), *[shape(r, f32) for r in results],
            shape((2, D, F), f32), shape((F, D), f32),
        ),
        in_specs=[
            rows_of(T // steps, D), rows_of(T // steps, D), whole(share, W1), whole(share, W2),
            rows_of(2, D // steps, F), rows_of(F // steps, D),
        ],
        out_specs=(
            rows_of(T // steps, D), rows_of(T // steps, D), *[whole(*r) for r in results],
            rows_of(2, D // steps, F), rows_of(F // steps, D),
        ),
        compiler_params=pltpu.CompilerParams(vmem_limit_bytes=VMEM_BYTES),
        name="finish",
    )(out, gtok, gw1, gw2, gein.reshape(2, D, F), geout)
    return (out, gtok, gqkv, gao.T, gna[0], gnf[0], gsi, gso.T, gein, geout)


def solution(mesh):
    placed = (
        P("dp", None),
        P("dp", None),
        P("dp", None),
        P("dp", None),
        P(None, None, "tensor"),
        P("tensor", None),
        P(),
        P(),
        P(None, None, "tensor"),
        P("tensor", None),
        P(None, None, ("dp", "tensor")),
        P(("dp", "tensor"), None),
        P("dp", None),
    )
    return jax.shard_map(
        fused if mesh.shape["dp"] == EXPERTS else local,
        mesh=mesh,
        in_specs=placed,
        out_specs=(
            P("dp", None),
            P("dp", None),
            P(None, "dp", "tensor"),
            P("tensor", "dp"),
            P("dp"),
            P("dp"),
            P(None, "dp", "tensor"),
            P("tensor", "dp"),
            P(None, None, ("dp", "tensor")),
            P(("dp", "tensor"), None),
        ),
        check_vma=False,
    )
```
